512 devices in a mesh: tile: 128 (over y, z, core), rep: 4 (over x).
Axes of the slice: x: 4, y: 8, z: 8, core: 2. Of those that a mesh axis runs over, the one named last changes fastest.
Arguments:
- inputs: bfloat16 [4, 6, 1024, 16, 256], P('rep', None, 'tile'), may hold values from -6 to 6
- cotangent: bfloat16 [4, 2, 2048, 32, 128], P('rep', None, 'tile'), may hold values from -6 to 6
- first_weight: bfloat16 [3, 3, 3, 256, 128], replicated, may hold values from -0.078125 to 0.078125
- second_weight: bfloat16 [3, 3, 3, 128, 128], replicated, may hold values from -0.109375 to 0.109375
- tile_clip: int32 [4, 128], P('rep'), may hold values from 0 to 7, never falling along the last dimension, each value on 1 to 32 neighbouring positions
- clip_cols: int32 [4, 8], P('rep'), may hold values from 10 to 16, as said below
- clip_start: int32 [4, 8], P('rep'), may hold values from 0 to 2
Outputs:
- input_grad: bfloat16 [4, 6, 1024, 16, 256], P('rep', None, 'tile')
- grad_first: float32 [3, 3, 3, 256, 128], P(None, None, None, None, 'rep')
- grad_second: float32 [3, 3, 3, 128, 128], P(None, None, None, None, 'rep')
The draws below stay inside these ranges and needn't reach their ends.
Inputs may be any that keep to these rules, and one draw needn't show every extreme that they name: `tile_clip`: clip numbers never fall along the tiles of a group; each clip 0 to 7 has 1 to 32 consecutive tiles, and one has exactly 32. `clip_cols`: each clip has 16 columns (1080p) or 2 * 16 // 3 (720p); both kinds occur in every group.
All inputs are finite; a program needn't handle non-finite values.
Results may differ from the reference program's by a relative error of at most 0.018.
Values may be sent and summed in bfloat16 or wider, within the bound.
No kernel may reach another device: no remote copies, remote signals or barrier semaphores. Data moves between devices by JAX's collectives and lax.ppermute only.
A program may use at most 64 MiB of HBM per device.

```python
import math
import jax
import jax.numpy as jnp
import numpy as np
from jax import lax

C0 = 256
C1 = 128
TH = 8
TW = 16
F = 2
NF = 6
CLIPS = 8
MOST_TILES = 32
GRAD_CELLS = 524288
N_TILE = 128
N_REP = 4


def draw_clip_cols(key, part):
    key = jax.random.fold_in(key, 11)
    wide_flag = jax.random.randint(key, (N_REP, CLIPS), 0, 2)
    place = jax.random.randint(jax.random.fold_in(key, 5), (N_REP, 1), 0, CLIPS)
    clip_order = jnp.arange(CLIPS)[None, :]
    wide_flag = jnp.where(clip_order == place, 1, wide_flag)
    wide_flag = jnp.where(clip_order == (place + 1) % CLIPS, 0, wide_flag)
    return jnp.where(wide_flag == 1, TW, 2 * TW // 3).astype(jnp.int32)


def plant(entries, stream_key, low, high):
    longest = entries.shape.index(max(entries.shape))
    spots = []
    for shift in (0, 1):
        where = [jax.random.randint(jax.random.fold_in(stream_key, axis), (), 0, length) for axis, length in enumerate(entries.shape)]
        where[longest] = (where[longest] + shift) % entries.shape[longest]
        spots.append(tuple(where))
    return entries.at[spots[0]].set(low).at[spots[1]].set(high)


def block_scale(own_key, extent, pieces, low, top_value):
    loudness = 1.0
    for dim, shards_of in pieces:
        draws = jax.random.uniform(jax.random.fold_in(jax.random.fold_in(own_key, 6), dim), (shards_of,), jnp.float32, low / len(pieces), top_value / len(pieces))
        loudness = loudness * jnp.repeat(jnp.exp(draws), extent[dim] // shards_of).reshape((-1,) + (1,) * (len(extent) - 1 - dim))
    return loudness


def length_profile(amount, total, most, slope):
    loads = [(1 << 20) // math.isqrt(rank ** slope) + 1 for rank in range(2, amount + 1)]
    rest, counts = total - most - (amount - 1), [1] * (amount - 1)
    while rest > 0:
        movable = [i for i in range(amount - 1) if counts[i] < most]
        whole, remaining = sum([loads[i] for i in movable]), rest
        for i in movable:
            extra = min(most - counts[i], max(1, remaining * loads[i] // whole), rest)
            counts[i] = counts[i] + extra
            rest = rest - extra
    return np.array([most] + counts)


def uneven_parts(key, count, total, most, lean):
    if count == 2:
        one = jax.random.randint(key, (), max(1, total - most), min(most, total - 1) + 1)
        return jnp.stack([one, total - one])
    tallies = jnp.asarray(length_profile(count, total, most, lean), jnp.int32)
    couples = (count - 1) // 2
    giver, taker = tallies[1:1 + 2 * couples:2], tallies[2:2 + 2 * couples:2]
    margin = jnp.minimum(giver - 1, most - taker)
    shifted = jax.random.randint(jax.random.fold_in(key, 1), (couples,), 0, 1 << 20) % (margin + 1)
    tallies = tallies.at[1:1 + 2 * couples:2].set(giver - shifted).at[2:2 + 2 * couples:2].set(taker + shifted)
    return tallies[jax.random.permutation(jax.random.fold_in(key, 2), count)]


def normal_values(rng, extent, deviation, most, pieces=(), held_as=jnp.bfloat16):
    entries = jax.random.normal(rng, extent, jnp.float32) * deviation
    if len(pieces) > 0:
        entries = block_scale(rng, extent, pieces, -0.22, 0.18) * entries
    return jnp.clip(entries, min=-most, max=most).astype(held_as)


def setup_inputs(seed: int = 0) -> dict:
    key_list = jax.random.split(jax.random.key(seed), 8)
    inputs = normal_values(key_list[0], (N_REP, NF, TH * N_TILE, TW, C0), 1.0, 6.0, ((0, 4), (2, 128)))
    cotangent = normal_values(key_list[1], (N_REP, F, 2 * TH * N_TILE, 2 * TW, C1), 1.0, 6.0, ((0, 4), (2, 128)))
    first_weight = normal_values(key_list[2], (3, 3, 3, C0, C1), (27 * C0) ** -0.5, 0.078125)
    second_weight = normal_values(key_list[3], (3, 3, 3, C1, C1), (27 * C1) ** -0.5, 0.109375)
    tile_clip = jax.vmap(lambda own: jnp.searchsorted(jnp.cumsum(uneven_parts(own, CLIPS, N_TILE, MOST_TILES, 2)), jnp.arange(N_TILE), side="right"))(jax.random.split(key_list[4], N_REP)).reshape((N_REP, N_TILE)).astype(jnp.int32)
    clip_cols = draw_clip_cols(jax.random.fold_in(key_list[7], 71), 0)
    clip_start = plant(jax.random.randint(key_list[6], (N_REP, CLIPS), 0, 3), jax.random.fold_in(key_list[6], 1), 0, 2).astype(jnp.int32)
    return {"inputs": inputs, "cotangent": cotangent, "first_weight": first_weight, "second_weight": second_weight, "tile_clip": tile_clip, "clip_cols": clip_cols, "clip_start": clip_start}


def silu_slope(values):
    sigmoid_of = jax.nn.sigmoid(values)
    return sigmoid_of * (1.0 + values * (1.0 - sigmoid_of))

def row_flags(row_first, row_count, row_limit, up_same, down_same):
    offsets = row_first + jnp.arange(row_count)
    return jnp.where(offsets < 0, up_same, jnp.where(offsets >= row_limit, down_same, True)).astype(jnp.float32)

def conv_rows(values, kernel):
    return lax.conv_general_dilated(values[None].astype(jnp.float32), kernel.astype(jnp.float32), (1, 1, 1), ((0, 0), (0, 0), (1, 1)), dimension_numbers=('NDHWC', 'DHWIO', 'NDHWC'), precision=lax.Precision.HIGHEST)[0]

def flipped(kernel):
    return jnp.transpose(kernel[::-1, ::-1, ::-1], (0, 1, 2, 4, 3))

def frame_pad(values, before, after, extra_rows):
    return jnp.pad(values, ((before, after), (extra_rows, extra_rows), (0, 0), (0, 0)))

def upsample(values):
    return jnp.repeat(jnp.repeat(values, 2, axis=1), 2, axis=2)

def down_sum(values):
    shape_now = values.shape
    return values.reshape(shape_now[0], shape_now[1] // 2, 2, shape_now[2] // 2, 2, shape_now[3]).sum(axis=(2, 4))

def weight_grad(values, cot_values):
    padded = jnp.pad(values, ((0, 0), (0, 0), (1, 1), (0, 0))).astype(jnp.float32)
    cot_float = cot_values.astype(jnp.float32)
    frames_out, rows_out, width_out = (cot_values.shape[0], cot_values.shape[1], cot_values.shape[2])
    tap_terms = []
    for depth_tap in range(3):
        for height in range(3):
            for across in range(3):
                window = padded[depth_tap:depth_tap + frames_out, height:height + rows_out, across:across + width_out]
                tap_terms.append(jnp.einsum('fhwi,fhwo->io', window, cot_float, precision=lax.Precision.HIGHEST))
    return jnp.stack(tap_terms).reshape(3, 3, 3, values.shape[3], cot_values.shape[3])

def eff_inputs(extended, from_start):
    first_frame = extended[4]
    head_frames = jnp.where(from_start, jnp.broadcast_to(first_frame, extended[:4].shape), extended[:4])
    return jnp.concatenate([head_frames, extended[4:]], 0)

def finish_grad(act_grad, core_float, col_low, from_start):
    pre_input = act_grad * silu_slope(core_float) * col_low[None, None, :, None]
    carried = lax.optimization_barrier(jnp.sum(pre_input[:4], axis=0))
    moved_grad = jnp.concatenate([jnp.zeros_like(pre_input[:4]), (pre_input[4] + carried)[None], pre_input[5:]], 0)
    return jnp.where(from_start, moved_grad, pre_input).astype(jnp.bfloat16)

def tile_backward(ext_in, ext_cot, first_weight, second_weight, up_same, down_same, columns, from_start):
    col_low = (jnp.arange(TW) < columns).astype(jnp.float32)
    col_high = (jnp.arange(2 * TW) < 2 * columns).astype(jnp.float32)
    eff = eff_inputs(ext_in, from_start).astype(jnp.float32)
    mask_act = row_flags(-2, TH + 4, TH, up_same, down_same)[:, None] * col_low[None, :]
    activated = (jax.nn.silu(eff) * mask_act[None, :, :, None]).astype(jnp.bfloat16)
    first_out = conv_rows(activated, first_weight)
    upsampled = upsample(first_out)
    mask_second = row_flags(-2, 2 * TH + 4, 2 * TH, up_same, down_same)[:, None] * col_high[None, :]
    second_in = (jax.nn.silu(upsampled) * mask_second[None, :, :, None]).astype(jnp.bfloat16)
    mask_cot = row_flags(-3, 2 * TH + 6, 2 * TH, up_same, down_same)[:, None] * col_high[None, :]
    cot_masked = (ext_cot.astype(jnp.float32) * mask_cot[None, :, :, None]).astype(jnp.bfloat16)
    second_grad = conv_rows(frame_pad(cot_masked, 2, 2, 0), flipped(second_weight))
    pre_grad = second_grad * silu_slope(upsampled) * mask_second[None, :, :, None]
    first_grad = down_sum(pre_grad).astype(jnp.bfloat16)
    grad_second = weight_grad(second_in[:, 1:2 * TH + 3], cot_masked[:, 3:3 + 2 * TH])
    grad_first = weight_grad(activated[:, 1:TH + 3], first_grad[:, 1:TH + 1])
    act_grad = conv_rows(frame_pad(first_grad, 2, 2, 0), flipped(first_weight))
    input_grad = finish_grad(act_grad, eff[:, 2:TH + 2], col_low, from_start)
    return (input_grad, grad_first, grad_second)

def with_rims(tile_stack, depth_rows):
    zero_tile = jnp.zeros_like(tile_stack[:, :1])
    tile_above = jnp.concatenate([zero_tile, tile_stack[:, :-1]], 1)
    tile_below = jnp.concatenate([tile_stack[:, 1:], zero_tile], 1)
    return jnp.concatenate([tile_above[:, :, :, -depth_rows:], tile_stack, tile_below[:, :, :, :depth_rows]], axis=3)

def reference(inputs, cotangent, first_weight, second_weight, tile_clip, clip_cols, clip_start):
    tiles_in = inputs.reshape(N_REP, NF, N_TILE, TH, TW, C0).transpose(0, 2, 1, 3, 4, 5)
    tiles_cot = cotangent.reshape(N_REP, F, N_TILE, 2 * TH, 2 * TW, C1).transpose(0, 2, 1, 3, 4, 5)
    ext_in = with_rims(tiles_in, 2).reshape(N_REP * N_TILE, NF, TH + 4, TW, C0)
    ext_cot = with_rims(tiles_cot, 3).reshape(N_REP * N_TILE, F, 2 * TH + 6, 2 * TW, C1)
    no_clip = jnp.full((N_REP, 1), -1, jnp.int32)
    clip_above = jnp.concatenate([no_clip, tile_clip[:, :-1]], 1)
    clip_below = jnp.concatenate([tile_clip[:, 1:], no_clip], 1)
    up_same = (clip_above == tile_clip).reshape(-1)
    down_same = (clip_below == tile_clip).reshape(-1)
    columns = jnp.take_along_axis(clip_cols, tile_clip, 1).reshape(-1)
    from_start = (jnp.take_along_axis(clip_start, tile_clip, 1) == 0).reshape(-1)

    def visit_tile(totals_now, tile_item):
        grad_in, grad_a, grad_b = tile_backward(tile_item[0], tile_item[1], first_weight, second_weight, tile_item[2], tile_item[3], tile_item[4], tile_item[5])
        rounded_a = lax.optimization_barrier(grad_a.astype(jnp.bfloat16)).astype(jnp.float32)
        rounded_b = lax.optimization_barrier(grad_b.astype(jnp.bfloat16)).astype(jnp.float32)
        return ((totals_now[0] + rounded_a, totals_now[1] + rounded_b), grad_in)
    start_totals = (jnp.zeros((3, 3, 3, C0, C1), jnp.float32), jnp.zeros((3, 3, 3, C1, C1), jnp.float32))
    totals, input_tiles = lax.scan(visit_tile, start_totals, (ext_in, ext_cot, up_same, down_same, columns, from_start))
    input_grad = input_tiles.reshape(N_REP, N_TILE, NF, TH, TW, C0).transpose(0, 2, 1, 3, 4, 5).reshape(N_REP, NF, N_TILE * TH, TW, C0)
    grad_scale = 1.0 / math.sqrt(GRAD_CELLS)
    return (input_grad, totals[0] * grad_scale, totals[1] * grad_scale)
```

```python
import math

import jax
import jax.numpy as jnp
from jax import lax
from jax.experimental import pallas as pl
from jax.experimental.pallas import tpu as pltpu
from jax.sharding import Mesh
from jax.sharding import PartitionSpec as P

TILE_AXES = ("y", "z", "core")
PLANE_AXES = ("y", "z")
BF = jnp.bfloat16
F32 = jnp.float32
NT = (((1,), (1,)), ((), ()))
TN = (((0,), (0,)), ((), ()))
LAST = 128
IN_BLOCKS = 24
HALO_BLOCKS = 36


def dot(lhs, rhs, dims=(((1,), (0,)), ((), ()))):
    return lax.dot_general(lhs, rhs, dims, preferred_element_type=F32)


def pack_kernel(in_ref, cot_ref, to_next, to_previous):
    for out, row_in, row_cot in ((to_next, 6, 13), (to_previous, 0, 0)):
        for frame in range(6):
            for row in range(2):
                for half in range(2):
                    out[frame * 4 + row * 2 + half] = in_ref[
                        frame, row_in + row, :, half * LAST : (half + 1) * LAST
                    ]
        for frame in range(2):
            for row in range(3):
                for half in range(2):
                    out[IN_BLOCKS + frame * 6 + row * 2 + half] = cot_ref[
                        frame, row_cot + row, half * 16 : (half + 1) * 16, :
                    ]


def sigmoid(values):
    return 1.0 / (1.0 + jnp.exp(-values))


def column_shifts(values, column):
    left = jnp.where(column == 0, 0.0, pltpu.roll(values, 1, 1))
    right = jnp.where(column == 15, 0.0, pltpu.roll(values, 15, 1))
    return left, right


def main_kernel(
    clip_ref,
    cols_ref,
    start_ref,
    in_ref,
    cot_ref,
    above_ref,
    below_ref,
    w1_ref,
    w2_ref,
    grad_ref,
    part_ref,
    act,
    pair,
    cots,
    seconds,
    firsts,
):
    tile = lax.axis_index(TILE_AXES)
    tiles = lax.axis_size(TILE_AXES)
    own = clip_ref[0, tile]
    up_same = (tile > 0) & (clip_ref[0, jnp.maximum(tile - 1, 0)] == own)
    down_same = (tile + 1 < tiles) & (clip_ref[0, jnp.minimum(tile + 1, tiles - 1)] == own)
    up_scale = jnp.where(up_same, 1.0, 0.0)
    down_scale = jnp.where(down_same, 1.0, 0.0)
    columns = cols_ref[0, own]
    from_start = start_ref[0, own] == 0

    col_256 = lax.broadcasted_iota(jnp.int32, (1, 16, 256), 1)
    low_256 = jnp.where(col_256 < columns, 1.0, 0.0)

    def activated(values, scale):
        wide = values.astype(F32)
        return wide * sigmoid(wide) * (low_256 * scale)

    def frame_of(frame):
        return jnp.where(from_start, 4, frame) if frame < 4 else frame

    for frame in range(6):
        source = frame_of(frame)

        def halo(ref):
            blocks = ref[pl.ds(source * 4, 4)]
            return jnp.concatenate(
                [
                    jnp.concatenate([blocks[0:1], blocks[1:2]], 2),
                    jnp.concatenate([blocks[2:3], blocks[3:4]], 2),
                ],
                0,
            )

        for first, count, raw, scale in (
            (0, 2, halo(above_ref), up_scale),
            (2, 8, in_ref[source], 1.0),
            (10, 2, halo(below_ref), down_scale),
        ):
            values = activated(raw, scale)
            left, right = column_shifts(values, col_256)
            act[0, frame, first : first + count] = left.astype(BF)
            act[1, frame, first : first + count] = values.astype(BF)
            act[2, frame, first : first + count] = right.astype(BF)

    first_out = None
    for step in range(9):
        kt, kh = step // 3, step % 3
        window = jnp.concatenate(
            [act[kw, kt : kt + 4, kh : kh + 10].reshape(640, 256) for kw in range(3)], 1
        )
        term = dot(window, w1_ref[step * 3 : step * 3 + 3].reshape(768, LAST))
        first_out = term if first_out is None else first_out + term
    first_out = first_out.reshape(40, 16, LAST)
    column = lax.broadcasted_iota(jnp.int32, (1, 16, LAST), 1)
    low = jnp.where(column < columns, 1.0, 0.0)
    row = lax.broadcasted_iota(jnp.int32, (40, 1, 1), 0) % 10
    row_scale = jnp.where(row == 0, up_scale, jnp.where(row == 9, down_scale, 1.0))
    gate = sigmoid(first_out)
    second_in = (first_out * gate * low).astype(BF).reshape(4, 10, 16, LAST)
    seconds[...] = second_in[:, 1:9]
    slope = gate * (1.0 + first_out * (1.0 - gate)) * (low * row_scale)

    wide_column = lax.broadcasted_iota(jnp.int32, (1, 32, LAST), 1)
    high = jnp.where(wide_column < 2 * columns, 1.0, 0.0)
    pair[:, :, 0:8] = jnp.zeros((2, 21, 8, LAST), F32)
    pair[:, :, 40:48] = jnp.zeros((2, 21, 8, LAST), F32)
    for frame in range(2):
        rows = []
        for ref, scale in ((above_ref, up_scale), (None, 1.0), (below_ref, down_scale)):
            if ref is None:
                rows += [cot_ref[frame, r : r + 1].astype(F32) * high for r in range(16)]
                continue
            for r in range(3):
                at = IN_BLOCKS + frame * 6 + r * 2
                block = ref[at : at + 2].reshape(1, 32, LAST)
                rows.append(block.astype(F32) * (high * scale))
        for i in range(-2, 9):
            pair[frame, i + 2 : i + 3, 8:40] = rows[2 * i + 4] + rows[2 * i + 5]
        for i in range(-1, 9):
            pair[frame, i + 12 : i + 13, 8:40] = rows[2 * i + 3] + rows[2 * i + 4]
        for slot in range(21):
            before, even, odd, after = (
                pair[frame, slot, pl.ds(begin, 16, 2), :] for begin in (7, 8, 9, 10)
            )
            for kw, value in ((0, odd + after), (1, even + odd), (2, before + even)):
                rounded = value.astype(BF)
                if slot >= 11:
                    targets = ((1, slot - 11),)
                else:
                    targets = ((0, slot - 1), (2, slot))
                for kh, place in targets:
                    if 0 <= place < 10:
                        tap = kh * 3 + kw
                        cots[frame, place, :, tap * LAST : (tap + 1) * LAST] = rounded

    flat = jnp.concatenate(
        [
            jnp.concatenate([w2_ref[kt * 9 + tap] for tap in range(9)], 1)
            for kt in range(3)
        ],
        0,
    )
    spread = dot(cots[...].reshape(320, 1152), flat, NT)
    for frame in range(4):
        total = None
        for kt in range(3):
            if 0 <= frame - kt < 2:
                term = spread[
                    (frame - kt) * 160 : (frame - kt + 1) * 160, kt * LAST : (kt + 1) * LAST
                ]
                total = term if total is None else total + term
        first_grad = total.reshape(10, 16, LAST) * slope[frame * 10 : frame * 10 + 10]
        before, after = column_shifts(first_grad, column)
        for kw, value in ((0, after), (1, first_grad), (2, before)):
            rounded = value.astype(BF)
            for kh in range(3):
                tap = kh * 3 + kw
                firsts[frame, :, :, tap * LAST : (tap + 1) * LAST] = rounded[2 - kh : 10 - kh]

    cores, reps = part_ref.shape[0], part_ref.shape[1]
    depth = LAST // cores // reps

    def put(block, tap, third):
        part = block.astype(BF).reshape(reps, cores, depth, LAST)
        for core in range(cores):
            part_ref[core, :, tap * 3 + third] = part[:, core]

    seconds_all = jnp.concatenate([seconds[kt : kt + 2].reshape(256, LAST) for kt in range(3)], 1)
    act_all = jnp.concatenate([act[1, kt : kt + 4, 2:10].reshape(512, 256) for kt in range(3)], 1)
    for tap in range(9):
        here = slice(tap * LAST, (tap + 1) * LAST)
        block = dot(cots[:, 1:9, :, here].reshape(256, LAST), seconds_all, TN)
        for kt in range(3):
            put(block[:, kt * LAST : (kt + 1) * LAST], kt * 9 + tap, 2)
        block = dot(firsts[:, :, :, here].reshape(512, LAST), act_all, TN)
        for kt in range(3):
            for half in range(2):
                at = kt * 256 + half * LAST
                put(block[:, at : at + LAST], kt * 9 + tap, half)

    shifted = firsts[...].reshape(512, 1152)
    by_depth = [
        dot(shifted, jnp.concatenate([w1_ref[kt * 9 + tap] for tap in range(9)], 1), NT)
        for kt in range(3)
    ]
    keep = jnp.where(from_start, 0.0, 1.0)
    carried = None
    for frame in range(6):
        total = None
        for kt in range(3):
            if 0 <= frame - kt < 4:
                term = by_depth[kt][(frame - kt) * 128 : (frame - kt + 1) * 128]
                total = term if total is None else total + term
        wide = in_ref[frame_of(frame)].astype(F32)
        gate = sigmoid(wide)
        pre = total.reshape(8, 16, 256) * (gate * (1.0 + wide * (1.0 - gate)) * low_256)
        if frame < 4:
            carried = pre if carried is None else carried + pre
            grad_ref[frame] = (pre * keep).astype(BF)
        elif frame == 4:
            grad_ref[frame] = (pre + carried * (1.0 - keep)).astype(BF)
        else:
            grad_ref[frame] = pre.astype(BF)


def finish_kernel(scale, whole_ref, first_ref, second_ref):
    cores, depth = whole_ref.shape[0], whole_ref.shape[2]
    for tap in range(27):
        for third in range(3):
            for core in range(cores):
                block = whole_ref[core, tap * 3 + third].astype(F32) * scale
                rows = slice(core * depth, (core + 1) * depth)
                if third == 2:
                    second_ref[tap, rows, :] = block
                else:
                    first_ref[tap, rows, third * LAST : (third + 1) * LAST] = block


VMEM = pl.BlockSpec(memory_space=pltpu.VMEM)
SMEM = pl.BlockSpec(memory_space=pltpu.SMEM)


def wide_sum(parts):
    return jnp.sum(parts.astype(F32), axis=0).astype(BF)


def body(inputs, cotangent, first_weight, second_weight, tile_clip, clip_cols, clip_start):
    tiles = lax.axis_size(TILE_AXES)
    cores, reps, plane = lax.axis_size("core"), lax.axis_size("x"), lax.axis_size(PLANE_AXES)
    local_in, local_cot = inputs[0], cotangent[0]
    halo_shape = jax.ShapeDtypeStruct((HALO_BLOCKS, 16, LAST), BF)
    to_next, to_previous = pl.pallas_call(
        pack_kernel,
        out_shape=(halo_shape, halo_shape),
        in_specs=[VMEM, VMEM],
        out_specs=(VMEM, VMEM),
        compiler_params=pltpu.CompilerParams(vmem_limit_bytes=8 << 20),
    )(local_in, local_cot)
    above = lax.ppermute(to_next, TILE_AXES, [(i, (i + 1) % tiles) for i in range(tiles)])
    below = lax.ppermute(to_previous, TILE_AXES, [((i + 1) % tiles, i) for i in range(tiles)])

    depth = LAST // cores // reps
    input_grad, parts = pl.pallas_call(
        main_kernel,
        out_shape=(
            jax.ShapeDtypeStruct(local_in.shape, BF),
            jax.ShapeDtypeStruct((cores, reps, 81, depth, LAST), BF),
        ),
        in_specs=[SMEM, SMEM, SMEM] + [VMEM] * 6,
        out_specs=(VMEM, VMEM),
        scratch_shapes=[
            pltpu.VMEM((3, 6, 12, 16, 256), BF),
            pltpu.VMEM((2, 21, 48, LAST), F32),
            pltpu.VMEM((2, 10, 16, 9 * LAST), BF),
            pltpu.VMEM((4, 8, 16, LAST), BF),
            pltpu.VMEM((4, 8, 16, 9 * LAST), BF),
        ],
        compiler_params=pltpu.CompilerParams(vmem_limit_bytes=48 << 20),
    )(
        tile_clip,
        clip_cols,
        clip_start,
        local_in,
        local_cot,
        above,
        below,
        first_weight.reshape(27, 256, LAST),
        second_weight.reshape(27, LAST, LAST),
    )

    rows = 81 * depth
    parts = parts.reshape(cores, reps, rows, LAST)
    of_core = wide_sum(lax.all_to_all(parts, "core", 0, 0, tiled=True))
    of_rep = wide_sum(lax.all_to_all(of_core, "x", 0, 0, tiled=True))
    share = -(-rows // plane // 8) * 8
    of_rep = jnp.pad(of_rep, ((0, share * plane - rows), (0, 0))).reshape(plane, share, LAST)
    own = wide_sum(lax.all_to_all(of_rep, PLANE_AXES, 0, 0, tiled=True))
    own = jnp.broadcast_to(own[None], (plane, share, LAST))
    half = lax.all_to_all(own, PLANE_AXES, 0, 0, tiled=True)
    half = half.reshape(plane * share, LAST)[:rows]
    whole = lax.all_gather(half, "core", axis=0).reshape(cores, 81, depth, LAST)

    cell_total = tiles * reps * cotangent.shape[1] * cotangent.shape[2] * cotangent.shape[3]
    scale = 1.0 / math.sqrt(cell_total)
    first, second = pl.pallas_call(
        lambda *refs: finish_kernel(scale, *refs),
        out_shape=(
            jax.ShapeDtypeStruct((27, LAST // reps, 256), F32),
            jax.ShapeDtypeStruct((27, LAST // reps, LAST), F32),
        ),
        in_specs=[VMEM],
        out_specs=(VMEM, VMEM),
        compiler_params=pltpu.CompilerParams(vmem_limit_bytes=16 << 20),
    )(whole)
    first = jnp.swapaxes(first, 1, 2).reshape(3, 3, 3, 256, LAST // reps)
    second = jnp.swapaxes(second, 1, 2).reshape(3, 3, 3, LAST, LAST // reps)
    return input_grad[None], first, second


def solution(mesh):
    devices = mesh.devices
    tiles, reps = devices.shape
    side = math.isqrt(tiles // 2)
    wide_mesh = Mesh(devices.reshape(side, tiles // 2 // side, 2, reps), ("y", "z", "core", "x"))
    in_specs = (
        P("x", None, TILE_AXES, None, None),
        P("x", None, TILE_AXES, None, None),
        P(),
        P(),
        P("x", None),
        P("x", None),
        P("x", None),
    )
    out_specs = (
        P("x", None, TILE_AXES, None, None),
        P(None, None, None, None, "x"),
        P(None, None, None, None, "x"),
    )
    return jax.shard_map(
        body, mesh=wide_mesh, in_specs=in_specs, out_specs=out_specs, check_vma=False
    )
```

```python
import math

import jax
import jax.numpy as jnp
from jax import lax
from jax.experimental import pallas as pl
from jax.experimental.pallas import tpu as pltpu
from jax.sharding import Mesh
from jax.sharding import PartitionSpec as P

TILE_AXES = ("y", "z", "core")
PLANE_AXES = ("y", "z")
BF = jnp.bfloat16
F32 = jnp.float32
NT = (((1,), (1,)), ((), ()))
TN = (((0,), (0,)), ((), ()))
LAST = 128
TILE_COT = 96
TILE_BLOCKS = 160
RIM_COT = 24
RIM_BLOCKS = 36
PACK_SECOND = 40
PACK_ROW = 72
PACK_BLOCKS = 76
UP, DOWN, COLS, KEEP, SIB_COLS, SIB_KEEP, RIM_SCALE, SIB_SCALE = range(8)
SECOND_AT = 24
EXTRA_AT = 36
GRAD_BLOCKS = 42


def dot(lhs, rhs, dims=(((1,), (0,)), ((), ()))):
    return lax.dot_general(lhs, rhs, dims, preferred_element_type=F32)


def sigmoid(values):
    return 1.0 / (1.0 + jnp.exp(-values))


def column_shifts(values):
    column = lax.broadcasted_iota(jnp.int32, (1, 16, values.shape[2]), 1)
    left = jnp.where(column == 0, 0.0, pltpu.roll(values, 1, 1))
    right = jnp.where(column == 15, 0.0, pltpu.roll(values, 15, 1))
    return left, right


def scale_of(scales, which):
    return scales[which : which + 1].reshape(1, 1, LAST)


def low_mask(scales, which):
    column = lax.broadcasted_iota(jnp.int32, (1, 16, LAST), 1).astype(F32)
    return jnp.where(column < scale_of(scales, which), 1.0, 0.0)


def high_mask(scales, which):
    column = lax.broadcasted_iota(jnp.int32, (1, 32, LAST), 1).astype(F32)
    return jnp.where(column < 2.0 * scale_of(scales, which), 1.0, 0.0)


def twice(values):
    return jnp.concatenate([values, values], 2)


def joined(blocks):
    halves = blocks.reshape(blocks.shape[0] // 2, 2, 16, LAST)
    return jnp.concatenate([halves[:, 0], halves[:, 1]], 2)


def tile_rows(tile_ref, frame):
    return joined(tile_ref[frame * 16 : frame * 16 + 16]).astype(F32)


def eff_frame(read, frame, keep):
    values = read(frame)
    return jnp.where(keep > 0.5, values, read(4)) if frame < 4 else values


def load_scales(clip_ref, cols_ref, start_ref):
    tile = lax.axis_index(TILE_AXES)
    tiles = lax.axis_size(TILE_AXES)
    even = lax.axis_index("core") == 0
    own = clip_ref[0, tile]
    up_same = (tile > 0) & (clip_ref[0, jnp.maximum(tile - 1, 0)] == own)
    down_same = (tile + 1 < tiles) & (clip_ref[0, jnp.minimum(tile + 1, tiles - 1)] == own)
    sibling = clip_ref[0, jnp.where(even, tile + 1, tile - 1)]
    up = jnp.where(up_same, 1.0, 0.0)
    down = jnp.where(down_same, 1.0, 0.0)
    return (
        up,
        down,
        cols_ref[0, own].astype(F32),
        jnp.where(start_ref[0, own] == 0, 0.0, 1.0),
        cols_ref[0, sibling].astype(F32),
        jnp.where(start_ref[0, sibling] == 0, 0.0, 1.0),
        jnp.where(even, up, down),
        jnp.where(even, down, up),
    )


def pack_kernel(
    clip_any, cols_any, start_any, in_any, cot_any, tile_ref, rim_ref, scales_ref,
    clip_ref, cols_ref, start_ref, in_ref, cot_ref, sems,
):
    copies = [
        pltpu.make_async_copy(source, target, sems.at[n])
        for n, (source, target) in enumerate(
            (
                (clip_any, clip_ref),
                (cols_any, cols_ref),
                (start_any, start_ref),
                (in_any, in_ref),
                (cot_any, cot_ref),
            )
        )
    ]
    for copy in copies:
        copy.start()
    for copy in copies[:3]:
        copy.wait()
    for row, value in enumerate(load_scales(clip_ref, cols_ref, start_ref)):
        scales_ref[row : row + 1] = jnp.full((1, LAST), value, F32)
    odd = lax.axis_index("core")
    copies[3].wait()
    for frame in range(6):
        for row in range(8):
            for half in range(2):
                tile_ref[frame * 16 + row * 2 + half] = in_ref[
                    frame, row, :, half * LAST : (half + 1) * LAST
                ]
    copies[4].wait()
    for frame in range(2):
        for half in range(2):
            for row in range(16):
                tile_ref[TILE_COT + frame * 32 + row * 2 + half] = cot_ref[
                    frame, row, half * 16 : (half + 1) * 16, :
                ]
    for frame in range(6):
        rim_ref[frame * 4 : frame * 4 + 4] = tile_ref[pl.ds(frame * 16 + odd * 12, 4)]
    for frame in range(2):
        at = RIM_COT + frame * 6
        rim_ref[at : at + 6] = tile_ref[pl.ds(TILE_COT + frame * 32 + odd * 26, 6)]


def pair_sums(rows, first, pair, put):
    zeros = jnp.zeros((pair.shape[0], 8, LAST), F32)
    pair[:, 0:8] = zeros
    pair[:, 40:48] = zeros
    count = rows.shape[0] - 1
    pair[0:count, 8:40] = rows[0:count] + rows[1 : count + 1]
    before, even, odd, after = (pair[0:count, pl.ds(begin, 16, 2), :] for begin in (7, 8, 9, 10))
    for kw, value in ((0, odd + after), (1, even + odd), (2, before + even)):
        put(kw, value.astype(BF))


def first_kernel(
    scales, tile_ref, sib_ref, rim_ref, w1_any, w2_any, packet_ref,
    w1_ref, w2_ref, act, rows, pair, cots, sems,
):
    load_w1 = pltpu.make_async_copy(w1_any, w1_ref, sems.at[0])
    load_w2 = pltpu.make_async_copy(w2_any, w2_ref, sems.at[1])
    load_w1.start()
    load_w2.start()
    odd = lax.axis_index("core")
    keep = twice(scale_of(scales, KEEP))
    low = low_mask(scales, COLS)
    wide_low = twice(low)
    rim_scale, sib_scale = scale_of(scales, RIM_SCALE), scale_of(scales, SIB_SCALE)
    rim_at = odd * 10
    sib_at = 10 - odd * 10

    for frame in range(6):
        for at, count, read, mask in (
            (rim_at, 2, lambda f: joined(rim_ref[f * 4 : f * 4 + 4]).astype(F32), wide_low * twice(rim_scale)),
            (2, 8, lambda f: tile_rows(tile_ref, f), wide_low),
            (sib_at, 2, lambda f: joined(sib_ref[pl.ds(f * 16 + odd * 12, 4)]).astype(F32), wide_low * twice(sib_scale)),
        ):
            values = eff_frame(read, frame, keep)
            values = values * sigmoid(values) * mask
            left, right = column_shifts(values)
            act[0, frame, pl.ds(at, count)] = left.astype(BF)
            act[1, frame, pl.ds(at, count)] = values.astype(BF)
            act[2, frame, pl.ds(at, count)] = right.astype(BF)

    high = high_mask(scales, COLS)
    for frame in range(2):
        at = TILE_COT + frame * 32
        rows[frame, 3:19] = tile_ref[at : at + 32].reshape(16, 32, LAST).astype(F32) * high
        raw = rim_ref[RIM_COT + frame * 6 : RIM_COT + frame * 6 + 6].reshape(3, 32, LAST)
        rows[frame, pl.ds(odd * 19, 3)] = raw.astype(F32) * (high * rim_scale)
        raw = sib_ref[pl.ds(at + odd * 26, 6)].reshape(3, 32, LAST)
        rows[frame, pl.ds(19 - odd * 19, 3)] = raw.astype(F32) * (high * sib_scale)
        far = rows[frame, pl.ds(2 + odd * 17, 1)].reshape(2, 16, LAST)
        packet_ref[PACK_ROW + frame * 2 : PACK_ROW + frame * 2 + 2] = far.astype(BF)

    load_w1.wait()
    first_out = None
    for step in range(9):
        kt, kh = step // 3, step % 3
        window = jnp.concatenate(
            [act[kw, kt : kt + 4, kh : kh + 10].reshape(640, 256) for kw in range(3)], 1
        )
        term = dot(window, w1_ref[step * 3 : step * 3 + 3].reshape(768, LAST))
        first_out = term if first_out is None else first_out + term
    first_out = first_out.reshape(40, 16, LAST)
    row = lax.broadcasted_iota(jnp.int32, (40, 1, 1), 0) % 10
    row_scale = jnp.where(
        row == 0, scale_of(scales, UP), jnp.where(row == 9, scale_of(scales, DOWN), 1.0)
    )
    gate = sigmoid(first_out)
    second_in = (first_out * gate * low).astype(BF).reshape(4, 10, 16, LAST)
    packet_ref[PACK_SECOND:PACK_ROW] = second_in[:, 1:9].reshape(32, 16, LAST)
    slope = gate * (1.0 + first_out * (1.0 - gate)) * (low * row_scale)

    for frame in range(2):

        def put(kw, sums):
            for n in range(21):
                if n % 2 == 1:
                    targets = ((1, n // 2),)
                else:
                    targets = ((0, n // 2 - 1), (2, n // 2))
                for kh, place in targets:
                    if 0 <= place < 10:
                        tap = kh * 3 + kw
                        cots[frame, place, :, tap * LAST : (tap + 1) * LAST] = sums[n]

        pair_sums(rows[frame], -3, pair, put)

    load_w2.wait()
    flat = jnp.concatenate(
        [
            jnp.concatenate([w2_ref[kt * 9 + tap] for tap in range(9)], 1)
            for kt in range(3)
        ],
        0,
    )
    spread = dot(cots[...].reshape(320, 1152), flat, NT)
    for frame in range(4):
        total = None
        for kt in range(3):
            if 0 <= frame - kt < 2:
                term = spread[
                    (frame - kt) * 160 : (frame - kt + 1) * 160, kt * LAST : (kt + 1) * LAST
                ]
                total = term if total is None else total + term
        first_grad = total.reshape(10, 16, LAST) * slope[frame * 10 : frame * 10 + 10]
        packet_ref[frame * 10 : frame * 10 + 10] = first_grad.astype(BF)


def input_kernel(
    scales, tile_ref, sib_ref, packet_ref, w1_any, grad_ref, act_ref, w1_ref, firsts, sems
):
    load_w1 = pltpu.make_async_copy(w1_any, w1_ref, sems.at[0])
    load_w1.start()
    for frame in range(4):
        first_grad = packet_ref[frame * 10 : frame * 10 + 10]
        before, after = column_shifts(first_grad.astype(F32))
        for kw, value in ((0, after.astype(BF)), (1, first_grad), (2, before.astype(BF))):
            for kh in range(3):
                tap = kh * 3 + kw
                firsts[frame, :, :, tap * LAST : (tap + 1) * LAST] = value[2 - kh : 10 - kh]
    load_w1.wait()
    shifted = firsts[...].reshape(512, 1152)
    by_depth = [
        dot(shifted, jnp.concatenate([w1_ref[kt * 9 + tap] for tap in range(9)], 1), NT)
        for kt in range(3)
    ]
    keep = twice(scale_of(scales, KEEP))
    low = twice(low_mask(scales, COLS))
    carried = None
    for frame in range(6):
        total = None
        for kt in range(3):
            if 0 <= frame - kt < 4:
                term = by_depth[kt][(frame - kt) * 128 : (frame - kt + 1) * 128]
                total = term if total is None else total + term
        values = eff_frame(lambda f: tile_rows(tile_ref, f), frame, keep)
        gate = sigmoid(values)
        act_ref[0, frame] = (values * gate * low).astype(BF)
        pre = total.reshape(8, 16, 256) * (gate * (1.0 + values * (1.0 - gate)) * low)
        if frame < 4:
            carried = pre if carried is None else carried + pre
            grad_ref[frame] = (pre * keep).astype(BF)
        elif frame == 4:
            grad_ref[frame] = (pre + carried * (1.0 - keep)).astype(BF)
        else:
            grad_ref[frame] = pre.astype(BF)
    keep = twice(scale_of(scales, SIB_KEEP))
    low = twice(low_mask(scales, SIB_COLS))
    for frame in range(6):
        values = eff_frame(lambda f: tile_rows(sib_ref, f), frame, keep)
        act_ref[1, frame] = (values * sigmoid(values) * low).astype(BF)


def weight_kernel(
    scales, tile_ref, sib_ref, packet_ref, sib_packet_ref, act_ref, part_ref, rows, pair, sums, cols
):
    odd = lax.axis_index("core")
    reps = part_ref.shape[0]
    link = scale_of(scales, SIB_SCALE)
    for own, tile, other, packet, which in (
        (True, tile_ref, sib_ref, packet_ref, COLS),
        (False, sib_ref, tile_ref, sib_packet_ref, SIB_COLS),
    ):
        slot = 0 if own else 1
        lower = odd if own else 1 - odd
        high = high_mask(scales, which)
        for frame in range(2):
            at = TILE_COT + frame * 32
            rows[1:17] = tile[at : at + 32].reshape(16, 32, LAST).astype(F32) * high
            far = packet[PACK_ROW + frame * 2 : PACK_ROW + frame * 2 + 2].reshape(1, 32, LAST)
            rows[pl.ds(lower * 17, 1)] = far.astype(F32)
            near = other[pl.ds(at + lower * 30, 2)].reshape(1, 32, LAST)
            rows[pl.ds(17 - lower * 17, 1)] = near.astype(F32) * (high * link)

            def put(kw, values):
                for n in range(17):
                    place = n // 2 if n % 2 == 0 else 9 + n // 2
                    sums[kw, slot, frame, place] = values[n]

            pair_sums(rows[...], -1, pair, put)
        for frame in range(4):
            first_grad = packet[frame * 10 : frame * 10 + 10]
            before, after = column_shifts(first_grad.astype(F32))
            cols[0, slot, frame] = after.astype(BF)
            cols[1, slot, frame] = first_grad
            cols[2, slot, frame] = before.astype(BF)

    act_all = jnp.concatenate([act_ref[:, kt : kt + 4].reshape(1024, 256) for kt in range(3)], 1)
    seconds = [
        ref[PACK_SECOND:PACK_ROW].reshape(4, 8, 16, LAST) for ref in (packet_ref, sib_packet_ref)
    ]
    second_all = jnp.concatenate(
        [
            jnp.concatenate([part[kt : kt + 2].reshape(256, LAST) for part in seconds], 0)
            for kt in range(3)
        ],
        1,
    )

    def put_block(block, at):
        part_ref[:, at] = block.astype(BF).reshape(reps, LAST // reps, LAST)

    def first_taps(step, at):
        tap = 5 * odd + step
        window = cols[tap % 3, :, :, pl.ds(2 - tap // 3, 8)].reshape(1024, LAST)
        block = dot(window, act_all, TN)
        for n in range(6):
            put_block(block[:, n * LAST : (n + 1) * LAST], at + n)

    def second_taps(step, at):
        tap = 4 * odd + step
        kh = tap // 3
        begin = jnp.where(kh == 0, 1, jnp.where(kh == 1, 9, 0))
        window = sums[tap % 3, :, :, pl.ds(begin, 8)].reshape(512, LAST)
        block = dot(window, second_all, TN)
        for n in range(3):
            put_block(block[:, n * LAST : (n + 1) * LAST], at + n)

    for step in range(4):
        first_taps(step, step * 6)
        second_taps(step, SECOND_AT + step * 3)

    @pl.when(odd == 0)
    def _():
        first_taps(4, EXTRA_AT)

    @pl.when(odd == 1)
    def _():
        second_taps(4, EXTRA_AT)
        part_ref[:, EXTRA_AT + 3 : EXTRA_AT + 6] = jnp.zeros((reps, 3, LAST // reps, LAST), BF)


def finish_kernel(scale, whole_ref, first_ref, second_ref):
    for core in range(2):

        def block(at):
            return whole_ref[core, at].astype(F32) * scale

        for step in range(5 - core):
            for kt in range(3):
                for half in range(2):
                    at = (step * 6 if step < 4 else EXTRA_AT) + kt * 2 + half
                    tap = kt * 9 + 5 * core + step
                    first_ref[tap, :, half * LAST : (half + 1) * LAST] = block(at)
        for step in range(4 + core):
            for kt in range(3):
                at = (SECOND_AT + step * 3 if step < 4 else EXTRA_AT) + kt
                second_ref[kt * 9 + 4 * core + step] = block(at)


VMEM = pl.BlockSpec(memory_space=pltpu.VMEM)
HBM = pl.BlockSpec(memory_space=pltpu.HBM)


def params(mebibytes):
    return pltpu.CompilerParams(vmem_limit_bytes=mebibytes << 20)


def cost(flops, moved):
    return pl.CostEstimate(flops=flops, bytes_accessed=moved, transcendentals=0)


def wide_sum(parts):
    return jnp.sum(parts.astype(F32), axis=0).astype(BF)


def blocks(count):
    return jax.ShapeDtypeStruct((count, 16, LAST), BF)


def body(inputs, cotangent, first_weight, second_weight, tile_clip, clip_cols, clip_start):
    tiles = lax.axis_size(TILE_AXES)
    reps, plane = lax.axis_size("x"), lax.axis_size(PLANE_AXES)
    local_in, local_cot, tile_clip, clip_cols, clip_start, w1, w2 = (
        pltpu.with_memory_space_constraint(array, pltpu.HBM)
        for array in (
            inputs[0],
            cotangent[0],
            tile_clip,
            clip_cols,
            clip_start,
            first_weight.reshape(27, 256, LAST),
            second_weight.reshape(27, LAST, LAST),
        )
    )
    tile, rim, scales = pl.pallas_call(
        pack_kernel,
        out_shape=(blocks(TILE_BLOCKS), blocks(RIM_BLOCKS), jax.ShapeDtypeStruct((8, LAST), F32)),
        in_specs=[HBM] * 5,
        out_specs=(VMEM, VMEM, VMEM),
        scratch_shapes=[
            pltpu.SMEM(tile_clip.shape, jnp.int32),
            pltpu.SMEM(clip_cols.shape, jnp.int32),
            pltpu.SMEM(clip_start.shape, jnp.int32),
            pltpu.VMEM(local_in.shape, BF),
            pltpu.VMEM(local_cot.shape, BF),
            pltpu.SemaphoreType.DMA((5,)),
        ],
        compiler_params=params(8),
    )(tile_clip, clip_cols, clip_start, local_in, local_cot)

    swap = [(0, 1), (1, 0)]
    across = [(i, (i + 1) % tiles) for i in range(1, tiles, 2)]
    across += [(b, a) for a, b in across]
    rim = lax.ppermute(rim, TILE_AXES, across)
    sibling = lax.ppermute(tile, "core", swap)

    packet = pl.pallas_call(
        first_kernel,
        out_shape=blocks(PACK_BLOCKS),
        in_specs=[VMEM] * 4 + [HBM] * 2,
        out_specs=VMEM,
        scratch_shapes=[
            pltpu.VMEM((27, 256, LAST), BF),
            pltpu.VMEM((27, LAST, LAST), BF),
            pltpu.VMEM((3, 6, 12, 16, 256), BF),
            pltpu.VMEM((2, 22, 32, LAST), F32),
            pltpu.VMEM((21, 48, LAST), F32),
            pltpu.VMEM((2, 10, 16, 9 * LAST), BF),
            pltpu.SemaphoreType.DMA((2,)),
        ],
        compiler_params=params(32),
        cost_estimate=cost(2 * 10**9, 4 * 10**6),
    )(scales, tile, sibling, rim, w1, w2)

    sib_packet = lax.ppermute(packet, "core", swap)

    input_grad, act = pl.pallas_call(
        input_kernel,
        out_shape=(
            jax.ShapeDtypeStruct(local_in.shape, BF),
            jax.ShapeDtypeStruct((2, 6, 8, 16, 256), BF),
        ),
        in_specs=[VMEM] * 4 + [HBM],
        out_specs=(VMEM, VMEM),
        scratch_shapes=[
            pltpu.VMEM((27, 256, LAST), BF),
            pltpu.VMEM((4, 8, 16, 9 * LAST), BF),
            pltpu.SemaphoreType.DMA((1,)),
        ],
        compiler_params=params(32),
        cost_estimate=cost(2 * 10**9, 4 * 10**6),
    )(scales, tile, sibling, packet, w1)

    depth = LAST // reps
    parts = pl.pallas_call(
        weight_kernel,
        out_shape=jax.ShapeDtypeStruct((reps, GRAD_BLOCKS, depth, LAST), BF),
        in_specs=[VMEM] * 6,
        out_specs=VMEM,
        scratch_shapes=[
            pltpu.VMEM((18, 32, LAST), F32),
            pltpu.VMEM((17, 48, LAST), F32),
            pltpu.VMEM((3, 2, 2, 17, 16, LAST), BF),
            pltpu.VMEM((3, 2, 4, 10, 16, LAST), BF),
        ],
        compiler_params=params(32),
        cost_estimate=cost(2 * 10**9, 4 * 10**6),
    )(scales, tile, sibling, packet, sib_packet, act)

    count = GRAD_BLOCKS * depth
    parts = parts.reshape(reps, count, LAST)
    of_rep = wide_sum(lax.all_to_all(parts, "x", 0, 0, tiled=True))
    share = -(-count // plane // 8) * 8
    of_rep = jnp.pad(of_rep, ((0, share * plane - count), (0, 0))).reshape(plane, share, LAST)
    own = wide_sum(lax.all_to_all(of_rep, PLANE_AXES, 0, 0, tiled=True))
    own = jnp.broadcast_to(own[None], (plane, share, LAST))
    half = lax.all_to_all(own, PLANE_AXES, 0, 0, tiled=True)
    half = half.reshape(plane * share, LAST)[:count]
    whole = lax.all_gather(half, "core", axis=0).reshape(2, GRAD_BLOCKS, depth, LAST)

    cell_total = tiles * reps * cotangent.shape[1] * cotangent.shape[2] * cotangent.shape[3]
    scale = 1.0 / math.sqrt(cell_total)
    first, second = pl.pallas_call(
        lambda *refs: finish_kernel(scale, *refs),
        out_shape=(
            jax.ShapeDtypeStruct((27, depth, 256), F32),
            jax.ShapeDtypeStruct((27, depth, LAST), F32),
        ),
        in_specs=[VMEM],
        out_specs=(VMEM, VMEM),
        compiler_params=params(16),
    )(whole)
    first = jnp.swapaxes(first, 1, 2).reshape(3, 3, 3, 256, depth)
    second = jnp.swapaxes(second, 1, 2).reshape(3, 3, 3, LAST, depth)
    return input_grad[None], first, second


def solution(mesh):
    devices = mesh.devices
    tiles, reps = devices.shape
    side = math.isqrt(tiles // 2)
    wide_mesh = Mesh(devices.reshape(side, tiles // 2 // side, 2, reps), ("y", "z", "core", "x"))
    in_specs = (
        P("x", None, TILE_AXES, None, None),
        P("x", None, TILE_AXES, None, None),
        P(),
        P(),
        P("x", None),
        P("x", None),
        P("x", None),
    )
    out_specs = (
        P("x", None, TILE_AXES, None, None),
        P(None, None, None, None, "x"),
        P(None, None, None, None, "x"),
    )
    return jax.shard_map(
        body, mesh=wide_mesh, in_specs=in_specs, out_specs=out_specs, check_vma=False
    )
```

```python
import math

import jax
import jax.numpy as jnp
from jax import lax
from jax.experimental import pallas as pl
from jax.experimental.pallas import tpu as pltpu
from jax.sharding import Mesh
from jax.sharding import PartitionSpec as P

TILE_AXES = ("y", "z", "core")
PLANE_AXES = ("y", "z")
BF = jnp.bfloat16
F32 = jnp.float32
NT = (((1,), (1,)), ((), ()))
TN = (((0,), (0,)), ((), ()))
LAST = 128
TILE_COT = 96
TILE_BLOCKS = 160
RIM_COT = 24
RIM_BLOCKS = 36
PACK_SECOND = 40
PACK_ROW = 72
PACK_BLOCKS = 76
UP, DOWN, COLS, KEEP, SIB_COLS, SIB_KEEP, RIM_SCALE, SIB_SCALE = range(8)
SECOND_AT = 24
EXTRA_AT = 36
GRAD_BLOCKS = 42


def dot(lhs, rhs, dims=(((1,), (0,)), ((), ()))):
    return lax.dot_general(lhs, rhs, dims, preferred_element_type=F32)


def sigmoid(values):
    return 1.0 / (1.0 + jnp.exp(-values))


def column_shifts(values):
    column = lax.broadcasted_iota(jnp.int32, (1, 16, values.shape[2]), 1)
    left = jnp.where(column == 0, 0.0, pltpu.roll(values, 1, 1))
    right = jnp.where(column == 15, 0.0, pltpu.roll(values, 15, 1))
    return left, right


def scale_of(scales, which):
    return scales[which : which + 1].reshape(1, 1, LAST)


def low_mask(scales, which):
    column = lax.broadcasted_iota(jnp.int32, (1, 16, LAST), 1).astype(F32)
    return jnp.where(column < scale_of(scales, which), 1.0, 0.0)


def high_mask(scales, which):
    column = lax.broadcasted_iota(jnp.int32, (1, 32, LAST), 1).astype(F32)
    return jnp.where(column < 2.0 * scale_of(scales, which), 1.0, 0.0)


def twice(values):
    return jnp.concatenate([values, values], 2)


def joined(blocks):
    halves = blocks.reshape(blocks.shape[0] // 2, 2, 16, LAST)
    return jnp.concatenate([halves[:, 0], halves[:, 1]], 2)


def tile_rows(tile_ref, frame):
    return joined(tile_ref[frame * 16 : frame * 16 + 16]).astype(F32)


def eff_frame(read, frame, keep):
    values = read(frame)
    return jnp.where(keep > 0.5, values, read(4)) if frame < 4 else values


def load_scales(clip_ref, cols_ref, start_ref):
    tile = lax.axis_index(TILE_AXES)
    tiles = lax.axis_size(TILE_AXES)
    even = lax.axis_index("core") == 0
    own = clip_ref[0, tile]
    up_same = (tile > 0) & (clip_ref[0, jnp.maximum(tile - 1, 0)] == own)
    down_same = (tile + 1 < tiles) & (clip_ref[0, jnp.minimum(tile + 1, tiles - 1)] == own)
    sibling = clip_ref[0, jnp.where(even, tile + 1, tile - 1)]
    up = jnp.where(up_same, 1.0, 0.0)
    down = jnp.where(down_same, 1.0, 0.0)
    return (
        up,
        down,
        cols_ref[0, own].astype(F32),
        jnp.where(start_ref[0, own] == 0, 0.0, 1.0),
        cols_ref[0, sibling].astype(F32),
        jnp.where(start_ref[0, sibling] == 0, 0.0, 1.0),
        jnp.where(even, up, down),
        jnp.where(even, down, up),
    )


def rim_kernel(in_any, cot_any, rim_ref, in_ref, cot_ref, sems):
    odd = lax.axis_index("core")
    copies = (
        pltpu.make_async_copy(in_any.at[:, pl.ds(odd * 6, 2)], in_ref, sems.at[0]),
        pltpu.make_async_copy(cot_any.at[:, pl.ds(odd * 13, 3)], cot_ref, sems.at[1]),
    )
    for copy in copies:
        copy.start()
    copies[0].wait()
    for frame in range(6):
        for row in range(2):
            for half in range(2):
                rim_ref[frame * 4 + row * 2 + half] = in_ref[
                    frame, row, :, half * LAST : (half + 1) * LAST
                ]
    copies[1].wait()
    for frame in range(2):
        for row in range(3):
            for half in range(2):
                rim_ref[RIM_COT + frame * 6 + row * 2 + half] = cot_ref[
                    frame, row, half * 16 : (half + 1) * 16, :
                ]


def pack_kernel(
    clip_any, cols_any, start_any, in_any, cot_any, rim_any, tile_ref, scales_ref,
    clip_ref, cols_ref, start_ref, in_ref, cot_ref, sems,
):
    copies = [
        pltpu.make_async_copy(source, target, sems.at[n])
        for n, (source, target) in enumerate(
            (
                (clip_any, clip_ref),
                (cols_any, cols_ref),
                (start_any, start_ref),
                (in_any, in_ref),
                (cot_any, cot_ref),
            )
        )
    ]
    for copy in copies:
        copy.start()
    for copy in copies[:3]:
        copy.wait()
    for row, value in enumerate(load_scales(clip_ref, cols_ref, start_ref)):
        scales_ref[row : row + 1] = jnp.full((1, LAST), value, F32)
    copies[3].wait()
    for frame in range(6):
        for row in range(8):
            for half in range(2):
                tile_ref[frame * 16 + row * 2 + half] = in_ref[
                    frame, row, :, half * LAST : (half + 1) * LAST
                ]
    copies[4].wait()
    for frame in range(2):
        for half in range(2):
            for row in range(16):
                tile_ref[TILE_COT + frame * 32 + row * 2 + half] = cot_ref[
                    frame, row, half * 16 : (half + 1) * 16, :
                ]


def pair_sums(rows, pair, put):
    count = rows.shape[0] - 1
    zeros = jnp.zeros((count, 8, LAST), F32)
    pair[0:count, 0:8] = zeros
    pair[0:count, 40:48] = zeros
    pair[0:count, 8:40] = rows[0:count] + rows[1 : count + 1]
    before, even, odd, after = (pair[0:count, pl.ds(begin, 16, 2), :] for begin in (7, 8, 9, 10))
    for kw, value in ((0, odd + after), (1, even + odd), (2, before + even)):
        put(kw, value.astype(BF))


def tap_sums(rows, first, begin, count, pair, cots):
    def put(kw, sums):
        for n in range(sums.shape[0]):
            row = first + n
            if row % 2 == 0:
                targets = ((1, row // 2),)
            else:
                targets = ((0, (row - 1) // 2), (2, (row + 1) // 2))
            for kh, place in targets:
                if begin <= place < begin + count:
                    tap = kh * 3 + kw
                    cots[place - begin, :, tap * LAST : (tap + 1) * LAST] = sums[n]

    pair_sums(rows, pair, put)


def shifted_act(act, at, values):
    left, right = column_shifts(values)
    for kw, shifted in enumerate((left, values, right)):
        act[(kw, *at)] = shifted.astype(BF)


def first_conv(windows, w1_ref):
    total = None
    for step in range(9):
        window = jnp.concatenate([windows(kw, step // 3, step % 3) for kw in range(3)], 1)
        term = dot(window, w1_ref[step * 3 : step * 3 + 3].reshape(768, LAST))
        total = term if total is None else total + term
    return total


def second_conv_back(cots, w2_ref, slope, put):
    flat = jnp.concatenate(
        [
            jnp.concatenate([w2_ref[kt * 9 + tap] for tap in range(9)], 1)
            for kt in range(3)
        ],
        0,
    )
    spread = dot(cots, flat, NT)
    cells = spread.shape[0] // 2
    for frame in range(4):
        total = None
        for kt in range(3):
            if 0 <= frame - kt < 2:
                term = spread[
                    (frame - kt) * cells : (frame - kt + 1) * cells, kt * LAST : (kt + 1) * LAST
                ]
                total = term if total is None else total + term
        put(frame, (total * slope[frame]).astype(BF))


def inner_kernel(
    scales, tile_ref, w1_any, w2_any, first_ref, second_ref, act_ref, w1_ref, w2_ref,
    act, pair, cots, sems,
):
    load_w1 = pltpu.make_async_copy(w1_any, w1_ref, sems.at[0])
    load_w2 = pltpu.make_async_copy(w2_any, w2_ref, sems.at[1])
    load_w1.start()
    load_w2.start()
    keep = twice(scale_of(scales, KEEP))
    low = low_mask(scales, COLS)
    for frame in range(6):
        values = eff_frame(lambda f: tile_rows(tile_ref, f), frame, keep)
        values = values * sigmoid(values) * twice(low)
        shifted_act(act, (frame,), values)
        act_ref[frame] = values.astype(BF)
    load_w1.wait()
    first_out = first_conv(
        lambda kw, kt, kh: act[kw, kt : kt + 4, kh : kh + 6].reshape(384, 256), w1_ref
    ).reshape(24, 16, LAST)
    gate = sigmoid(first_out)
    second_ref[...] = (first_out * gate * low).astype(BF).reshape(4, 6, 16, LAST)
    slope = gate * (1.0 + first_out * (1.0 - gate)) * low
    high = high_mask(scales, COLS)
    for frame in range(2):
        at = TILE_COT + frame * 32
        rows = tile_ref[at + 2 : at + 30].reshape(14, 32, LAST).astype(F32) * high
        tap_sums(rows, 1, 1, 6, pair, cots.at[frame])
    load_w2.wait()

    def put(frame, first_grad):
        first_ref[frame] = first_grad.reshape(6, 16, LAST)

    second_conv_back(cots[...].reshape(192, 1152), w2_ref, slope.reshape(4, 96, LAST), put)


def edge_kernel(
    scales, tile_ref, sib_ref, rim_ref, first_ref, second_ref, w1_ref, w2_ref, packet_ref,
    act, rows, pair, cots,
):
    odd = lax.axis_index("core")
    even = 1 - odd
    keep = twice(scale_of(scales, KEEP))
    low = low_mask(scales, COLS)
    wide_low = twice(low)
    rim_scale, sib_scale = scale_of(scales, RIM_SCALE), scale_of(scales, SIB_SCALE)
    for frame in range(6):
        for part, at, read, mask in (
            (odd, odd * 2, lambda f: joined(rim_ref[f * 4 : f * 4 + 4]), wide_low * twice(rim_scale)),
            (0, 2, lambda f: joined(tile_ref[f * 16 : f * 16 + 4]), wide_low),
            (1, 0, lambda f: joined(tile_ref[f * 16 + 12 : f * 16 + 16]), wide_low),
            (even, even * 2, lambda f: joined(sib_ref[pl.ds(f * 16 + odd * 12, 4)]), wide_low * twice(sib_scale)),
        ):
            values = eff_frame(lambda f, read=read: read(f).astype(F32), frame, keep)
            shifted_act(act, (frame, part, pl.ds(at, 2)), values * sigmoid(values) * mask)
    high = high_mask(scales, COLS)
    for frame in range(2):
        at = TILE_COT + frame * 32
        own = tile_ref[at : at + 32].reshape(16, 32, LAST)
        rows[frame, 0, 3:6] = own[0:3].astype(F32) * high
        rows[frame, 1, 0:3] = own[13:16].astype(F32) * high
        raw = rim_ref[RIM_COT + frame * 6 : RIM_COT + frame * 6 + 6].reshape(3, 32, LAST)
        rows[frame, odd, pl.ds(odd * 3, 3)] = raw.astype(F32) * (high * rim_scale)
        raw = sib_ref[pl.ds(at + odd * 26, 6)].reshape(3, 32, LAST)
        rows[frame, even, pl.ds(even * 3, 3)] = raw.astype(F32) * (high * sib_scale)
        far = rows[frame, odd, pl.ds(2 + odd, 1)].reshape(2, 16, LAST)
        packet_ref[PACK_ROW + frame * 2 : PACK_ROW + frame * 2 + 2] = far.astype(BF)
        tap_sums(rows[frame, 0], -3, -1, 2, pair, cots.at[frame, 0])
        tap_sums(rows[frame, 1], 13, 7, 2, pair, cots.at[frame, 1])
    first_out = first_conv(
        lambda kw, kt, kh: act[kw, kt : kt + 4, :, kh : kh + 2].reshape(256, 256), w1_ref
    ).reshape(16, 16, LAST)
    row = lax.broadcasted_iota(jnp.int32, (16, 1, 1), 0) % 4
    row_scale = jnp.where(
        row == 0, scale_of(scales, UP), jnp.where(row == 3, scale_of(scales, DOWN), 1.0)
    )
    gate = sigmoid(first_out)
    second_in = (first_out * gate * low).astype(BF)
    slope = gate * (1.0 + first_out * (1.0 - gate)) * (low * row_scale)
    for frame in range(4):
        at = PACK_SECOND + frame * 8
        packet_ref[at] = second_in[frame * 4 + 1]
        packet_ref[at + 1 : at + 7] = second_ref[frame]
        packet_ref[at + 7] = second_in[frame * 4 + 2]

    def put(frame, first_grad):
        blocks_now = first_grad.reshape(4, 16, LAST)
        packet_ref[frame * 10 : frame * 10 + 2] = blocks_now[0:2]
        packet_ref[frame * 10 + 2 : frame * 10 + 8] = first_ref[frame]
        packet_ref[frame * 10 + 8 : frame * 10 + 10] = blocks_now[2:4]

    second_conv_back(cots[...].reshape(128, 1152), w2_ref, slope.reshape(4, 64, LAST), put)


def sibling_kernel(scales, tile_ref, sib_ref, act_ref, sums_ref, rows, pair):
    keep = twice(scale_of(scales, SIB_KEEP))
    low = twice(low_mask(scales, SIB_COLS))
    for frame in range(6):
        values = eff_frame(lambda f: tile_rows(sib_ref, f), frame, keep)
        act_ref[frame] = (values * sigmoid(values) * low).astype(BF)
    odd = lax.axis_index("core")
    link = scale_of(scales, SIB_SCALE)
    rows[...] = jnp.zeros((18, 32, LAST), F32)
    for slot, tile, other, which in (
        (0, tile_ref, sib_ref, COLS),
        (1, sib_ref, tile_ref, SIB_COLS),
    ):
        lower = odd if slot == 0 else 1 - odd
        high = high_mask(scales, which)
        for frame in range(2):
            at = TILE_COT + frame * 32
            rows[1:17] = tile[at : at + 32].reshape(16, 32, LAST).astype(F32) * high
            near = other[pl.ds(at + lower * 30, 2)].reshape(1, 32, LAST)
            rows[pl.ds(17 - lower * 17, 1)] = near.astype(F32) * (high * link)

            def put(kw, values):
                for n in range(17):
                    place = n // 2 if n % 2 == 0 else 9 + n // 2
                    sums_ref[kw, slot, frame, place] = values[n]

            pair_sums(rows[...], pair, put)


def input_kernel(scales, tile_ref, packet_ref, w1_ref, grad_ref, firsts):
    for frame in range(4):
        first_grad = packet_ref[frame * 10 : frame * 10 + 10]
        before, after = column_shifts(first_grad.astype(F32))
        for kw, value in ((0, after.astype(BF)), (1, first_grad), (2, before.astype(BF))):
            for kh in range(3):
                tap = kh * 3 + kw
                firsts[frame, :, :, tap * LAST : (tap + 1) * LAST] = value[2 - kh : 10 - kh]
    shifted = firsts[...].reshape(512, 1152)
    by_depth = [
        dot(shifted, jnp.concatenate([w1_ref[kt * 9 + tap] for tap in range(9)], 1), NT)
        for kt in range(3)
    ]
    keep = twice(scale_of(scales, KEEP))
    low = twice(low_mask(scales, COLS))
    carried = None
    for frame in range(6):
        total = None
        for kt in range(3):
            if 0 <= frame - kt < 4:
                term = by_depth[kt][(frame - kt) * 128 : (frame - kt + 1) * 128]
                total = term if total is None else total + term
        values = eff_frame(lambda f: tile_rows(tile_ref, f), frame, keep)
        gate = sigmoid(values)
        pre = total.reshape(8, 16, 256) * (gate * (1.0 + values * (1.0 - gate)) * low)
        if frame < 4:
            carried = pre if carried is None else carried + pre
            grad_ref[frame] = (pre * keep).astype(BF)
        elif frame == 4:
            grad_ref[frame] = (pre + carried * (1.0 - keep)).astype(BF)
        else:
            grad_ref[frame] = pre.astype(BF)


def weight_kernel(
    scales, tile_ref, sib_ref, packet_ref, sib_packet_ref, act_ref, sib_act_ref, sums_ref,
    part_ref, pair, sums, cols,
):
    odd = lax.axis_index("core")
    reps = part_ref.shape[0]
    sums[...] = sums_ref[...]
    for slot, tile, packet, which in (
        (0, tile_ref, packet_ref, COLS),
        (1, sib_ref, sib_packet_ref, SIB_COLS),
    ):
        lower = odd if slot == 0 else 1 - odd
        high = high_mask(scales, which)
        for frame in range(2):
            far = packet[PACK_ROW + frame * 2 : PACK_ROW + frame * 2 + 2].reshape(1, 32, LAST)
            last = tile[pl.ds(TILE_COT + frame * 32 + lower * 30, 2)].reshape(1, 32, LAST)
            rows = jnp.concatenate([far.astype(F32), last.astype(F32) * high], 0)

            def put(kw, values):
                sums[kw, slot, frame, pl.ds(lower * 8, 1)] = values

            pair_sums(rows, pair, put)
        for frame in range(4):
            first_grad = packet[frame * 10 : frame * 10 + 10]
            before, after = column_shifts(first_grad.astype(F32))
            cols[0, slot, frame] = after.astype(BF)
            cols[1, slot, frame] = first_grad
            cols[2, slot, frame] = before.astype(BF)

    def both(refs, kt, frames):
        return jnp.concatenate(
            [ref[kt : kt + frames].reshape(frames * 128, ref.shape[3]) for ref in refs], 0
        )

    act_all = jnp.concatenate([both((act_ref, sib_act_ref), kt, 4) for kt in range(3)], 1)
    seconds = [
        ref[PACK_SECOND:PACK_ROW].reshape(4, 8, 16, LAST) for ref in (packet_ref, sib_packet_ref)
    ]
    second_all = jnp.concatenate([both(seconds, kt, 2) for kt in range(3)], 1)

    def put_block(block, at):
        part_ref[:, at] = block.astype(BF).reshape(reps, LAST // reps, LAST)

    def first_taps(step, at):
        tap = 5 * odd + step
        window = cols[tap % 3, :, :, pl.ds(2 - tap // 3, 8)].reshape(1024, LAST)
        block = dot(window, act_all, TN)
        for n in range(6):
            put_block(block[:, n * LAST : (n + 1) * LAST], at + n)

    def second_taps(step, at):
        tap = 4 * odd + step
        kh = tap // 3
        begin = jnp.where(kh == 0, 1, jnp.where(kh == 1, 9, 0))
        window = sums[tap % 3, :, :, pl.ds(begin, 8)].reshape(512, LAST)
        block = dot(window, second_all, TN)
        for n in range(3):
            put_block(block[:, n * LAST : (n + 1) * LAST], at + n)

    for step in range(4):
        first_taps(step, step * 6)
        second_taps(step, SECOND_AT + step * 3)

    @pl.when(odd == 0)
    def _():
        first_taps(4, EXTRA_AT)

    @pl.when(odd == 1)
    def _():
        second_taps(4, EXTRA_AT)
        part_ref[:, EXTRA_AT + 3 : EXTRA_AT + 6] = jnp.zeros((reps, 3, LAST // reps, LAST), BF)


def finish_kernel(scale, whole_ref, first_ref, second_ref):
    for core in range(2):

        def block(at):
            return whole_ref[core, at].astype(F32) * scale

        for step in range(5 - core):
            for kt in range(3):
                for half in range(2):
                    at = (step * 6 if step < 4 else EXTRA_AT) + kt * 2 + half
                    tap = kt * 9 + 5 * core + step
                    first_ref[tap, :, half * LAST : (half + 1) * LAST] = block(at)
        for step in range(4 + core):
            for kt in range(3):
                at = (SECOND_AT + step * 3 if step < 4 else EXTRA_AT) + kt
                second_ref[kt * 9 + 4 * core + step] = block(at)


VMEM = pl.BlockSpec(memory_space=pltpu.VMEM)
HBM = pl.BlockSpec(memory_space=pltpu.HBM)
ANY = pl.BlockSpec(memory_space=pl.ANY)


def params(mebibytes):
    return pltpu.CompilerParams(vmem_limit_bytes=mebibytes << 20)


def cost(flops, moved):
    return pl.CostEstimate(flops=flops, bytes_accessed=moved, transcendentals=0)


def wide_sum(parts):
    return jnp.sum(parts.astype(F32), axis=0).astype(BF)


def blocks(count):
    return jax.ShapeDtypeStruct((count, 16, LAST), BF)


def body(inputs, cotangent, first_weight, second_weight, tile_clip, clip_cols, clip_start):
    tiles = lax.axis_size(TILE_AXES)
    reps, plane = lax.axis_size("x"), lax.axis_size(PLANE_AXES)
    local_in, local_cot, tile_clip, clip_cols, clip_start, w1, w2 = (
        pltpu.with_memory_space_constraint(array, pltpu.HBM)
        for array in (
            inputs[0],
            cotangent[0],
            tile_clip,
            clip_cols,
            clip_start,
            first_weight.reshape(27, 256, LAST),
            second_weight.reshape(27, LAST, LAST),
        )
    )
    swap = [(0, 1), (1, 0)]
    across = [(i, (i + 1) % tiles) for i in range(1, tiles, 2)]
    across += [(b, a) for a, b in across]
    own_rim = pl.pallas_call(
        rim_kernel,
        out_shape=blocks(RIM_BLOCKS),
        in_specs=[HBM] * 2,
        out_specs=VMEM,
        scratch_shapes=[
            pltpu.VMEM((6, 2, 16, 256), BF),
            pltpu.VMEM((2, 3, 32, LAST), BF),
            pltpu.SemaphoreType.DMA((2,)),
        ],
        compiler_params=params(4),
        cost_estimate=cost(10**5, 3 * 10**5),
    )(local_in, local_cot)
    rim = lax.ppermute(own_rim, TILE_AXES, across)

    tile, scales = pl.pallas_call(
        pack_kernel,
        out_shape=(blocks(TILE_BLOCKS), jax.ShapeDtypeStruct((8, LAST), F32)),
        in_specs=[HBM] * 5 + [ANY],
        out_specs=(VMEM, VMEM),
        scratch_shapes=[
            pltpu.SMEM(tile_clip.shape, jnp.int32),
            pltpu.SMEM(clip_cols.shape, jnp.int32),
            pltpu.SMEM(clip_start.shape, jnp.int32),
            pltpu.VMEM(local_in.shape, BF),
            pltpu.VMEM(local_cot.shape, BF),
            pltpu.SemaphoreType.DMA((5,)),
        ],
        compiler_params=params(8),
        cost_estimate=cost(10**6, 2 * 10**6),
    )(tile_clip, clip_cols, clip_start, local_in, local_cot, own_rim)
    sibling = lax.ppermute(tile, "core", swap)

    inner_first, inner_second, act, w1, w2 = pl.pallas_call(
        inner_kernel,
        out_shape=(
            jax.ShapeDtypeStruct((4, 6, 16, LAST), BF),
            jax.ShapeDtypeStruct((4, 6, 16, LAST), BF),
            jax.ShapeDtypeStruct((6, 8, 16, 256), BF),
            jax.ShapeDtypeStruct(w1.shape, BF),
            jax.ShapeDtypeStruct(w2.shape, BF),
        ),
        in_specs=[VMEM] * 2 + [HBM] * 2,
        out_specs=(VMEM,) * 5,
        scratch_shapes=[
            pltpu.VMEM((3, 6, 8, 16, 256), BF),
            pltpu.VMEM((13, 48, LAST), F32),
            pltpu.VMEM((2, 6, 16, 9 * LAST), BF),
            pltpu.SemaphoreType.DMA((2,)),
        ],
        compiler_params=params(24),
        cost_estimate=cost(2 * 10**9, 4 * 10**6),
    )(scales, tile, w1, w2)

    sib_act, sums = pl.pallas_call(
        sibling_kernel,
        out_shape=(
            jax.ShapeDtypeStruct((6, 8, 16, 256), BF),
            jax.ShapeDtypeStruct((3, 2, 2, 17, 16, LAST), BF),
        ),
        in_specs=[VMEM] * 3,
        out_specs=(VMEM, VMEM),
        scratch_shapes=[
            pltpu.VMEM((18, 32, LAST), F32),
            pltpu.VMEM((17, 48, LAST), F32),
        ],
        compiler_params=params(16),
        cost_estimate=cost(10**9, 2 * 10**6),
    )(scales, tile, sibling)

    packet = pl.pallas_call(
        edge_kernel,
        out_shape=blocks(PACK_BLOCKS),
        in_specs=[VMEM] * 8,
        out_specs=VMEM,
        scratch_shapes=[
            pltpu.VMEM((3, 6, 2, 4, 16, 256), BF),
            pltpu.VMEM((2, 2, 6, 32, LAST), F32),
            pltpu.VMEM((5, 48, LAST), F32),
            pltpu.VMEM((2, 2, 2, 16, 9 * LAST), BF),
        ],
        compiler_params=params(16),
        cost_estimate=cost(10**9, 4 * 10**6),
    )(scales, tile, sibling, rim, inner_first, inner_second, w1, w2)
    sib_packet = lax.ppermute(packet, "core", swap)

    input_grad = pl.pallas_call(
        input_kernel,
        out_shape=jax.ShapeDtypeStruct(local_in.shape, BF),
        in_specs=[VMEM] * 4,
        out_specs=VMEM,
        scratch_shapes=[pltpu.VMEM((4, 8, 16, 9 * LAST), BF)],
        compiler_params=params(24),
        cost_estimate=cost(2 * 10**9, 4 * 10**6),
    )(scales, tile, packet, w1)

    depth = LAST // reps
    parts = pl.pallas_call(
        weight_kernel,
        out_shape=jax.ShapeDtypeStruct((reps, GRAD_BLOCKS, depth, LAST), BF),
        in_specs=[VMEM] * 8,
        out_specs=VMEM,
        scratch_shapes=[
            pltpu.VMEM((1, 48, LAST), F32),
            pltpu.VMEM((3, 2, 2, 17, 16, LAST), BF),
            pltpu.VMEM((3, 2, 4, 10, 16, LAST), BF),
        ],
        compiler_params=params(24),
        cost_estimate=cost(2 * 10**9, 4 * 10**6),
    )(scales, tile, sibling, packet, sib_packet, act, sib_act, sums)

    count = GRAD_BLOCKS * depth
    parts = parts.reshape(reps, count, LAST)
    of_rep = wide_sum(lax.all_to_all(parts, "x", 0, 0, tiled=True))
    share = -(-count // plane // 8) * 8
    of_rep = jnp.pad(of_rep, ((0, share * plane - count), (0, 0))).reshape(plane, share, LAST)
    own = wide_sum(lax.all_to_all(of_rep, PLANE_AXES, 0, 0, tiled=True))
    own = jnp.broadcast_to(own[None], (plane, share, LAST))
    half = lax.all_to_all(own, PLANE_AXES, 0, 0, tiled=True)
    half = half.reshape(plane * share, LAST)[:count]
    whole = lax.all_gather(half, "core", axis=0).reshape(2, GRAD_BLOCKS, depth, LAST)

    cell_total = tiles * reps * cotangent.shape[1] * cotangent.shape[2] * cotangent.shape[3]
    scale = 1.0 / math.sqrt(cell_total)
    first, second = pl.pallas_call(
        lambda *refs: finish_kernel(scale, *refs),
        out_shape=(
            jax.ShapeDtypeStruct((27, depth, 256), F32),
            jax.ShapeDtypeStruct((27, depth, LAST), F32),
        ),
        in_specs=[VMEM],
        out_specs=(VMEM, VMEM),
        compiler_params=params(16),
    )(whole)
    first = jnp.swapaxes(first, 1, 2).reshape(3, 3, 3, 256, depth)
    second = jnp.swapaxes(second, 1, 2).reshape(3, 3, 3, LAST, depth)
    return input_grad[None], first, second


def solution(mesh):
    devices = mesh.devices
    tiles, reps = devices.shape
    side = math.isqrt(tiles // 2)
    wide_mesh = Mesh(devices.reshape(side, tiles // 2 // side, 2, reps), ("y", "z", "core", "x"))
    in_specs = (
        P("x", None, TILE_AXES, None, None),
        P("x", None, TILE_AXES, None, None),
        P(),
        P(),
        P("x", None),
        P("x", None),
        P("x", None),
    )
    out_specs = (
        P("x", None, TILE_AXES, None, None),
        P(None, None, None, None, "x"),
        P(None, None, None, None, "x"),
    )
    return jax.shard_map(
        body, mesh=wide_mesh, in_specs=in_specs, out_specs=out_specs, check_vma=False
    )
```

```python
import math

import jax
import jax.numpy as jnp
from jax import lax
from jax.experimental import pallas as pl
from jax.experimental.pallas import tpu as pltpu
from jax.sharding import Mesh
from jax.sharding import PartitionSpec as P

TILE_AXES = ("yh", "yl", "zh", "zl", "core")
NEAR_AXES = ("yl", "x", "zl")
FAR_AXES = ("zh", "yh")
PLANE_AXES = ("yl", "zl", "zh", "yh")
BF = jnp.bfloat16
F32 = jnp.float32
NT = (((1,), (1,)), ((), ()))
TN = (((0,), (0,)), ((), ()))
LAST = 128
TILE_COT = 96
TILE_BLOCKS = 160
RIM_COT = 24
RIM_BLOCKS = 36
PACK_SECOND = 40
PACK_ROW = 72
PACK_BLOCKS = 76
UP, DOWN, COLS, KEEP, SIB_COLS, SIB_KEEP, RIM_SCALE, SIB_SCALE = range(8)
SECOND_AT = 24
EXTRA_AT = 36
GRAD_BLOCKS = 42


def dot(lhs, rhs, dims=(((1,), (0,)), ((), ()))):
    return lax.dot_general(lhs, rhs, dims, preferred_element_type=F32)


def sigmoid(values):
    return 1.0 / (1.0 + jnp.exp(-values))


def column_shifts(values):
    column = lax.broadcasted_iota(jnp.int32, (1, 16, values.shape[2]), 1)
    left = jnp.where(column == 0, 0.0, pltpu.roll(values, 1, 1))
    right = jnp.where(column == 15, 0.0, pltpu.roll(values, 15, 1))
    return left, right


def scale_of(scales, which):
    return scales[which : which + 1].reshape(1, 1, LAST)


def low_mask(scales, which):
    column = lax.broadcasted_iota(jnp.int32, (1, 16, LAST), 1).astype(F32)
    return jnp.where(column < scale_of(scales, which), 1.0, 0.0)


def high_mask(scales, which):
    column = lax.broadcasted_iota(jnp.int32, (1, 32, LAST), 1).astype(F32)
    return jnp.where(column < 2.0 * scale_of(scales, which), 1.0, 0.0)


def twice(values):
    return jnp.concatenate([values, values], 2)


def joined(blocks):
    halves = blocks.reshape(blocks.shape[0] // 2, 2, 16, LAST)
    return jnp.concatenate([halves[:, 0], halves[:, 1]], 2)


def tile_rows(tile_ref, frame):
    return joined(tile_ref[frame * 16 : frame * 16 + 16]).astype(F32)


def eff_frame(read, frame, keep):
    values = read(frame)
    return jnp.where(keep > 0.5, values, read(4)) if frame < 4 else values


def load_scales(clip_ref, cols_ref, start_ref):
    tile = lax.axis_index(TILE_AXES)
    tiles = lax.axis_size(TILE_AXES)
    even = lax.axis_index("core") == 0
    own = clip_ref[0, tile]
    up_same = (tile > 0) & (clip_ref[0, jnp.maximum(tile - 1, 0)] == own)
    down_same = (tile + 1 < tiles) & (clip_ref[0, jnp.minimum(tile + 1, tiles - 1)] == own)
    sibling = clip_ref[0, jnp.where(even, tile + 1, tile - 1)]
    up = jnp.where(up_same, 1.0, 0.0)
    down = jnp.where(down_same, 1.0, 0.0)
    return (
        up,
        down,
        cols_ref[0, own].astype(F32),
        jnp.where(start_ref[0, own] == 0, 0.0, 1.0),
        cols_ref[0, sibling].astype(F32),
        jnp.where(start_ref[0, sibling] == 0, 0.0, 1.0),
        jnp.where(even, up, down),
        jnp.where(even, down, up),
    )


def rim_kernel(in_any, cot_any, rim_ref, in_ref, cot_ref, sems):
    odd = lax.axis_index("core")
    copies = (
        pltpu.make_async_copy(in_any.at[:, pl.ds(odd * 6, 2)], in_ref, sems.at[0]),
        pltpu.make_async_copy(cot_any.at[:, pl.ds(odd * 13, 3)], cot_ref, sems.at[1]),
    )
    for copy in copies:
        copy.start()
    copies[0].wait()
    for frame in range(6):
        for row in range(2):
            for half in range(2):
                rim_ref[frame * 4 + row * 2 + half] = in_ref[
                    frame, row, :, half * LAST : (half + 1) * LAST
                ]
    copies[1].wait()
    for frame in range(2):
        for row in range(3):
            for half in range(2):
                rim_ref[RIM_COT + frame * 6 + row * 2 + half] = cot_ref[
                    frame, row, half * 16 : (half + 1) * 16, :
                ]


def pack_kernel(
    clip_any, cols_any, start_any, in_any, cot_any, rim_any, tile_ref, scales_ref,
    clip_ref, cols_ref, start_ref, in_ref, cot_ref, sems,
):
    copies = [
        pltpu.make_async_copy(source, target, sems.at[n])
        for n, (source, target) in enumerate(
            (
                (clip_any, clip_ref),
                (cols_any, cols_ref),
                (start_any, start_ref),
                (in_any, in_ref),
                (cot_any, cot_ref),
            )
        )
    ]
    for copy in copies:
        copy.start()
    for copy in copies[:3]:
        copy.wait()
    for row, value in enumerate(load_scales(clip_ref, cols_ref, start_ref)):
        scales_ref[row : row + 1] = jnp.full((1, LAST), value, F32)
    copies[3].wait()
    for frame in range(6):
        for row in range(8):
            for half in range(2):
                tile_ref[frame * 16 + row * 2 + half] = in_ref[
                    frame, row, :, half * LAST : (half + 1) * LAST
                ]
    copies[4].wait()
    for frame in range(2):
        for half in range(2):
            for row in range(16):
                tile_ref[TILE_COT + frame * 32 + row * 2 + half] = cot_ref[
                    frame, row, half * 16 : (half + 1) * 16, :
                ]


def pair_sums(rows, pair, put):
    count = rows.shape[0] - 1
    zeros = jnp.zeros((count, 8, LAST), F32)
    pair[0:count, 0:8] = zeros
    pair[0:count, 40:48] = zeros
    pair[0:count, 8:40] = rows[0:count] + rows[1 : count + 1]
    before, even, odd, after = (pair[0:count, pl.ds(begin, 16, 2), :] for begin in (7, 8, 9, 10))
    for kw, value in ((0, odd + after), (1, even + odd), (2, before + even)):
        put(kw, value.astype(BF))


def tap_sums(rows, first, begin, count, pair, cots):
    def put(kw, sums):
        for n in range(sums.shape[0]):
            row = first + n
            if row % 2 == 0:
                targets = ((1, row // 2),)
            else:
                targets = ((0, (row - 1) // 2), (2, (row + 1) // 2))
            for kh, place in targets:
                if begin <= place < begin + count:
                    tap = kh * 3 + kw
                    cots[place - begin, :, tap * LAST : (tap + 1) * LAST] = sums[n]

    pair_sums(rows, pair, put)


def shifted_act(act, at, values):
    left, right = column_shifts(values)
    for kw, shifted in enumerate((left, values, right)):
        act[(kw, *at)] = shifted.astype(BF)


def first_conv(windows, w1_ref):
    total = None
    for step in range(9):
        window = jnp.concatenate([windows(kw, step // 3, step % 3) for kw in range(3)], 1)
        term = dot(window, w1_ref[step * 3 : step * 3 + 3].reshape(768, LAST))
        total = term if total is None else total + term
    return total


def second_conv_back(cots, w2_ref, slope, put):
    flat = jnp.concatenate(
        [
            jnp.concatenate([w2_ref[kt * 9 + tap] for tap in range(9)], 1)
            for kt in range(3)
        ],
        0,
    )
    spread = dot(cots, flat, NT)
    cells = spread.shape[0] // 2
    for frame in range(4):
        total = None
        for kt in range(3):
            if 0 <= frame - kt < 2:
                term = spread[
                    (frame - kt) * cells : (frame - kt + 1) * cells, kt * LAST : (kt + 1) * LAST
                ]
                total = term if total is None else total + term
        put(frame, (total * slope[frame]).astype(BF))


def inner_kernel(
    scales, tile_ref, w1_any, w2_any, first_ref, second_ref, act_ref, w1_ref, w2_ref,
    act, pair, cots, sems,
):
    load_w1 = pltpu.make_async_copy(w1_any, w1_ref, sems.at[0])
    load_w2 = pltpu.make_async_copy(w2_any, w2_ref, sems.at[1])
    load_w1.start()
    load_w2.start()
    keep = twice(scale_of(scales, KEEP))
    low = low_mask(scales, COLS)
    for frame in range(6):
        values = eff_frame(lambda f: tile_rows(tile_ref, f), frame, keep)
        values = values * sigmoid(values) * twice(low)
        shifted_act(act, (frame,), values)
        act_ref[frame] = values.astype(BF)
    load_w1.wait()
    first_out = first_conv(
        lambda kw, kt, kh: act[kw, kt : kt + 4, kh : kh + 6].reshape(384, 256), w1_ref
    ).reshape(24, 16, LAST)
    gate = sigmoid(first_out)
    second_ref[...] = (first_out * gate * low).astype(BF).reshape(4, 6, 16, LAST)
    slope = gate * (1.0 + first_out * (1.0 - gate)) * low
    high = high_mask(scales, COLS)
    for frame in range(2):
        at = TILE_COT + frame * 32
        rows = tile_ref[at + 2 : at + 30].reshape(14, 32, LAST).astype(F32) * high
        tap_sums(rows, 1, 1, 6, pair, cots.at[frame])
    load_w2.wait()

    def put(frame, first_grad):
        first_ref[frame] = first_grad.reshape(6, 16, LAST)

    second_conv_back(cots[...].reshape(192, 1152), w2_ref, slope.reshape(4, 96, LAST), put)


def edge_kernel(
    rim_ref, scales, tile_ref, sib_ref, first_ref, second_ref, w1_ref, w2_ref, packet_ref,
    act, rows, pair, cots,
):
    odd = lax.axis_index("core")
    even = 1 - odd
    keep = twice(scale_of(scales, KEEP))
    low = low_mask(scales, COLS)
    wide_low = twice(low)
    rim_scale, sib_scale = scale_of(scales, RIM_SCALE), scale_of(scales, SIB_SCALE)
    for frame in range(6):
        for part, at, read, mask in (
            (odd, odd * 2, lambda f: joined(rim_ref[f * 4 : f * 4 + 4]), wide_low * twice(rim_scale)),
            (0, 2, lambda f: joined(tile_ref[f * 16 : f * 16 + 4]), wide_low),
            (1, 0, lambda f: joined(tile_ref[f * 16 + 12 : f * 16 + 16]), wide_low),
            (even, even * 2, lambda f: joined(sib_ref[pl.ds(f * 16 + odd * 12, 4)]), wide_low * twice(sib_scale)),
        ):
            values = eff_frame(lambda f, read=read: read(f).astype(F32), frame, keep)
            shifted_act(act, (frame, part, pl.ds(at, 2)), values * sigmoid(values) * mask)
    high = high_mask(scales, COLS)
    for frame in range(2):
        at = TILE_COT + frame * 32
        own = tile_ref[at : at + 32].reshape(16, 32, LAST)
        rows[frame, 0, 3:6] = own[0:3].astype(F32) * high
        rows[frame, 1, 0:3] = own[13:16].astype(F32) * high
        raw = rim_ref[RIM_COT + frame * 6 : RIM_COT + frame * 6 + 6].reshape(3, 32, LAST)
        rows[frame, odd, pl.ds(odd * 3, 3)] = raw.astype(F32) * (high * rim_scale)
        raw = sib_ref[pl.ds(at + odd * 26, 6)].reshape(3, 32, LAST)
        rows[frame, even, pl.ds(even * 3, 3)] = raw.astype(F32) * (high * sib_scale)
        far = rows[frame, odd, pl.ds(2 + odd, 1)].reshape(2, 16, LAST)
        packet_ref[PACK_ROW + frame * 2 : PACK_ROW + frame * 2 + 2] = far.astype(BF)
        tap_sums(rows[frame, 0], -3, -1, 2, pair, cots.at[frame, 0])
        tap_sums(rows[frame, 1], 13, 7, 2, pair, cots.at[frame, 1])
    first_out = first_conv(
        lambda kw, kt, kh: act[kw, kt : kt + 4, :, kh : kh + 2].reshape(256, 256), w1_ref
    ).reshape(16, 16, LAST)
    row = lax.broadcasted_iota(jnp.int32, (16, 1, 1), 0) % 4
    row_scale = jnp.where(
        row == 0, scale_of(scales, UP), jnp.where(row == 3, scale_of(scales, DOWN), 1.0)
    )
    gate = sigmoid(first_out)
    second_in = (first_out * gate * low).astype(BF)
    slope = gate * (1.0 + first_out * (1.0 - gate)) * (low * row_scale)
    for frame in range(4):
        at = PACK_SECOND + frame * 8
        packet_ref[at] = second_in[frame * 4 + 1]
        packet_ref[at + 1 : at + 7] = second_ref[frame]
        packet_ref[at + 7] = second_in[frame * 4 + 2]

    def put(frame, first_grad):
        blocks_now = first_grad.reshape(4, 16, LAST)
        packet_ref[frame * 10 : frame * 10 + 2] = blocks_now[0:2]
        packet_ref[frame * 10 + 2 : frame * 10 + 8] = first_ref[frame]
        packet_ref[frame * 10 + 8 : frame * 10 + 10] = blocks_now[2:4]

    second_conv_back(cots[...].reshape(128, 1152), w2_ref, slope.reshape(4, 64, LAST), put)


def sibling_kernel(scales, tile_ref, sib_ref, act_ref, sums_ref, rows, pair):
    keep = twice(scale_of(scales, SIB_KEEP))
    low = twice(low_mask(scales, SIB_COLS))
    for frame in range(6):
        values = eff_frame(lambda f: tile_rows(sib_ref, f), frame, keep)
        act_ref[frame] = (values * sigmoid(values) * low).astype(BF)
    odd = lax.axis_index("core")
    link = scale_of(scales, SIB_SCALE)
    rows[...] = jnp.zeros((18, 32, LAST), F32)
    for slot, tile, other, which in (
        (0, tile_ref, sib_ref, COLS),
        (1, sib_ref, tile_ref, SIB_COLS),
    ):
        lower = odd if slot == 0 else 1 - odd
        high = high_mask(scales, which)
        for frame in range(2):
            at = TILE_COT + frame * 32
            rows[1:17] = tile[at : at + 32].reshape(16, 32, LAST).astype(F32) * high
            near = other[pl.ds(at + lower * 30, 2)].reshape(1, 32, LAST)
            rows[pl.ds(17 - lower * 17, 1)] = near.astype(F32) * (high * link)

            def put(kw, values):
                for n in range(17):
                    place = n // 2 if n % 2 == 0 else 9 + n // 2
                    sums_ref[kw, slot, frame, place] = values[n]

            pair_sums(rows[...], pair, put)


def input_kernel(scales, in_any, packet_ref, w1_any, grad_ref, in_ref, w1_ref, firsts, sems):
    load_in = pltpu.make_async_copy(in_any, in_ref, sems.at[0])
    load_w1 = pltpu.make_async_copy(w1_any, w1_ref, sems.at[1])
    load_w1.start()
    load_in.start()
    for frame in range(4):
        first_grad = packet_ref[frame * 10 : frame * 10 + 10]
        before, after = column_shifts(first_grad.astype(F32))
        for kw, value in ((0, after.astype(BF)), (1, first_grad), (2, before.astype(BF))):
            for kh in range(3):
                tap = kh * 3 + kw
                firsts[frame, :, :, tap * LAST : (tap + 1) * LAST] = value[2 - kh : 10 - kh]
    load_w1.wait()
    load_in.wait()
    shifted = firsts[...].reshape(512, 1152)
    by_depth = [
        dot(shifted, jnp.concatenate([w1_ref[kt * 9 + tap] for tap in range(9)], 1), NT)
        for kt in range(3)
    ]
    keep = twice(scale_of(scales, KEEP))
    low = twice(low_mask(scales, COLS))
    carried = None
    for frame in range(6):
        total = None
        for kt in range(3):
            if 0 <= frame - kt < 4:
                term = by_depth[kt][(frame - kt) * 128 : (frame - kt + 1) * 128]
                total = term if total is None else total + term
        values = eff_frame(lambda f: in_ref[f].astype(F32), frame, keep)
        gate = sigmoid(values)
        pre = total.reshape(8, 16, 256) * (gate * (1.0 + values * (1.0 - gate)) * low)
        if frame < 4:
            carried = pre if carried is None else carried + pre
            grad_ref[frame] = (pre * keep).astype(BF)
        elif frame == 4:
            grad_ref[frame] = (pre + carried * (1.0 - keep)).astype(BF)
        else:
            grad_ref[frame] = pre.astype(BF)


def weight_kernel(
    scales, tile_ref, sib_ref, packet_ref, sib_packet_ref, act_ref, sib_act_ref, sums_ref,
    part_ref, pair, sums, cols,
):
    odd = lax.axis_index("core")
    near_y, reps, near_z, per_quarter, depth = part_ref.shape[:5]
    sums[...] = sums_ref[...]
    for slot, tile, packet, which in (
        (0, tile_ref, packet_ref, COLS),
        (1, sib_ref, sib_packet_ref, SIB_COLS),
    ):
        lower = odd if slot == 0 else 1 - odd
        high = high_mask(scales, which)
        for frame in range(2):
            far = packet[PACK_ROW + frame * 2 : PACK_ROW + frame * 2 + 2].reshape(1, 32, LAST)
            last = tile[pl.ds(TILE_COT + frame * 32 + lower * 30, 2)].reshape(1, 32, LAST)
            rows = jnp.concatenate([far.astype(F32), last.astype(F32) * high], 0)

            def put(kw, values):
                sums[kw, slot, frame, pl.ds(lower * 8, 1)] = values

            pair_sums(rows, pair, put)
        for frame in range(4):
            first_grad = packet[frame * 10 : frame * 10 + 10]
            before, after = column_shifts(first_grad.astype(F32))
            cols[0, slot, frame] = after.astype(BF)
            cols[1, slot, frame] = first_grad
            cols[2, slot, frame] = before.astype(BF)

    def both(refs, kt, frames):
        return jnp.concatenate(
            [ref[kt : kt + frames].reshape(frames * 128, ref.shape[3]) for ref in refs], 0
        )

    act_all = jnp.concatenate([both((act_ref, sib_act_ref), kt, 4) for kt in range(3)], 1)
    seconds = [
        ref[PACK_SECOND:PACK_ROW].reshape(4, 8, 16, LAST) for ref in (packet_ref, sib_packet_ref)
    ]
    second_all = jnp.concatenate([both(seconds, kt, 2) for kt in range(3)], 1)

    def put_block(block, at):
        halves = block.astype(BF).reshape(reps, 2, depth, LAST)
        for half in range(2):
            quarter, place = divmod(at * 2 + half, per_quarter)
            part_ref[quarter // near_z, :, quarter % near_z, place] = halves[:, half]

    def first_taps(step, at):
        tap = 5 * odd + step
        window = cols[tap % 3, :, :, pl.ds(2 - tap // 3, 8)].reshape(1024, LAST)
        block = dot(window, act_all, TN)
        for n in range(6):
            put_block(block[:, n * LAST : (n + 1) * LAST], at + n)

    def second_taps(step, at):
        tap = 4 * odd + step
        kh = tap // 3
        begin = jnp.where(kh == 0, 1, jnp.where(kh == 1, 9, 0))
        window = sums[tap % 3, :, :, pl.ds(begin, 8)].reshape(512, LAST)
        block = dot(window, second_all, TN)
        for n in range(3):
            put_block(block[:, n * LAST : (n + 1) * LAST], at + n)

    for step in range(4):
        first_taps(step, step * 6)
        second_taps(step, SECOND_AT + step * 3)

    @pl.when(odd == 0)
    def _():
        first_taps(4, EXTRA_AT)

    @pl.when(odd == 1)
    def _():
        second_taps(4, EXTRA_AT)
        for at in range(EXTRA_AT + 3, EXTRA_AT + 6):
            put_block(jnp.zeros((LAST, LAST), F32), at)


def near_sum_kernel(parts_ref, scales, sum_ref, token_ref):
    token_ref[...] = scales[...]
    rows = parts_ref.shape[1]
    total = parts_ref[0].astype(F32)
    for n in range(1, parts_ref.shape[0]):
        total = total + parts_ref[n].astype(F32)
    sum_ref[0:rows] = total.astype(BF)
    if sum_ref.shape[0] > rows:
        sum_ref[rows:] = jnp.zeros((sum_ref.shape[0] - rows, LAST), BF)


def far_sum_kernel(parts_ref, _, copies_ref):
    total = parts_ref[0].astype(F32)
    for n in range(1, parts_ref.shape[0]):
        total = total + parts_ref[n].astype(F32)
    copies_ref[...] = jnp.broadcast_to(total.astype(BF)[None], copies_ref.shape)


def finish_kernel(scale, per_quarter, whole_ref, first_ref, second_ref):
    depth = first_ref.shape[1] // 2
    for core in range(2):

        def put(target, tap, columns, at):
            for half in range(2):
                quarter, place = divmod(at * 2 + half, per_quarter)
                rows = whole_ref[core, quarter, place * depth : (place + 1) * depth]
                target[tap, half * depth : (half + 1) * depth, columns] = rows.astype(F32) * scale

        for step in range(5 - core):
            for kt in range(3):
                for half in range(2):
                    at = (step * 6 if step < 4 else EXTRA_AT) + kt * 2 + half
                    columns = slice(half * LAST, (half + 1) * LAST)
                    put(first_ref, kt * 9 + 5 * core + step, columns, at)
        for step in range(4 + core):
            for kt in range(3):
                at = (SECOND_AT + step * 3 if step < 4 else EXTRA_AT) + kt
                put(second_ref, kt * 9 + 4 * core + step, slice(0, LAST), at)


VMEM = pl.BlockSpec(memory_space=pltpu.VMEM)
HBM = pl.BlockSpec(memory_space=pltpu.HBM)
ANY = pl.BlockSpec(memory_space=pl.ANY)


def params(mebibytes):
    return pltpu.CompilerParams(vmem_limit_bytes=mebibytes << 20)


def cost(flops, moved):
    return pl.CostEstimate(flops=flops, bytes_accessed=moved, transcendentals=0)


def wide_sum(parts):
    return jnp.sum(parts.astype(F32), axis=0).astype(BF)


def blocks(count):
    return jax.ShapeDtypeStruct((count, 16, LAST), BF)


def body(inputs, cotangent, first_weight, second_weight, tile_clip, clip_cols, clip_start):
    tiles = lax.axis_size(TILE_AXES)
    reps, near_y, near_z = (lax.axis_size(name) for name in ("x", "yl", "zl"))
    far, plane = lax.axis_size(FAR_AXES), lax.axis_size(PLANE_AXES)
    local_in, local_cot, tile_clip, clip_cols, clip_start, w1, w2 = (
        pltpu.with_memory_space_constraint(array, pltpu.HBM)
        for array in (
            inputs[0],
            cotangent[0],
            tile_clip,
            clip_cols,
            clip_start,
            first_weight.reshape(27, 256, LAST),
            second_weight.reshape(27, LAST, LAST),
        )
    )
    swap = [(0, 1), (1, 0)]
    across = [(i, (i + 1) % tiles) for i in range(1, tiles, 2)]
    across += [(b, a) for a, b in across]
    own_rim = pl.pallas_call(
        rim_kernel,
        out_shape=blocks(RIM_BLOCKS),
        in_specs=[HBM] * 2,
        out_specs=VMEM,
        scratch_shapes=[
            pltpu.VMEM((6, 2, 16, 256), BF),
            pltpu.VMEM((2, 3, 32, LAST), BF),
            pltpu.SemaphoreType.DMA((2,)),
        ],
        compiler_params=params(4),
        cost_estimate=cost(10**5, 3 * 10**5),
    )(local_in, local_cot)
    rim = lax.ppermute(own_rim, TILE_AXES, across)

    tile, scales = pl.pallas_call(
        pack_kernel,
        out_shape=(blocks(TILE_BLOCKS), jax.ShapeDtypeStruct((8, LAST), F32)),
        in_specs=[HBM] * 5 + [ANY],
        out_specs=(VMEM, VMEM),
        scratch_shapes=[
            pltpu.SMEM(tile_clip.shape, jnp.int32),
            pltpu.SMEM(clip_cols.shape, jnp.int32),
            pltpu.SMEM(clip_start.shape, jnp.int32),
            pltpu.VMEM(local_in.shape, BF),
            pltpu.VMEM(local_cot.shape, BF),
            pltpu.SemaphoreType.DMA((5,)),
        ],
        compiler_params=params(8),
        cost_estimate=cost(10**6, 2 * 10**6),
    )(tile_clip, clip_cols, clip_start, local_in, local_cot, own_rim)
    sibling = lax.ppermute(tile, "core", swap)

    inner_first, inner_second, act, inner_w1, inner_w2 = pl.pallas_call(
        inner_kernel,
        out_shape=(
            jax.ShapeDtypeStruct((4, 6, 16, LAST), BF),
            jax.ShapeDtypeStruct((4, 6, 16, LAST), BF),
            jax.ShapeDtypeStruct((6, 8, 16, 256), BF),
            jax.ShapeDtypeStruct(w1.shape, BF),
            jax.ShapeDtypeStruct(w2.shape, BF),
        ),
        in_specs=[VMEM] * 2 + [HBM] * 2,
        out_specs=(VMEM,) * 5,
        scratch_shapes=[
            pltpu.VMEM((3, 6, 8, 16, 256), BF),
            pltpu.VMEM((13, 48, LAST), F32),
            pltpu.VMEM((2, 6, 16, 9 * LAST), BF),
            pltpu.SemaphoreType.DMA((2,)),
        ],
        compiler_params=params(24),
        cost_estimate=cost(2 * 10**9, 4 * 10**6),
    )(scales, tile, w1, w2)

    sib_act, sums = pl.pallas_call(
        sibling_kernel,
        out_shape=(
            jax.ShapeDtypeStruct((6, 8, 16, 256), BF),
            jax.ShapeDtypeStruct((3, 2, 2, 17, 16, LAST), BF),
        ),
        in_specs=[VMEM] * 3,
        out_specs=(VMEM, VMEM),
        scratch_shapes=[
            pltpu.VMEM((18, 32, LAST), F32),
            pltpu.VMEM((17, 48, LAST), F32),
        ],
        compiler_params=params(16),
        cost_estimate=cost(10**9, 2 * 10**6),
    )(scales, tile, sibling)

    packet = pl.pallas_call(
        edge_kernel,
        out_shape=blocks(PACK_BLOCKS),
        in_specs=[VMEM] * 8,
        out_specs=VMEM,
        scratch_shapes=[
            pltpu.VMEM((3, 6, 2, 4, 16, 256), BF),
            pltpu.VMEM((2, 2, 6, 32, LAST), F32),
            pltpu.VMEM((5, 48, LAST), F32),
            pltpu.VMEM((2, 2, 2, 16, 9 * LAST), BF),
        ],
        compiler_params=params(16),
        cost_estimate=cost(10**9, 4 * 10**6),
    )(rim, scales, tile, sibling, inner_first, inner_second, inner_w1, inner_w2)
    sib_packet = lax.ppermute(packet, "core", swap)

    depth = LAST // reps
    quarters = near_y * near_z
    per_quarter = 2 * GRAD_BLOCKS // quarters
    parts = pl.pallas_call(
        weight_kernel,
        out_shape=jax.ShapeDtypeStruct(
            (near_y, reps, near_z, per_quarter, depth // 2, LAST), BF
        ),
        in_specs=[VMEM] * 8,
        out_specs=VMEM,
        scratch_shapes=[
            pltpu.VMEM((1, 48, LAST), F32),
            pltpu.VMEM((3, 2, 2, 17, 16, LAST), BF),
            pltpu.VMEM((3, 2, 4, 10, 16, LAST), BF),
        ],
        compiler_params=params(24),
        cost_estimate=cost(2 * 10**9, 4 * 10**6),
    )(scales, tile, sibling, packet, sib_packet, act, sib_act, sums)

    count = per_quarter * depth // 2
    share = -(-count // far // 8) * 8
    parts = parts.reshape(near_y * reps * near_z, count, LAST)
    near, token = pl.pallas_call(
        near_sum_kernel,
        out_shape=(
            jax.ShapeDtypeStruct((far * share, LAST), BF),
            jax.ShapeDtypeStruct(scales.shape, F32),
        ),
        in_specs=[VMEM, VMEM],
        out_specs=(VMEM, VMEM),
        compiler_params=params(8),
        cost_estimate=cost(10**6, 2 * 10**6),
    )(lax.all_to_all(parts, NEAR_AXES, 0, 0, tiled=True), scales)
    input_grad = pl.pallas_call(
        input_kernel,
        out_shape=jax.ShapeDtypeStruct(local_in.shape, BF),
        in_specs=[VMEM, HBM, VMEM, HBM],
        out_specs=VMEM,
        scratch_shapes=[
            pltpu.VMEM(local_in.shape, BF),
            pltpu.VMEM(w1.shape, BF),
            pltpu.VMEM((4, 8, 16, 9 * LAST), BF),
            pltpu.SemaphoreType.DMA((2,)),
        ],
        compiler_params=params(24),
        cost_estimate=cost(2 * 10**9, 4 * 10**6),
    )(token, local_in, packet, w1)

    near = near.reshape(far, share, LAST)
    copies = pl.pallas_call(
        far_sum_kernel,
        out_shape=jax.ShapeDtypeStruct((plane, share, LAST), BF),
        in_specs=[VMEM, ANY],
        out_specs=VMEM,
        compiler_params=params(8),
        cost_estimate=cost(10**5, 5 * 10**5),
    )(
        lax.all_to_all(near, FAR_AXES, 0, 0, tiled=True),
        pltpu.with_memory_space_constraint(input_grad, pltpu.HBM),
    )
    half = lax.all_to_all(copies, PLANE_AXES, 0, 0, tiled=True)
    whole = lax.all_gather(half.reshape(quarters, far * share, LAST), "core", axis=0)

    cell_total = tiles * reps * cotangent.shape[1] * cotangent.shape[2] * cotangent.shape[3]
    scale = 1.0 / math.sqrt(cell_total)
    first, second = pl.pallas_call(
        lambda *refs: finish_kernel(scale, per_quarter, *refs),
        out_shape=(
            jax.ShapeDtypeStruct((27, depth, 256), F32),
            jax.ShapeDtypeStruct((27, depth, LAST), F32),
        ),
        in_specs=[VMEM],
        out_specs=(VMEM, VMEM),
        compiler_params=params(16),
    )(whole)
    first = jnp.swapaxes(first, 1, 2).reshape(3, 3, 3, 256, depth)
    second = jnp.swapaxes(second, 1, 2).reshape(3, 3, 3, LAST, depth)
    return input_grad[None], first, second


def solution(mesh):
    devices = mesh.devices
    tiles, reps = devices.shape
    height = math.isqrt(tiles // 2)
    width = tiles // 2 // height
    near_y, near_z = math.gcd(height, 2), math.gcd(width, 2)
    wide_mesh = Mesh(
        devices.reshape(height // near_y, near_y, width // near_z, near_z, 2, reps),
        (*TILE_AXES, "x"),
    )
    in_specs = (
        P("x", None, TILE_AXES, None, None),
        P("x", None, TILE_AXES, None, None),
        P(),
        P(),
        P("x", None),
        P("x", None),
        P("x", None),
    )
    out_specs = (
        P("x", None, TILE_AXES, None, None),
        P(None, None, None, None, "x"),
        P(None, None, None, None, "x"),
    )
    return jax.shard_map(
        body, mesh=wide_mesh, in_specs=in_specs, out_specs=out_specs, check_vma=False
    )
```

```python
import math

import jax
import jax.numpy as jnp
from jax import lax
from jax.experimental import pallas as pl
from jax.experimental.pallas import tpu as pltpu
from jax.sharding import Mesh
from jax.sharding import PartitionSpec as P

TILE_AXES = ("yh", "yl", "zh", "zl", "core")
NEAR_AXES = ("yl", "x", "zl")
FAR_AXES = ("zh", "yh")
PLANE_AXES = ("yl", "zl", "zh", "yh")
BF = jnp.bfloat16
F32 = jnp.float32
NT = (((1,), (1,)), ((), ()))
TN = (((0,), (0,)), ((), ()))
LAST = 128
TILE_COT = 96
TILE_BLOCKS = 160
RIM_COT = 24
RIM_BLOCKS = 36
PACK_SECOND = 40
PACK_ROW = 72
PACK_BLOCKS = 76
UP, DOWN, COLS, KEEP, SIB_COLS, SIB_KEEP, RIM_SCALE, SIB_SCALE = range(8)
SECOND_AT = 24
EXTRA_AT = 36
GRAD_BLOCKS = 42


def dot(lhs, rhs, dims=(((1,), (0,)), ((), ()))):
    return lax.dot_general(lhs, rhs, dims, preferred_element_type=F32)


def sigmoid(values):
    return 1.0 / (1.0 + jnp.exp(-values))


def column_shifts(values):
    column = lax.broadcasted_iota(jnp.int32, (1, 16, values.shape[2]), 1)
    left = jnp.where(column == 0, 0.0, pltpu.roll(values, 1, 1))
    right = jnp.where(column == 15, 0.0, pltpu.roll(values, 15, 1))
    return left, right


def scale_of(scales, which):
    return scales[which : which + 1].reshape(1, 1, LAST)


def low_mask(scales, which):
    column = lax.broadcasted_iota(jnp.int32, (1, 16, LAST), 1).astype(F32)
    return jnp.where(column < scale_of(scales, which), 1.0, 0.0)


def high_mask(scales, which):
    column = lax.broadcasted_iota(jnp.int32, (1, 32, LAST), 1).astype(F32)
    return jnp.where(column < 2.0 * scale_of(scales, which), 1.0, 0.0)


def twice(values):
    return jnp.concatenate([values, values], 2)


def joined(blocks):
    halves = blocks.reshape(blocks.shape[0] // 2, 2, 16, LAST)
    return jnp.concatenate([halves[:, 0], halves[:, 1]], 2)


def tile_rows(tile_ref, frame):
    return joined(tile_ref[frame * 16 : frame * 16 + 16]).astype(F32)


def eff_frame(read, frame, keep):
    values = read(frame)
    return jnp.where(keep > 0.5, values, read(4)) if frame < 4 else values


def load_scales(clip_ref, cols_ref, start_ref):
    tile = lax.axis_index(TILE_AXES)
    tiles = lax.axis_size(TILE_AXES)
    even = lax.axis_index("core") == 0
    own = clip_ref[0, tile]
    up_same = (tile > 0) & (clip_ref[0, jnp.maximum(tile - 1, 0)] == own)
    down_same = (tile + 1 < tiles) & (clip_ref[0, jnp.minimum(tile + 1, tiles - 1)] == own)
    sibling = clip_ref[0, jnp.where(even, tile + 1, tile - 1)]
    up = jnp.where(up_same, 1.0, 0.0)
    down = jnp.where(down_same, 1.0, 0.0)
    return (
        up,
        down,
        cols_ref[0, own].astype(F32),
        jnp.where(start_ref[0, own] == 0, 0.0, 1.0),
        cols_ref[0, sibling].astype(F32),
        jnp.where(start_ref[0, sibling] == 0, 0.0, 1.0),
        jnp.where(even, up, down),
        jnp.where(even, down, up),
    )


def pack_kernel(
    clip_any, cols_any, start_any, in_any, cot_any, rim_ref, tile_ref, scales_ref,
    clip_ref, cols_ref, start_ref, in_ref, cot_ref, sems,
):
    copies = [
        pltpu.make_async_copy(source, target, sems.at[n])
        for n, (source, target) in enumerate(
            (
                (clip_any, clip_ref),
                (cols_any, cols_ref),
                (start_any, start_ref),
                (in_any, in_ref),
                (cot_any, cot_ref),
            )
        )
    ]
    for copy in copies:
        copy.start()
    copies[3].wait()
    for frame in range(6):
        for row in range(8):
            for half in range(2):
                tile_ref[frame * 16 + row * 2 + half] = in_ref[
                    frame, row, :, half * LAST : (half + 1) * LAST
                ]
    copies[4].wait()
    for frame in range(2):
        for half in range(2):
            for row in range(16):
                tile_ref[TILE_COT + frame * 32 + row * 2 + half] = cot_ref[
                    frame, row, half * 16 : (half + 1) * 16, :
                ]
    odd = lax.axis_index("core")
    for frame in range(6):
        rim_ref[frame * 4 : frame * 4 + 4] = tile_ref[pl.ds(frame * 16 + odd * 12, 4)]
    for frame in range(2):
        at = RIM_COT + frame * 6
        rim_ref[at : at + 6] = tile_ref[pl.ds(TILE_COT + frame * 32 + odd * 26, 6)]
    for copy in copies[:3]:
        copy.wait()
    for row, value in enumerate(load_scales(clip_ref, cols_ref, start_ref)):
        scales_ref[row : row + 1] = jnp.full((1, LAST), value, F32)


def pair_sums(rows, pair, put):
    count = rows.shape[0] - 1
    zeros = jnp.zeros((count, 8, LAST), F32)
    pair[0:count, 0:8] = zeros
    pair[0:count, 40:48] = zeros
    pair[0:count, 8:40] = rows[0:count] + rows[1 : count + 1]
    before, even, odd, after = (pair[0:count, pl.ds(begin, 16, 2), :] for begin in (7, 8, 9, 10))
    for kw, value in ((0, odd + after), (1, even + odd), (2, before + even)):
        put(kw, value.astype(BF))


def tap_sums(rows, first, begin, count, pair, cots):
    def put(kw, sums):
        for n in range(sums.shape[0]):
            row = first + n
            if row % 2 == 0:
                targets = ((1, row // 2),)
            else:
                targets = ((0, (row - 1) // 2), (2, (row + 1) // 2))
            for kh, place in targets:
                if begin <= place < begin + count:
                    tap = kh * 3 + kw
                    cots[place - begin, :, tap * LAST : (tap + 1) * LAST] = sums[n]

    pair_sums(rows, pair, put)


def shifted_act(act, at, values):
    left, right = column_shifts(values)
    for kw, shifted in enumerate((left, values, right)):
        act[(kw, *at)] = shifted.astype(BF)


def first_conv(windows, w1_ref):
    total = None
    for step in range(9):
        window = jnp.concatenate([windows(kw, step // 3, step % 3) for kw in range(3)], 1)
        term = dot(window, w1_ref[step * 3 : step * 3 + 3].reshape(768, LAST))
        total = term if total is None else total + term
    return total


def second_conv_back(cots, w2_ref, slope, put):
    flat = jnp.concatenate(
        [
            jnp.concatenate([w2_ref[kt * 9 + tap] for tap in range(9)], 1)
            for kt in range(3)
        ],
        0,
    )
    spread = dot(cots, flat, NT)
    cells = spread.shape[0] // 2
    for frame in range(4):
        total = None
        for kt in range(3):
            if 0 <= frame - kt < 2:
                term = spread[
                    (frame - kt) * cells : (frame - kt + 1) * cells, kt * LAST : (kt + 1) * LAST
                ]
                total = term if total is None else total + term
        put(frame, (total * slope[frame]).astype(BF))


def inner_kernel(
    scales, tile_ref, w1_any, w2_any, first_ref, second_ref, act_ref, w1_ref, w2_ref,
    act, pair, cots, sems,
):
    load_w1 = pltpu.make_async_copy(w1_any, w1_ref, sems.at[0])
    load_w2 = pltpu.make_async_copy(w2_any, w2_ref, sems.at[1])
    load_w1.start()
    load_w2.start()
    keep = twice(scale_of(scales, KEEP))
    low = low_mask(scales, COLS)
    for frame in range(6):
        values = eff_frame(lambda f: tile_rows(tile_ref, f), frame, keep)
        values = values * sigmoid(values) * twice(low)
        shifted_act(act, (frame,), values)
        act_ref[frame] = values.astype(BF)
    load_w1.wait()
    first_out = first_conv(
        lambda kw, kt, kh: act[kw, kt : kt + 4, kh : kh + 6].reshape(384, 256), w1_ref
    ).reshape(24, 16, LAST)
    gate = sigmoid(first_out)
    second_ref[...] = (first_out * gate * low).astype(BF).reshape(4, 6, 16, LAST)
    slope = gate * (1.0 + first_out * (1.0 - gate)) * low
    high = high_mask(scales, COLS)
    for frame in range(2):
        at = TILE_COT + frame * 32
        rows = tile_ref[at + 2 : at + 30].reshape(14, 32, LAST).astype(F32) * high
        tap_sums(rows, 1, 1, 6, pair, cots.at[frame])
    load_w2.wait()

    def put(frame, first_grad):
        first_ref[frame] = first_grad.reshape(6, 16, LAST)

    second_conv_back(cots[...].reshape(192, 1152), w2_ref, slope.reshape(4, 96, LAST), put)


def edge_kernel(
    rim_ref, scales, tile_ref, sib_ref, first_ref, second_ref, w1_ref, w2_ref, packet_ref,
    act, rows, pair, cots,
):
    odd = lax.axis_index("core")
    even = 1 - odd
    keep = twice(scale_of(scales, KEEP))
    low = low_mask(scales, COLS)
    wide_low = twice(low)
    rim_scale, sib_scale = scale_of(scales, RIM_SCALE), scale_of(scales, SIB_SCALE)
    for frame in range(6):
        for part, at, read, mask in (
            (odd, odd * 2, lambda f: joined(rim_ref[f * 4 : f * 4 + 4]), wide_low * twice(rim_scale)),
            (0, 2, lambda f: joined(tile_ref[f * 16 : f * 16 + 4]), wide_low),
            (1, 0, lambda f: joined(tile_ref[f * 16 + 12 : f * 16 + 16]), wide_low),
            (even, even * 2, lambda f: joined(sib_ref[pl.ds(f * 16 + odd * 12, 4)]), wide_low * twice(sib_scale)),
        ):
            values = eff_frame(lambda f, read=read: read(f).astype(F32), frame, keep)
            shifted_act(act, (frame, part, pl.ds(at, 2)), values * sigmoid(values) * mask)
    high = high_mask(scales, COLS)
    for frame in range(2):
        at = TILE_COT + frame * 32
        own = tile_ref[at : at + 32].reshape(16, 32, LAST)
        rows[frame, 0, 3:6] = own[0:3].astype(F32) * high
        rows[frame, 1, 0:3] = own[13:16].astype(F32) * high
        raw = rim_ref[RIM_COT + frame * 6 : RIM_COT + frame * 6 + 6].reshape(3, 32, LAST)
        rows[frame, odd, pl.ds(odd * 3, 3)] = raw.astype(F32) * (high * rim_scale)
        raw = sib_ref[pl.ds(at + odd * 26, 6)].reshape(3, 32, LAST)
        rows[frame, even, pl.ds(even * 3, 3)] = raw.astype(F32) * (high * sib_scale)
        far = rows[frame, odd, pl.ds(2 + odd, 1)].reshape(2, 16, LAST)
        packet_ref[PACK_ROW + frame * 2 : PACK_ROW + frame * 2 + 2] = far.astype(BF)
        tap_sums(rows[frame, 0], -3, -1, 2, pair, cots.at[frame, 0])
        tap_sums(rows[frame, 1], 13, 7, 2, pair, cots.at[frame, 1])
    first_out = first_conv(
        lambda kw, kt, kh: act[kw, kt : kt + 4, :, kh : kh + 2].reshape(256, 256), w1_ref
    ).reshape(16, 16, LAST)
    row = lax.broadcasted_iota(jnp.int32, (16, 1, 1), 0) % 4
    row_scale = jnp.where(
        row == 0, scale_of(scales, UP), jnp.where(row == 3, scale_of(scales, DOWN), 1.0)
    )
    gate = sigmoid(first_out)
    second_in = (first_out * gate * low).astype(BF)
    slope = gate * (1.0 + first_out * (1.0 - gate)) * (low * row_scale)
    for frame in range(4):
        at = PACK_SECOND + frame * 8
        packet_ref[at] = second_in[frame * 4 + 1]
        packet_ref[at + 1 : at + 7] = second_ref[frame]
        packet_ref[at + 7] = second_in[frame * 4 + 2]

    def put(frame, first_grad):
        blocks_now = first_grad.reshape(4, 16, LAST)
        packet_ref[frame * 10 : frame * 10 + 2] = blocks_now[0:2]
        packet_ref[frame * 10 + 2 : frame * 10 + 8] = first_ref[frame]
        packet_ref[frame * 10 + 8 : frame * 10 + 10] = blocks_now[2:4]

    second_conv_back(cots[...].reshape(128, 1152), w2_ref, slope.reshape(4, 64, LAST), put)


def sibling_kernel(scales, tile_ref, sib_ref, act_ref, sums_ref, token_ref, rows, pair):
    token_ref[...] = scales[...]
    keep = twice(scale_of(scales, SIB_KEEP))
    low = twice(low_mask(scales, SIB_COLS))
    for frame in range(6):
        values = eff_frame(lambda f: tile_rows(sib_ref, f), frame, keep)
        act_ref[frame] = (values * sigmoid(values) * low).astype(BF)
    odd = lax.axis_index("core")
    link = scale_of(scales, SIB_SCALE)
    rows[...] = jnp.zeros((18, 32, LAST), F32)
    for slot, tile, other, which in (
        (0, tile_ref, sib_ref, COLS),
        (1, sib_ref, tile_ref, SIB_COLS),
    ):
        lower = odd if slot == 0 else 1 - odd
        high = high_mask(scales, which)
        for frame in range(2):
            at = TILE_COT + frame * 32
            rows[1:17] = tile[at : at + 32].reshape(16, 32, LAST).astype(F32) * high
            near = other[pl.ds(at + lower * 30, 2)].reshape(1, 32, LAST)
            rows[pl.ds(17 - lower * 17, 1)] = near.astype(F32) * (high * link)

            def put(kw, values):
                for n in range(17):
                    place = n // 2 if n % 2 == 0 else 9 + n // 2
                    sums_ref[kw, slot, frame, place] = values[n]

            pair_sums(rows[...], pair, put)


def input_kernel(scales, in_any, packet_ref, w1_any, grad_ref, in_ref, w1_ref, firsts, sems):
    load_in = pltpu.make_async_copy(in_any, in_ref, sems.at[0])
    load_w1 = pltpu.make_async_copy(w1_any, w1_ref, sems.at[1])
    load_w1.start()
    load_in.start()
    for frame in range(4):
        first_grad = packet_ref[frame * 10 : frame * 10 + 10]
        before, after = column_shifts(first_grad.astype(F32))
        for kw, value in ((0, after.astype(BF)), (1, first_grad), (2, before.astype(BF))):
            for kh in range(3):
                tap = kh * 3 + kw
                firsts[frame, :, :, tap * LAST : (tap + 1) * LAST] = value[2 - kh : 10 - kh]
    load_w1.wait()
    load_in.wait()
    shifted = firsts[...].reshape(512, 1152)
    by_depth = [
        dot(shifted, jnp.concatenate([w1_ref[kt * 9 + tap] for tap in range(9)], 1), NT)
        for kt in range(3)
    ]
    keep = twice(scale_of(scales, KEEP))
    low = twice(low_mask(scales, COLS))
    carried = None
    for frame in range(6):
        total = None
        for kt in range(3):
            if 0 <= frame - kt < 4:
                term = by_depth[kt][(frame - kt) * 128 : (frame - kt + 1) * 128]
                total = term if total is None else total + term
        values = eff_frame(lambda f: in_ref[f].astype(F32), frame, keep)
        gate = sigmoid(values)
        pre = total.reshape(8, 16, 256) * (gate * (1.0 + values * (1.0 - gate)) * low)
        if frame < 4:
            carried = pre if carried is None else carried + pre
            grad_ref[frame] = (pre * keep).astype(BF)
        elif frame == 4:
            grad_ref[frame] = (pre + carried * (1.0 - keep)).astype(BF)
        else:
            grad_ref[frame] = pre.astype(BF)


def weight_kernel(
    packets_ref, scales, tile_ref, sib_ref, act_ref, sib_act_ref, sums_ref,
    part_ref, pair, sums, cols,
):
    odd = lax.axis_index("core")
    packet_ref, sib_packet_ref = packets_ref.at[odd], packets_ref.at[1 - odd]
    near_y, reps, near_z, per_quarter, depth = part_ref.shape[:5]
    sums[...] = sums_ref[...]
    for slot, tile, packet, which in (
        (0, tile_ref, packet_ref, COLS),
        (1, sib_ref, sib_packet_ref, SIB_COLS),
    ):
        lower = odd if slot == 0 else 1 - odd
        high = high_mask(scales, which)
        for frame in range(2):
            far = packet[PACK_ROW + frame * 2 : PACK_ROW + frame * 2 + 2].reshape(1, 32, LAST)
            last = tile[pl.ds(TILE_COT + frame * 32 + lower * 30, 2)].reshape(1, 32, LAST)
            rows = jnp.concatenate([far.astype(F32), last.astype(F32) * high], 0)

            def put(kw, values):
                sums[kw, slot, frame, pl.ds(lower * 8, 1)] = values

            pair_sums(rows, pair, put)
        for frame in range(4):
            first_grad = packet[frame * 10 : frame * 10 + 10]
            before, after = column_shifts(first_grad.astype(F32))
            cols[0, slot, frame] = after.astype(BF)
            cols[1, slot, frame] = first_grad
            cols[2, slot, frame] = before.astype(BF)

    def both(refs, kt, frames):
        return jnp.concatenate(
            [ref[kt : kt + frames].reshape(frames * 128, ref.shape[3]) for ref in refs], 0
        )

    act_all = jnp.concatenate([both((act_ref, sib_act_ref), kt, 4) for kt in range(3)], 1)
    seconds = [
        ref[PACK_SECOND:PACK_ROW].reshape(4, 8, 16, LAST) for ref in (packet_ref, sib_packet_ref)
    ]
    second_all = jnp.concatenate([both(seconds, kt, 2) for kt in range(3)], 1)

    def put_block(block, at):
        halves = block.astype(BF).reshape(reps, 2, depth, LAST)
        for half in range(2):
            quarter, place = divmod(at * 2 + half, per_quarter)
            part_ref[quarter // near_z, :, quarter % near_z, place] = halves[:, half]

    def first_taps(step, at):
        tap = 5 * odd + step
        window = cols[tap % 3, :, :, pl.ds(2 - tap // 3, 8)].reshape(1024, LAST)
        block = dot(window, act_all, TN)
        for n in range(6):
            put_block(block[:, n * LAST : (n + 1) * LAST], at + n)

    def second_taps(step, at):
        tap = 4 * odd + step
        kh = tap // 3
        begin = jnp.where(kh == 0, 1, jnp.where(kh == 1, 9, 0))
        window = sums[tap % 3, :, :, pl.ds(begin, 8)].reshape(512, LAST)
        block = dot(window, second_all, TN)
        for n in range(3):
            put_block(block[:, n * LAST : (n + 1) * LAST], at + n)

    for step in range(4):
        first_taps(step, step * 6)
        second_taps(step, SECOND_AT + step * 3)

    @pl.when(odd == 0)
    def _():
        first_taps(4, EXTRA_AT)

    @pl.when(odd == 1)
    def _():
        second_taps(4, EXTRA_AT)
        for at in range(EXTRA_AT + 3, EXTRA_AT + 6):
            put_block(jnp.zeros((LAST, LAST), F32), at)


def near_sum_kernel(parts_ref, sum_ref):
    rows = parts_ref.shape[1]
    total = parts_ref[0].astype(F32)
    for n in range(1, parts_ref.shape[0]):
        total = total + parts_ref[n].astype(F32)
    sum_ref[0:rows] = total.astype(BF)
    if sum_ref.shape[0] > rows:
        sum_ref[rows:] = jnp.zeros((sum_ref.shape[0] - rows, LAST), BF)


def far_sum_kernel(parts_ref, scales, copies_ref, token_ref):
    token_ref[...] = scales[...]
    total = parts_ref[0].astype(F32)
    for n in range(1, parts_ref.shape[0]):
        total = total + parts_ref[n].astype(F32)
    copies_ref[...] = jnp.broadcast_to(total.astype(BF)[None], copies_ref.shape)


def finish_kernel(scale, per_quarter, whole_ref, _, first_ref, second_ref):
    depth = first_ref.shape[1] // 2
    for core in range(2):

        def put(target, tap, columns, at):
            for half in range(2):
                quarter, place = divmod(at * 2 + half, per_quarter)
                rows = whole_ref[core, quarter, place * depth : (place + 1) * depth]
                target[tap, half * depth : (half + 1) * depth, columns] = rows.astype(F32) * scale

        for step in range(5 - core):
            for kt in range(3):
                for half in range(2):
                    at = (step * 6 if step < 4 else EXTRA_AT) + kt * 2 + half
                    columns = slice(half * LAST, (half + 1) * LAST)
                    put(first_ref, kt * 9 + 5 * core + step, columns, at)
        for step in range(4 + core):
            for kt in range(3):
                at = (SECOND_AT + step * 3 if step < 4 else EXTRA_AT) + kt
                put(second_ref, kt * 9 + 4 * core + step, slice(0, LAST), at)


VMEM = pl.BlockSpec(memory_space=pltpu.VMEM)
HBM = pl.BlockSpec(memory_space=pltpu.HBM)
ANY = pl.BlockSpec(memory_space=pl.ANY)


def params(mebibytes):
    return pltpu.CompilerParams(vmem_limit_bytes=mebibytes << 20)


def cost(flops, moved):
    return pl.CostEstimate(flops=flops, bytes_accessed=moved, transcendentals=0)


def wide_sum(parts):
    return jnp.sum(parts.astype(F32), axis=0).astype(BF)


def blocks(count):
    return jax.ShapeDtypeStruct((count, 16, LAST), BF)


def body(inputs, cotangent, first_weight, second_weight, tile_clip, clip_cols, clip_start):
    tiles = lax.axis_size(TILE_AXES)
    reps, near_y, near_z = (lax.axis_size(name) for name in ("x", "yl", "zl"))
    far, plane = lax.axis_size(FAR_AXES), lax.axis_size(PLANE_AXES)
    local_in, local_cot, tile_clip, clip_cols, clip_start, w1, w2 = (
        pltpu.with_memory_space_constraint(array, pltpu.HBM)
        for array in (
            inputs[0],
            cotangent[0],
            tile_clip,
            clip_cols,
            clip_start,
            first_weight.reshape(27, 256, LAST),
            second_weight.reshape(27, LAST, LAST),
        )
    )
    swap = [(0, 1), (1, 0)]
    across = [(i, (i + 1) % tiles) for i in range(1, tiles, 2)]
    across += [(b, a) for a, b in across]
    own_rim, tile, scales = pl.pallas_call(
        pack_kernel,
        out_shape=(blocks(RIM_BLOCKS), blocks(TILE_BLOCKS), jax.ShapeDtypeStruct((8, LAST), F32)),
        in_specs=[HBM] * 5,
        out_specs=(VMEM, VMEM, VMEM),
        scratch_shapes=[
            pltpu.SMEM(tile_clip.shape, jnp.int32),
            pltpu.SMEM(clip_cols.shape, jnp.int32),
            pltpu.SMEM(clip_start.shape, jnp.int32),
            pltpu.VMEM(local_in.shape, BF),
            pltpu.VMEM(local_cot.shape, BF),
            pltpu.SemaphoreType.DMA((5,)),
        ],
        compiler_params=params(8),
        cost_estimate=cost(10**6, 2 * 10**6),
    )(tile_clip, clip_cols, clip_start, local_in, local_cot)
    rim = lax.ppermute(own_rim, TILE_AXES, across)
    sibling = lax.ppermute(tile, "core", swap)

    inner_first, inner_second, act, inner_w1, inner_w2 = pl.pallas_call(
        inner_kernel,
        out_shape=(
            jax.ShapeDtypeStruct((4, 6, 16, LAST), BF),
            jax.ShapeDtypeStruct((4, 6, 16, LAST), BF),
            jax.ShapeDtypeStruct((6, 8, 16, 256), BF),
            jax.ShapeDtypeStruct(w1.shape, BF),
            jax.ShapeDtypeStruct(w2.shape, BF),
        ),
        in_specs=[VMEM] * 2 + [HBM] * 2,
        out_specs=(VMEM,) * 5,
        scratch_shapes=[
            pltpu.VMEM((3, 6, 8, 16, 256), BF),
            pltpu.VMEM((13, 48, LAST), F32),
            pltpu.VMEM((2, 6, 16, 9 * LAST), BF),
            pltpu.SemaphoreType.DMA((2,)),
        ],
        compiler_params=params(24),
        cost_estimate=cost(2 * 10**9, 4 * 10**6),
    )(scales, tile, w1, w2)

    sib_act, sums, scales = pl.pallas_call(
        sibling_kernel,
        out_shape=(
            jax.ShapeDtypeStruct((6, 8, 16, 256), BF),
            jax.ShapeDtypeStruct((3, 2, 2, 17, 16, LAST), BF),
            jax.ShapeDtypeStruct(scales.shape, F32),
        ),
        in_specs=[VMEM] * 3,
        out_specs=(VMEM, VMEM, VMEM),
        scratch_shapes=[
            pltpu.VMEM((18, 32, LAST), F32),
            pltpu.VMEM((17, 48, LAST), F32),
        ],
        compiler_params=params(16),
        cost_estimate=cost(10**9, 2 * 10**6),
    )(scales, tile, sibling)

    packet = pl.pallas_call(
        edge_kernel,
        out_shape=blocks(PACK_BLOCKS),
        in_specs=[VMEM] * 8,
        out_specs=VMEM,
        scratch_shapes=[
            pltpu.VMEM((3, 6, 2, 4, 16, 256), BF),
            pltpu.VMEM((2, 2, 6, 32, LAST), F32),
            pltpu.VMEM((5, 48, LAST), F32),
            pltpu.VMEM((2, 2, 2, 16, 9 * LAST), BF),
        ],
        compiler_params=params(16),
        cost_estimate=cost(10**9, 4 * 10**6),
    )(rim, scales, tile, sibling, inner_first, inner_second, inner_w1, inner_w2)
    packets = lax.all_gather(packet, "core", axis=0)

    depth = LAST // reps
    quarters = near_y * near_z
    per_quarter = 2 * GRAD_BLOCKS // quarters
    parts = pl.pallas_call(
        weight_kernel,
        out_shape=jax.ShapeDtypeStruct(
            (near_y, reps, near_z, per_quarter, depth // 2, LAST), BF
        ),
        in_specs=[VMEM] * 7,
        out_specs=VMEM,
        scratch_shapes=[
            pltpu.VMEM((1, 48, LAST), F32),
            pltpu.VMEM((3, 2, 2, 17, 16, LAST), BF),
            pltpu.VMEM((3, 2, 4, 10, 16, LAST), BF),
        ],
        compiler_params=params(24),
        cost_estimate=cost(2 * 10**9, 4 * 10**6),
    )(packets, scales, tile, sibling, act, sib_act, sums)

    count = per_quarter * depth // 2
    share = -(-count // far // 8) * 8
    parts = parts.reshape(near_y * reps * near_z, count, LAST)
    near = pl.pallas_call(
        near_sum_kernel,
        out_shape=jax.ShapeDtypeStruct((far * share, LAST), BF),
        in_specs=[VMEM],
        out_specs=VMEM,
        compiler_params=params(8),
        cost_estimate=cost(10**6, 2 * 10**6),
    )(lax.all_to_all(parts, NEAR_AXES, 0, 0, tiled=True))
    near = near.reshape(far, share, LAST)
    copies, token = pl.pallas_call(
        far_sum_kernel,
        out_shape=(
            jax.ShapeDtypeStruct((plane, share, LAST), BF),
            jax.ShapeDtypeStruct(scales.shape, F32),
        ),
        in_specs=[VMEM, VMEM],
        out_specs=(VMEM, VMEM),
        compiler_params=params(8),
        cost_estimate=cost(10**5, 5 * 10**5),
    )(lax.all_to_all(near, FAR_AXES, 0, 0, tiled=True), scales)
    input_grad = pl.pallas_call(
        input_kernel,
        out_shape=jax.ShapeDtypeStruct(local_in.shape, BF),
        in_specs=[VMEM, HBM, VMEM, HBM],
        out_specs=VMEM,
        scratch_shapes=[
            pltpu.VMEM(local_in.shape, BF),
            pltpu.VMEM(w1.shape, BF),
            pltpu.VMEM((4, 8, 16, 9 * LAST), BF),
            pltpu.SemaphoreType.DMA((2,)),
        ],
        compiler_params=params(24),
        cost_estimate=cost(2 * 10**9, 4 * 10**6),
    )(token, local_in, packet, w1)

    half = lax.all_to_all(copies, PLANE_AXES, 0, 0, tiled=True)
    whole = lax.all_gather(half.reshape(quarters, far * share, LAST), "core", axis=0)

    cell_total = tiles * reps * cotangent.shape[1] * cotangent.shape[2] * cotangent.shape[3]
    scale = 1.0 / math.sqrt(cell_total)
    first, second = pl.pallas_call(
        lambda *refs: finish_kernel(scale, per_quarter, *refs),
        out_shape=(
            jax.ShapeDtypeStruct((27, depth, 256), F32),
            jax.ShapeDtypeStruct((27, depth, LAST), F32),
        ),
        in_specs=[VMEM, ANY],
        out_specs=(VMEM, VMEM),
        compiler_params=params(16),
    )(whole, pltpu.with_memory_space_constraint(input_grad, pltpu.HBM))
    first = jnp.swapaxes(first, 1, 2).reshape(3, 3, 3, 256, depth)
    second = jnp.swapaxes(second, 1, 2).reshape(3, 3, 3, LAST, depth)
    return input_grad[None], first, second


def solution(mesh):
    devices = mesh.devices
    tiles, reps = devices.shape
    height = math.isqrt(tiles // 2)
    width = tiles // 2 // height
    near_y, near_z = math.gcd(height, 2), math.gcd(width, 2)
    wide_mesh = Mesh(
        devices.reshape(height // near_y, near_y, width // near_z, near_z, 2, reps),
        (*TILE_AXES, "x"),
    )
    in_specs = (
        P("x", None, TILE_AXES, None, None),
        P("x", None, TILE_AXES, None, None),
        P(),
        P(),
        P("x", None),
        P("x", None),
        P("x", None),
    )
    out_specs = (
        P("x", None, TILE_AXES, None, None),
        P(None, None, None, None, "x"),
        P(None, None, None, None, "x"),
    )
    return jax.shard_map(
        body, mesh=wide_mesh, in_specs=in_specs, out_specs=out_specs, check_vma=False
    )
```

```python
import math

import jax
import jax.numpy as jnp
import numpy as np
from jax import lax
from jax.experimental import pallas as pl
from jax.experimental.pallas import tpu as pltpu
from jax.sharding import Mesh
from jax.sharding import PartitionSpec as P

TILE_AXES = ("yh", "yl", "zh", "zl", "core")
ALL_AXES = (*TILE_AXES, "x")
PLANE_AXES = ("yl", "zl", "zh", "yh")
BF = jnp.bfloat16
F32 = jnp.float32
NT = (((1,), (1,)), ((), ()))
TN = (((0,), (0,)), ((), ()))
LAST = 128
TILE_COT = 96
TILE_BLOCKS = 160
RIM_COT = 24
RIM_BLOCKS = 36
PACK_SECOND = 40
PACK_ROW = 72
PACK_BLOCKS = 76
UP, DOWN, COLS, KEEP, SIB_COLS, SIB_KEEP, RIM_SCALE, SIB_SCALE = range(8)
SECOND_AT = 24
EXTRA_AT = 36
GRAD_BLOCKS = 42


def dot(lhs, rhs, dims=(((1,), (0,)), ((), ()))):
    return lax.dot_general(lhs, rhs, dims, preferred_element_type=F32)


def sigmoid(values):
    return 1.0 / (1.0 + jnp.exp(-values))


def column_shifts(values):
    column = lax.broadcasted_iota(jnp.int32, (1, 16, values.shape[2]), 1)
    left = jnp.where(column == 0, 0.0, pltpu.roll(values, 1, 1))
    right = jnp.where(column == 15, 0.0, pltpu.roll(values, 15, 1))
    return left, right


def scale_of(scales, which):
    return scales[which : which + 1].reshape(1, 1, LAST)


def low_mask(scales, which):
    column = lax.broadcasted_iota(jnp.int32, (1, 16, LAST), 1).astype(F32)
    return jnp.where(column < scale_of(scales, which), 1.0, 0.0)


def high_mask(scales, which):
    column = lax.broadcasted_iota(jnp.int32, (1, 32, LAST), 1).astype(F32)
    return jnp.where(column < 2.0 * scale_of(scales, which), 1.0, 0.0)


def twice(values):
    return jnp.concatenate([values, values], 2)


def joined(blocks):
    halves = blocks.reshape(blocks.shape[0] // 2, 2, 16, LAST)
    return jnp.concatenate([halves[:, 0], halves[:, 1]], 2)


def tile_rows(tile_ref, frame):
    return joined(tile_ref[frame * 16 : frame * 16 + 16]).astype(F32)


def eff_frame(read, frame, keep):
    values = read(frame)
    return jnp.where(keep > 0.5, values, read(4)) if frame < 4 else values


def load_scales(clip_ref, cols_ref, start_ref):
    tile = lax.axis_index(TILE_AXES)
    tiles = lax.axis_size(TILE_AXES)
    even = lax.axis_index("core") == 0
    own = clip_ref[0, tile]
    up_same = (tile > 0) & (clip_ref[0, jnp.maximum(tile - 1, 0)] == own)
    down_same = (tile + 1 < tiles) & (clip_ref[0, jnp.minimum(tile + 1, tiles - 1)] == own)
    sibling = clip_ref[0, jnp.where(even, tile + 1, tile - 1)]
    up = jnp.where(up_same, 1.0, 0.0)
    down = jnp.where(down_same, 1.0, 0.0)
    return (
        up,
        down,
        cols_ref[0, own].astype(F32),
        jnp.where(start_ref[0, own] == 0, 0.0, 1.0),
        cols_ref[0, sibling].astype(F32),
        jnp.where(start_ref[0, sibling] == 0, 0.0, 1.0),
        jnp.where(even, up, down),
        jnp.where(even, down, up),
    )


def pack_kernel(
    clip_any, cols_any, start_any, in_any, cot_any, rim_ref, tile_ref, scales_ref,
    clip_ref, cols_ref, start_ref, in_ref, cot_ref, sems,
):
    copies = [
        pltpu.make_async_copy(source, target, sems.at[n])
        for n, (source, target) in enumerate(
            (
                (clip_any, clip_ref),
                (cols_any, cols_ref),
                (start_any, start_ref),
                (in_any, in_ref),
                (cot_any, cot_ref),
            )
        )
    ]
    for copy in copies:
        copy.start()
    copies[3].wait()
    for frame in range(6):
        for row in range(8):
            for half in range(2):
                tile_ref[frame * 16 + row * 2 + half] = in_ref[
                    frame, row, :, half * LAST : (half + 1) * LAST
                ]
    copies[4].wait()
    for frame in range(2):
        for half in range(2):
            for row in range(16):
                tile_ref[TILE_COT + frame * 32 + row * 2 + half] = cot_ref[
                    frame, row, half * 16 : (half + 1) * 16, :
                ]
    odd = lax.axis_index("core")
    for frame in range(6):
        rim_ref[frame * 4 : frame * 4 + 4] = tile_ref[pl.ds(frame * 16 + odd * 12, 4)]
    for frame in range(2):
        at = RIM_COT + frame * 6
        rim_ref[at : at + 6] = tile_ref[pl.ds(TILE_COT + frame * 32 + odd * 26, 6)]
    for copy in copies[:3]:
        copy.wait()
    for row, value in enumerate(load_scales(clip_ref, cols_ref, start_ref)):
        scales_ref[row : row + 1] = jnp.full((1, LAST), value, F32)


def pair_sums(rows, pair, put):
    count = rows.shape[0] - 1
    zeros = jnp.zeros((count, 8, LAST), F32)
    pair[0:count, 0:8] = zeros
    pair[0:count, 40:48] = zeros
    pair[0:count, 8:40] = rows[0:count] + rows[1 : count + 1]
    before, even, odd, after = (pair[0:count, pl.ds(begin, 16, 2), :] for begin in (7, 8, 9, 10))
    for kw, value in ((0, odd + after), (1, even + odd), (2, before + even)):
        put(kw, value.astype(BF))


def tap_sums(rows, first, begin, count, pair, cots):
    def put(kw, sums):
        for n in range(sums.shape[0]):
            row = first + n
            if row % 2 == 0:
                targets = ((1, row // 2),)
            else:
                targets = ((0, (row - 1) // 2), (2, (row + 1) // 2))
            for kh, place in targets:
                if begin <= place < begin + count:
                    tap = kh * 3 + kw
                    cots[place - begin, :, tap * LAST : (tap + 1) * LAST] = sums[n]

    pair_sums(rows, pair, put)


def shifted_act(act, at, values):
    left, right = column_shifts(values)
    for kw, shifted in enumerate((left, values, right)):
        act[(kw, *at)] = shifted.astype(BF)


def first_conv(windows, w1_ref):
    total = None
    for step in range(9):
        window = jnp.concatenate([windows(kw, step // 3, step % 3) for kw in range(3)], 1)
        term = dot(window, w1_ref[step * 3 : step * 3 + 3].reshape(768, LAST))
        total = term if total is None else total + term
    return total


def second_conv_back(cots, w2_ref, slope, put):
    flat = jnp.concatenate(
        [
            jnp.concatenate([w2_ref[kt * 9 + tap] for tap in range(9)], 1)
            for kt in range(3)
        ],
        0,
    )
    spread = dot(cots, flat, NT)
    cells = spread.shape[0] // 2
    for frame in range(4):
        total = None
        for kt in range(3):
            if 0 <= frame - kt < 2:
                term = spread[
                    (frame - kt) * cells : (frame - kt + 1) * cells, kt * LAST : (kt + 1) * LAST
                ]
                total = term if total is None else total + term
        put(frame, (total * slope[frame]).astype(BF))


def inner_kernel(
    scales, tile_ref, w1_any, w2_any, first_ref, second_ref, act_ref, w1_ref, w2_ref,
    act, pair, cots, sems,
):
    load_w1 = pltpu.make_async_copy(w1_any, w1_ref, sems.at[0])
    load_w2 = pltpu.make_async_copy(w2_any, w2_ref, sems.at[1])
    load_w1.start()
    load_w2.start()
    keep = twice(scale_of(scales, KEEP))
    low = low_mask(scales, COLS)
    for frame in range(6):
        values = eff_frame(lambda f: tile_rows(tile_ref, f), frame, keep)
        values = values * sigmoid(values) * twice(low)
        shifted_act(act, (frame,), values)
        act_ref[frame] = values.astype(BF)
    load_w1.wait()
    first_out = first_conv(
        lambda kw, kt, kh: act[kw, kt : kt + 4, kh : kh + 6].reshape(384, 256), w1_ref
    ).reshape(24, 16, LAST)
    gate = sigmoid(first_out)
    second_ref[...] = (first_out * gate * low).astype(BF).reshape(4, 6, 16, LAST)
    slope = gate * (1.0 + first_out * (1.0 - gate)) * low
    high = high_mask(scales, COLS)
    for frame in range(2):
        at = TILE_COT + frame * 32
        rows = tile_ref[at + 2 : at + 30].reshape(14, 32, LAST).astype(F32) * high
        tap_sums(rows, 1, 1, 6, pair, cots.at[frame])
    load_w2.wait()

    def put(frame, first_grad):
        first_ref[frame] = first_grad.reshape(6, 16, LAST)

    second_conv_back(cots[...].reshape(192, 1152), w2_ref, slope.reshape(4, 96, LAST), put)


def edge_kernel(
    rim_ref, scales, tile_ref, sib_ref, first_ref, second_ref, w1_ref, w2_ref, packet_ref,
    act, rows, pair, cots,
):
    odd = lax.axis_index("core")
    even = 1 - odd
    keep = twice(scale_of(scales, KEEP))
    low = low_mask(scales, COLS)
    wide_low = twice(low)
    rim_scale, sib_scale = scale_of(scales, RIM_SCALE), scale_of(scales, SIB_SCALE)
    for frame in range(6):
        for part, at, read, mask in (
            (odd, odd * 2, lambda f: joined(rim_ref[f * 4 : f * 4 + 4]), wide_low * twice(rim_scale)),
            (0, 2, lambda f: joined(tile_ref[f * 16 : f * 16 + 4]), wide_low),
            (1, 0, lambda f: joined(tile_ref[f * 16 + 12 : f * 16 + 16]), wide_low),
            (even, even * 2, lambda f: joined(sib_ref[pl.ds(f * 16 + odd * 12, 4)]), wide_low * twice(sib_scale)),
        ):
            values = eff_frame(lambda f, read=read: read(f).astype(F32), frame, keep)
            shifted_act(act, (frame, part, pl.ds(at, 2)), values * sigmoid(values) * mask)
    high = high_mask(scales, COLS)
    for frame in range(2):
        at = TILE_COT + frame * 32
        own = tile_ref[at : at + 32].reshape(16, 32, LAST)
        rows[frame, 0, 3:6] = own[0:3].astype(F32) * high
        rows[frame, 1, 0:3] = own[13:16].astype(F32) * high
        raw = rim_ref[RIM_COT + frame * 6 : RIM_COT + frame * 6 + 6].reshape(3, 32, LAST)
        rows[frame, odd, pl.ds(odd * 3, 3)] = raw.astype(F32) * (high * rim_scale)
        raw = sib_ref[pl.ds(at + odd * 26, 6)].reshape(3, 32, LAST)
        rows[frame, even, pl.ds(even * 3, 3)] = raw.astype(F32) * (high * sib_scale)
        far = rows[frame, odd, pl.ds(2 + odd, 1)].reshape(2, 16, LAST)
        packet_ref[PACK_ROW + frame * 2 : PACK_ROW + frame * 2 + 2] = far.astype(BF)
        tap_sums(rows[frame, 0], -3, -1, 2, pair, cots.at[frame, 0])
        tap_sums(rows[frame, 1], 13, 7, 2, pair, cots.at[frame, 1])
    first_out = first_conv(
        lambda kw, kt, kh: act[kw, kt : kt + 4, :, kh : kh + 2].reshape(256, 256), w1_ref
    ).reshape(16, 16, LAST)
    row = lax.broadcasted_iota(jnp.int32, (16, 1, 1), 0) % 4
    row_scale = jnp.where(
        row == 0, scale_of(scales, UP), jnp.where(row == 3, scale_of(scales, DOWN), 1.0)
    )
    gate = sigmoid(first_out)
    second_in = (first_out * gate * low).astype(BF)
    slope = gate * (1.0 + first_out * (1.0 - gate)) * (low * row_scale)
    for frame in range(4):
        at = PACK_SECOND + frame * 8
        packet_ref[at] = second_in[frame * 4 + 1]
        packet_ref[at + 1 : at + 7] = second_ref[frame]
        packet_ref[at + 7] = second_in[frame * 4 + 2]

    def put(frame, first_grad):
        blocks_now = first_grad.reshape(4, 16, LAST)
        packet_ref[frame * 10 : frame * 10 + 2] = blocks_now[0:2]
        packet_ref[frame * 10 + 2 : frame * 10 + 8] = first_ref[frame]
        packet_ref[frame * 10 + 8 : frame * 10 + 10] = blocks_now[2:4]

    second_conv_back(cots[...].reshape(128, 1152), w2_ref, slope.reshape(4, 64, LAST), put)


def sibling_kernel(scales, tile_ref, sib_ref, act_ref, sums_ref, token_ref, rows, pair):
    token_ref[...] = scales[...]
    keep = twice(scale_of(scales, SIB_KEEP))
    low = twice(low_mask(scales, SIB_COLS))
    for frame in range(6):
        values = eff_frame(lambda f: tile_rows(sib_ref, f), frame, keep)
        act_ref[frame] = (values * sigmoid(values) * low).astype(BF)
    odd = lax.axis_index("core")
    link = scale_of(scales, SIB_SCALE)
    rows[...] = jnp.zeros((18, 32, LAST), F32)
    for slot, tile, other, which in (
        (0, tile_ref, sib_ref, COLS),
        (1, sib_ref, tile_ref, SIB_COLS),
    ):
        lower = odd if slot == 0 else 1 - odd
        high = high_mask(scales, which)
        for frame in range(2):
            at = TILE_COT + frame * 32
            rows[1:17] = tile[at : at + 32].reshape(16, 32, LAST).astype(F32) * high
            near = other[pl.ds(at + lower * 30, 2)].reshape(1, 32, LAST)
            rows[pl.ds(17 - lower * 17, 1)] = near.astype(F32) * (high * link)

            def put(kw, values):
                for n in range(17):
                    place = n // 2 if n % 2 == 0 else 9 + n // 2
                    sums_ref[kw, slot, frame, place] = values[n]

            pair_sums(rows[...], pair, put)


def input_kernel(scales, in_any, packet_ref, w1_any, grad_ref, in_ref, w1_ref, firsts, sems):
    load_in = pltpu.make_async_copy(in_any, in_ref, sems.at[0])
    load_w1 = pltpu.make_async_copy(w1_any, w1_ref, sems.at[1])
    load_w1.start()
    load_in.start()
    for frame in range(4):
        first_grad = packet_ref[frame * 10 : frame * 10 + 10]
        before, after = column_shifts(first_grad.astype(F32))
        for kw, value in ((0, after.astype(BF)), (1, first_grad), (2, before.astype(BF))):
            for kh in range(3):
                tap = kh * 3 + kw
                firsts[frame, :, :, tap * LAST : (tap + 1) * LAST] = value[2 - kh : 10 - kh]
    load_w1.wait()
    load_in.wait()
    shifted = firsts[...].reshape(512, 1152)
    by_depth = [
        dot(shifted, jnp.concatenate([w1_ref[kt * 9 + tap] for tap in range(9)], 1), NT)
        for kt in range(3)
    ]
    keep = twice(scale_of(scales, KEEP))
    low = twice(low_mask(scales, COLS))
    carried = None
    for frame in range(6):
        total = None
        for kt in range(3):
            if 0 <= frame - kt < 4:
                term = by_depth[kt][(frame - kt) * 128 : (frame - kt + 1) * 128]
                total = term if total is None else total + term
        values = eff_frame(lambda f: in_ref[f].astype(F32), frame, keep)
        gate = sigmoid(values)
        pre = total.reshape(8, 16, 256) * (gate * (1.0 + values * (1.0 - gate)) * low)
        if frame < 4:
            carried = pre if carried is None else carried + pre
            grad_ref[frame] = (pre * keep).astype(BF)
        elif frame == 4:
            grad_ref[frame] = (pre + carried * (1.0 - keep)).astype(BF)
        else:
            grad_ref[frame] = pre.astype(BF)


def weight_kernel(
    packets_ref, scales, tile_ref, sib_ref, act_ref, sib_act_ref, sums_ref,
    part_ref, pair, sums, cols,
):
    odd = lax.axis_index("core")
    packet_ref, sib_packet_ref = packets_ref.at[odd], packets_ref.at[1 - odd]
    reps, quarters, per_quarter, depth = part_ref.shape[:4]
    sums[...] = sums_ref[...]
    for slot, tile, packet, which in (
        (0, tile_ref, packet_ref, COLS),
        (1, sib_ref, sib_packet_ref, SIB_COLS),
    ):
        lower = odd if slot == 0 else 1 - odd
        high = high_mask(scales, which)
        for frame in range(2):
            far = packet[PACK_ROW + frame * 2 : PACK_ROW + frame * 2 + 2].reshape(1, 32, LAST)
            last = tile[pl.ds(TILE_COT + frame * 32 + lower * 30, 2)].reshape(1, 32, LAST)
            rows = jnp.concatenate([far.astype(F32), last.astype(F32) * high], 0)

            def put(kw, values):
                sums[kw, slot, frame, pl.ds(lower * 8, 1)] = values

            pair_sums(rows, pair, put)
        for frame in range(4):
            first_grad = packet[frame * 10 : frame * 10 + 10]
            before, after = column_shifts(first_grad.astype(F32))
            cols[0, slot, frame] = after.astype(BF)
            cols[1, slot, frame] = first_grad
            cols[2, slot, frame] = before.astype(BF)

    def both(refs, kt, frames):
        return jnp.concatenate(
            [ref[kt : kt + frames].reshape(frames * 128, ref.shape[3]) for ref in refs], 0
        )

    act_all = jnp.concatenate([both((act_ref, sib_act_ref), kt, 4) for kt in range(3)], 1)
    seconds = [
        ref[PACK_SECOND:PACK_ROW].reshape(4, 8, 16, LAST) for ref in (packet_ref, sib_packet_ref)
    ]
    second_all = jnp.concatenate([both(seconds, kt, 2) for kt in range(3)], 1)

    def put_block(block, at):
        halves = block.astype(BF).reshape(reps, 2, depth, LAST)
        for half in range(2):
            quarter, place = divmod(at * 2 + half, per_quarter)
            for rep in range(reps):
                first = rep + (quarter - rep) * odd
                part_ref[first, rep + quarter - first, place] = halves[rep, half]

    def first_taps(step, at):
        tap = 5 * odd + step
        window = cols[tap % 3, :, :, pl.ds(2 - tap // 3, 8)].reshape(1024, LAST)
        block = dot(window, act_all, TN)
        for n in range(6):
            put_block(block[:, n * LAST : (n + 1) * LAST], at + n)

    def second_taps(step, at):
        tap = 4 * odd + step
        kh = tap // 3
        begin = jnp.where(kh == 0, 1, jnp.where(kh == 1, 9, 0))
        window = sums[tap % 3, :, :, pl.ds(begin, 8)].reshape(512, LAST)
        block = dot(window, second_all, TN)
        for n in range(3):
            put_block(block[:, n * LAST : (n + 1) * LAST], at + n)

    for step in range(4):
        first_taps(step, step * 6)
        second_taps(step, SECOND_AT + step * 3)

    @pl.when(odd == 0)
    def _():
        first_taps(4, EXTRA_AT)

    @pl.when(odd == 1)
    def _():
        second_taps(4, EXTRA_AT)
        for at in range(EXTRA_AT + 3, EXTRA_AT + 6):
            put_block(jnp.zeros((LAST, LAST), F32), at)


def near_sum_kernel(parts_ref, sum_ref):
    shares, others, share, _ = sum_ref.shape
    rows = parts_ref.shape[2]
    for other in range(others):
        total = parts_ref[0, other].astype(F32)
        for n in range(1, parts_ref.shape[0]):
            total = total + parts_ref[n, other].astype(F32)
        if shares * share > rows:
            padding = jnp.zeros((shares * share - rows, LAST), F32)
            total = jnp.concatenate([total, padding], 0)
        sum_ref[:, other] = total.reshape(shares, share, LAST).astype(BF)


def far_sum_kernel(parts_ref, scales, copies_ref, token_ref):
    token_ref[...] = scales[...]
    total = parts_ref[0].astype(F32)
    for n in range(1, parts_ref.shape[0]):
        total = total + parts_ref[n].astype(F32)
    copies_ref[...] = jnp.broadcast_to(total.astype(BF)[None], copies_ref.shape)


def sum_groups(sizes):
    numbers = np.arange(math.prod(sizes)).reshape(sizes)
    even, odd = numbers[..., 0, :], numbers[..., 1, :]
    reps, quarters = sizes[5], sizes[1] * sizes[3]
    near = (
        even.reshape(-1, reps),
        odd.transpose(0, 2, 4, 1, 3).reshape(-1, quarters),
    )
    far = (
        even.transpose(4, 2, 0, 1, 3).reshape(reps, -1),
        odd.transpose(1, 3, 2, 0, 4).reshape(quarters, -1),
    )
    return [[row.tolist() for part in parts for row in part] for parts in (near, far)]


def finish_kernel(scale, per_quarter, whole_ref, _, first_ref, second_ref):
    depth = first_ref.shape[1] // 2
    for core in range(2):

        def put(target, tap, columns, at):
            for half in range(2):
                quarter, place = divmod(at * 2 + half, per_quarter)
                rows = whole_ref[core, quarter, place * depth : (place + 1) * depth]
                target[tap, half * depth : (half + 1) * depth, columns] = rows.astype(F32) * scale

        for step in range(5 - core):
            for kt in range(3):
                for half in range(2):
                    at = (step * 6 if step < 4 else EXTRA_AT) + kt * 2 + half
                    columns = slice(half * LAST, (half + 1) * LAST)
                    put(first_ref, kt * 9 + 5 * core + step, columns, at)
        for step in range(4 + core):
            for kt in range(3):
                at = (SECOND_AT + step * 3 if step < 4 else EXTRA_AT) + kt
                put(second_ref, kt * 9 + 4 * core + step, slice(0, LAST), at)


VMEM = pl.BlockSpec(memory_space=pltpu.VMEM)
HBM = pl.BlockSpec(memory_space=pltpu.HBM)
ANY = pl.BlockSpec(memory_space=pl.ANY)


def params(mebibytes):
    return pltpu.CompilerParams(vmem_limit_bytes=mebibytes << 20)


def cost(flops, moved):
    return pl.CostEstimate(flops=flops, bytes_accessed=moved, transcendentals=0)


def wide_sum(parts):
    return jnp.sum(parts.astype(F32), axis=0).astype(BF)


def blocks(count):
    return jax.ShapeDtypeStruct((count, 16, LAST), BF)


def body(inputs, cotangent, first_weight, second_weight, tile_clip, clip_cols, clip_start):
    tiles = lax.axis_size(TILE_AXES)
    reps, near_y, near_z = (lax.axis_size(name) for name in ("x", "yl", "zl"))
    plane = lax.axis_size(PLANE_AXES)
    near_groups, far_groups = sum_groups(tuple(map(lax.axis_size, ALL_AXES)))
    local_in, local_cot, tile_clip, clip_cols, clip_start, w1, w2 = (
        pltpu.with_memory_space_constraint(array, pltpu.HBM)
        for array in (
            inputs[0],
            cotangent[0],
            tile_clip,
            clip_cols,
            clip_start,
            first_weight.reshape(27, 256, LAST),
            second_weight.reshape(27, LAST, LAST),
        )
    )
    swap = [(0, 1), (1, 0)]
    across = [(i, (i + 1) % tiles) for i in range(1, tiles, 2)]
    across += [(b, a) for a, b in across]
    own_rim, tile, scales = pl.pallas_call(
        pack_kernel,
        out_shape=(blocks(RIM_BLOCKS), blocks(TILE_BLOCKS), jax.ShapeDtypeStruct((8, LAST), F32)),
        in_specs=[HBM] * 5,
        out_specs=(VMEM, VMEM, VMEM),
        scratch_shapes=[
            pltpu.SMEM(tile_clip.shape, jnp.int32),
            pltpu.SMEM(clip_cols.shape, jnp.int32),
            pltpu.SMEM(clip_start.shape, jnp.int32),
            pltpu.VMEM(local_in.shape, BF),
            pltpu.VMEM(local_cot.shape, BF),
            pltpu.SemaphoreType.DMA((5,)),
        ],
        compiler_params=params(8),
        cost_estimate=cost(10**6, 2 * 10**6),
    )(tile_clip, clip_cols, clip_start, local_in, local_cot)
    rim = lax.ppermute(own_rim, TILE_AXES, across)
    sibling = lax.ppermute(tile, "core", swap)

    inner_first, inner_second, act, inner_w1, inner_w2 = pl.pallas_call(
        inner_kernel,
        out_shape=(
            jax.ShapeDtypeStruct((4, 6, 16, LAST), BF),
            jax.ShapeDtypeStruct((4, 6, 16, LAST), BF),
            jax.ShapeDtypeStruct((6, 8, 16, 256), BF),
            jax.ShapeDtypeStruct(w1.shape, BF),
            jax.ShapeDtypeStruct(w2.shape, BF),
        ),
        in_specs=[VMEM] * 2 + [HBM] * 2,
        out_specs=(VMEM,) * 5,
        scratch_shapes=[
            pltpu.VMEM((3, 6, 8, 16, 256), BF),
            pltpu.VMEM((13, 48, LAST), F32),
            pltpu.VMEM((2, 6, 16, 9 * LAST), BF),
            pltpu.SemaphoreType.DMA((2,)),
        ],
        compiler_params=params(24),
        cost_estimate=cost(2 * 10**9, 4 * 10**6),
    )(scales, tile, w1, w2)

    sib_act, sums, scales = pl.pallas_call(
        sibling_kernel,
        out_shape=(
            jax.ShapeDtypeStruct((6, 8, 16, 256), BF),
            jax.ShapeDtypeStruct((3, 2, 2, 17, 16, LAST), BF),
            jax.ShapeDtypeStruct(scales.shape, F32),
        ),
        in_specs=[VMEM] * 3,
        out_specs=(VMEM, VMEM, VMEM),
        scratch_shapes=[
            pltpu.VMEM((18, 32, LAST), F32),
            pltpu.VMEM((17, 48, LAST), F32),
        ],
        compiler_params=params(16),
        cost_estimate=cost(10**9, 2 * 10**6),
    )(scales, tile, sibling)

    packet = pl.pallas_call(
        edge_kernel,
        out_shape=blocks(PACK_BLOCKS),
        in_specs=[VMEM] * 8,
        out_specs=VMEM,
        scratch_shapes=[
            pltpu.VMEM((3, 6, 2, 4, 16, 256), BF),
            pltpu.VMEM((2, 2, 6, 32, LAST), F32),
            pltpu.VMEM((5, 48, LAST), F32),
            pltpu.VMEM((2, 2, 2, 16, 9 * LAST), BF),
        ],
        compiler_params=params(16),
        cost_estimate=cost(10**9, 4 * 10**6),
    )(rim, scales, tile, sibling, inner_first, inner_second, inner_w1, inner_w2)
    packets = lax.all_gather(packet, "core", axis=0)

    depth = LAST // reps
    quarters = near_y * near_z
    per_quarter = 2 * GRAD_BLOCKS // quarters
    parts = pl.pallas_call(
        weight_kernel,
        out_shape=jax.ShapeDtypeStruct(
            (reps, quarters, per_quarter, depth // 2, LAST), BF
        ),
        in_specs=[VMEM] * 7,
        out_specs=VMEM,
        scratch_shapes=[
            pltpu.VMEM((1, 48, LAST), F32),
            pltpu.VMEM((3, 2, 2, 17, 16, LAST), BF),
            pltpu.VMEM((3, 2, 4, 10, 16, LAST), BF),
        ],
        compiler_params=params(24),
        cost_estimate=cost(2 * 10**9, 4 * 10**6),
    )(packets, scales, tile, sibling, act, sib_act, sums)

    count = per_quarter * depth // 2
    share = -(-count * quarters // plane // 8) * 8
    parts = parts.reshape(reps, quarters, count, LAST)

    def exchange(values, groups):
        return lax.all_to_all(values, ALL_AXES, 0, 0, axis_index_groups=groups, tiled=True)

    near = pl.pallas_call(
        near_sum_kernel,
        out_shape=jax.ShapeDtypeStruct((plane // quarters, quarters, share, LAST), BF),
        in_specs=[VMEM],
        out_specs=VMEM,
        compiler_params=params(8),
        cost_estimate=cost(10**6, 2 * 10**6),
    )(exchange(parts, near_groups))
    near = near.reshape(plane, share, LAST)
    copies, token = pl.pallas_call(
        far_sum_kernel,
        out_shape=(
            jax.ShapeDtypeStruct((plane, share, LAST), BF),
            jax.ShapeDtypeStruct(scales.shape, F32),
        ),
        in_specs=[VMEM, VMEM],
        out_specs=(VMEM, VMEM),
        compiler_params=params(8),
        cost_estimate=cost(10**5, 5 * 10**5),
    )(exchange(near, far_groups), scales)
    input_grad = pl.pallas_call(
        input_kernel,
        out_shape=jax.ShapeDtypeStruct(local_in.shape, BF),
        in_specs=[VMEM, HBM, VMEM, HBM],
        out_specs=VMEM,
        scratch_shapes=[
            pltpu.VMEM(local_in.shape, BF),
            pltpu.VMEM(w1.shape, BF),
            pltpu.VMEM((4, 8, 16, 9 * LAST), BF),
            pltpu.SemaphoreType.DMA((2,)),
        ],
        compiler_params=params(24),
        cost_estimate=cost(2 * 10**9, 4 * 10**6),
    )(token, local_in, packet, w1)

    half = lax.all_to_all(copies, PLANE_AXES, 0, 0, tiled=True)
    whole = lax.all_gather(half.reshape(quarters, plane // quarters * share, LAST), "core", axis=0)

    cell_total = tiles * reps * cotangent.shape[1] * cotangent.shape[2] * cotangent.shape[3]
    scale = 1.0 / math.sqrt(cell_total)
    first, second = pl.pallas_call(
        lambda *refs: finish_kernel(scale, per_quarter, *refs),
        out_shape=(
            jax.ShapeDtypeStruct((27, depth, 256), F32),
            jax.ShapeDtypeStruct((27, depth, LAST), F32),
        ),
        in_specs=[VMEM, ANY],
        out_specs=(VMEM, VMEM),
        compiler_params=params(16),
    )(whole, pltpu.with_memory_space_constraint(input_grad, pltpu.HBM))
    first = jnp.swapaxes(first, 1, 2).reshape(3, 3, 3, 256, depth)
    second = jnp.swapaxes(second, 1, 2).reshape(3, 3, 3, LAST, depth)
    return input_grad[None], first, second


def solution(mesh):
    devices = mesh.devices
    tiles, reps = devices.shape
    height = math.isqrt(tiles // 2)
    width = tiles // 2 // height
    near_y, near_z = math.gcd(height, 2), math.gcd(width, 2)
    wide_mesh = Mesh(
        devices.reshape(height // near_y, near_y, width // near_z, near_z, 2, reps),
        (*TILE_AXES, "x"),
    )
    in_specs = (
        P("x", None, TILE_AXES, None, None),
        P("x", None, TILE_AXES, None, None),
        P(),
        P(),
        P("x", None),
        P("x", None),
        P("x", None),
    )
    out_specs = (
        P("x", None, TILE_AXES, None, None),
        P(None, None, None, None, "x"),
        P(None, None, None, None, "x"),
    )
    return jax.shard_map(
        body, mesh=wide_mesh, in_specs=in_specs, out_specs=out_specs, check_vma=False
    )
```

```python
import math

import jax
import jax.numpy as jnp
import numpy as np
from jax import lax
from jax.experimental import pallas as pl
from jax.experimental.pallas import tpu as pltpu
from jax.sharding import Mesh
from jax.sharding import PartitionSpec as P

TILE_AXES = ("yh", "yl", "zh", "zl", "core")
ALL_AXES = (*TILE_AXES, "x")
PLANE_AXES = ("yl", "zl", "zh", "yh")
BF = jnp.bfloat16
F32 = jnp.float32
NT = (((1,), (1,)), ((), ()))
TN = (((0,), (0,)), ((), ()))
LAST = 128
TILE_COT = 96
TILE_BLOCKS = 160
RIM_COT = 24
RIM_BLOCKS = 36
PACK_SECOND = 40
PACK_ROW = 72
PACK_BLOCKS = 76
UP, DOWN, COLS, KEEP, SIB_COLS, SIB_KEEP, RIM_SCALE, SIB_SCALE = range(8)
SECOND_AT = 24
EXTRA_AT = 36
GRAD_BLOCKS = 42


def dot(lhs, rhs, dims=(((1,), (0,)), ((), ()))):
    return lax.dot_general(lhs, rhs, dims, preferred_element_type=F32)


def sigmoid(values):
    return 1.0 / (1.0 + jnp.exp(-values))


def column_shifts(values):
    column = lax.broadcasted_iota(jnp.int32, (1, 16, values.shape[2]), 1)
    left = jnp.where(column == 0, 0.0, pltpu.roll(values, 1, 1))
    right = jnp.where(column == 15, 0.0, pltpu.roll(values, 15, 1))
    return left, right


def scale_of(scales, which):
    return scales[which : which + 1].reshape(1, 1, LAST)


def low_mask(scales, which):
    column = lax.broadcasted_iota(jnp.int32, (1, 16, LAST), 1).astype(F32)
    return jnp.where(column < scale_of(scales, which), 1.0, 0.0)


def high_mask(scales, which):
    column = lax.broadcasted_iota(jnp.int32, (1, 32, LAST), 1).astype(F32)
    return jnp.where(column < 2.0 * scale_of(scales, which), 1.0, 0.0)


def twice(values):
    return jnp.concatenate([values, values], 2)


def joined(blocks):
    halves = blocks.reshape(blocks.shape[0] // 2, 2, 16, LAST)
    return jnp.concatenate([halves[:, 0], halves[:, 1]], 2)


def tile_rows(tile_ref, frame):
    return joined(tile_ref[frame * 16 : frame * 16 + 16]).astype(F32)


def eff_frame(read, frame, keep):
    values = read(frame)
    return jnp.where(keep > 0.5, values, read(4)) if frame < 4 else values


def load_scales(clip_ref, cols_ref, start_ref):
    tile = lax.axis_index(TILE_AXES)
    tiles = lax.axis_size(TILE_AXES)
    even = lax.axis_index("core") == 0
    own = clip_ref[0, tile]
    up_same = (tile > 0) & (clip_ref[0, jnp.maximum(tile - 1, 0)] == own)
    down_same = (tile + 1 < tiles) & (clip_ref[0, jnp.minimum(tile + 1, tiles - 1)] == own)
    sibling = clip_ref[0, jnp.where(even, tile + 1, tile - 1)]
    up = jnp.where(up_same, 1.0, 0.0)
    down = jnp.where(down_same, 1.0, 0.0)
    return (
        up,
        down,
        cols_ref[0, own].astype(F32),
        jnp.where(start_ref[0, own] == 0, 0.0, 1.0),
        cols_ref[0, sibling].astype(F32),
        jnp.where(start_ref[0, sibling] == 0, 0.0, 1.0),
        jnp.where(even, up, down),
        jnp.where(even, down, up),
    )


def pack_kernel(
    clip_any, cols_any, start_any, in_any, cot_any, rim_ref, tile_ref, scales_ref,
    clip_ref, cols_ref, start_ref, in_ref, cot_ref, sems,
):
    copies = [
        pltpu.make_async_copy(source, target, sems.at[n])
        for n, (source, target) in enumerate(
            (
                (clip_any, clip_ref),
                (cols_any, cols_ref),
                (start_any, start_ref),
                (in_any, in_ref),
                (cot_any, cot_ref),
            )
        )
    ]
    for copy in copies:
        copy.start()
    copies[3].wait()
    for frame in range(6):
        for row in range(8):
            for half in range(2):
                tile_ref[frame * 16 + row * 2 + half] = in_ref[
                    frame, row, :, half * LAST : (half + 1) * LAST
                ]
    copies[4].wait()
    for frame in range(2):
        for half in range(2):
            for row in range(16):
                tile_ref[TILE_COT + frame * 32 + row * 2 + half] = cot_ref[
                    frame, row, half * 16 : (half + 1) * 16, :
                ]
    odd = lax.axis_index("core")
    for frame in range(6):
        rim_ref[frame * 4 : frame * 4 + 4] = tile_ref[pl.ds(frame * 16 + odd * 12, 4)]
    for frame in range(2):
        at = RIM_COT + frame * 6
        rim_ref[at : at + 6] = tile_ref[pl.ds(TILE_COT + frame * 32 + odd * 26, 6)]
    for copy in copies[:3]:
        copy.wait()
    for row, value in enumerate(load_scales(clip_ref, cols_ref, start_ref)):
        scales_ref[row : row + 1] = jnp.full((1, LAST), value, F32)


def pair_sums(rows, pair, put):
    count = rows.shape[0] - 1
    zeros = jnp.zeros((count, 8, LAST), F32)
    pair[0:count, 0:8] = zeros
    pair[0:count, 40:48] = zeros
    pair[0:count, 8:40] = rows[0:count] + rows[1 : count + 1]
    before, even, odd, after = (pair[0:count, pl.ds(begin, 16, 2), :] for begin in (7, 8, 9, 10))
    for kw, value in ((0, odd + after), (1, even + odd), (2, before + even)):
        put(kw, value.astype(BF))


def tap_sums(rows, first, begin, count, pair, cots):
    def put(kw, sums):
        for n in range(sums.shape[0]):
            row = first + n
            if row % 2 == 0:
                targets = ((1, row // 2),)
            else:
                targets = ((0, (row - 1) // 2), (2, (row + 1) // 2))
            for kh, place in targets:
                if begin <= place < begin + count:
                    tap = kh * 3 + kw
                    cots[place - begin, :, tap * LAST : (tap + 1) * LAST] = sums[n]

    pair_sums(rows, pair, put)


def shifted_act(act, at, values):
    left, right = column_shifts(values)
    for kw, shifted in enumerate((left, values, right)):
        act[(kw, *at)] = shifted.astype(BF)


def first_conv(windows, w1_ref):
    total = None
    for step in range(9):
        window = jnp.concatenate([windows(kw, step // 3, step % 3) for kw in range(3)], 1)
        term = dot(window, w1_ref[step * 3 : step * 3 + 3].reshape(768, LAST))
        total = term if total is None else total + term
    return total


def second_conv_back(cots, w2_ref, slope, put):
    flat = jnp.concatenate(
        [
            jnp.concatenate([w2_ref[kt * 9 + tap] for tap in range(9)], 1)
            for kt in range(3)
        ],
        0,
    )
    spread = dot(cots, flat, NT)
    cells = spread.shape[0] // 2
    for frame in range(4):
        total = None
        for kt in range(3):
            if 0 <= frame - kt < 2:
                term = spread[
                    (frame - kt) * cells : (frame - kt + 1) * cells, kt * LAST : (kt + 1) * LAST
                ]
                total = term if total is None else total + term
        put(frame, (total * slope[frame]).astype(BF))


def inner_kernel(
    scales, tile_ref, w1_any, w2_any, first_ref, second_ref, act, w1_ref, w2_ref,
    pair, cots, sems,
):
    load_w1 = pltpu.make_async_copy(w1_any, w1_ref, sems.at[0])
    load_w2 = pltpu.make_async_copy(w2_any, w2_ref, sems.at[1])
    load_w1.start()
    load_w2.start()
    keep = twice(scale_of(scales, KEEP))
    low = low_mask(scales, COLS)
    for frame in range(6):
        values = eff_frame(lambda f: tile_rows(tile_ref, f), frame, keep)
        values = values * sigmoid(values) * twice(low)
        shifted_act(act, (frame,), values)
    load_w1.wait()
    first_out = first_conv(
        lambda kw, kt, kh: act[kw, kt : kt + 4, kh : kh + 6].reshape(384, 256), w1_ref
    ).reshape(24, 16, LAST)
    gate = sigmoid(first_out)
    second_ref[...] = (first_out * gate * low).astype(BF).reshape(4, 6, 16, LAST)
    slope = gate * (1.0 + first_out * (1.0 - gate)) * low
    high = high_mask(scales, COLS)
    for frame in range(2):
        at = TILE_COT + frame * 32
        rows = tile_ref[at + 2 : at + 30].reshape(14, 32, LAST).astype(F32) * high
        tap_sums(rows, 1, 1, 6, pair, cots.at[frame])
    load_w2.wait()

    def put(frame, first_grad):
        first_ref[frame] = first_grad.reshape(6, 16, LAST)

    second_conv_back(cots[...].reshape(192, 1152), w2_ref, slope.reshape(4, 96, LAST), put)


def edge_kernel(
    rim_ref, scales, tile_ref, sib_ref, first_ref, second_ref, own_act, w1_ref, w2_ref, packet_ref,
    act, rows, pair, cots,
):
    odd = lax.axis_index("core")
    even = 1 - odd
    keep = twice(scale_of(scales, KEEP))
    low = low_mask(scales, COLS)
    wide_low = twice(low)
    rim_scale, sib_scale = scale_of(scales, RIM_SCALE), scale_of(scales, SIB_SCALE)
    for frame in range(6):
        for part, at, read, mask in (
            (odd, odd * 2, lambda f: joined(rim_ref[f * 4 : f * 4 + 4]), wide_low * twice(rim_scale)),
            (even, even * 2, lambda f: joined(sib_ref[pl.ds(f * 16 + odd * 12, 4)]), wide_low * twice(sib_scale)),
        ):
            values = eff_frame(lambda f, read=read: read(f).astype(F32), frame, keep)
            shifted_act(act, (frame, part, pl.ds(at, 2)), values * sigmoid(values) * mask)
    act[:, :, 0, 2:4] = own_act[:, :, 0:2]
    act[:, :, 1, 0:2] = own_act[:, :, 6:8]
    high = high_mask(scales, COLS)
    for frame in range(2):
        at = TILE_COT + frame * 32
        own = tile_ref[at : at + 32].reshape(16, 32, LAST)
        rows[frame, 0, 3:6] = own[0:3].astype(F32) * high
        rows[frame, 1, 0:3] = own[13:16].astype(F32) * high
        raw = rim_ref[RIM_COT + frame * 6 : RIM_COT + frame * 6 + 6].reshape(3, 32, LAST)
        rows[frame, odd, pl.ds(odd * 3, 3)] = raw.astype(F32) * (high * rim_scale)
        raw = sib_ref[pl.ds(at + odd * 26, 6)].reshape(3, 32, LAST)
        rows[frame, even, pl.ds(even * 3, 3)] = raw.astype(F32) * (high * sib_scale)
        far = rows[frame, odd, pl.ds(2 + odd, 1)].reshape(2, 16, LAST)
        packet_ref[PACK_ROW + frame * 2 : PACK_ROW + frame * 2 + 2] = far.astype(BF)
        tap_sums(rows[frame, 0], -3, -1, 2, pair, cots.at[frame, 0])
        tap_sums(rows[frame, 1], 13, 7, 2, pair, cots.at[frame, 1])
    first_out = first_conv(
        lambda kw, kt, kh: act[kw, kt : kt + 4, :, kh : kh + 2].reshape(256, 256), w1_ref
    ).reshape(16, 16, LAST)
    row = lax.broadcasted_iota(jnp.int32, (16, 1, 1), 0) % 4
    row_scale = jnp.where(
        row == 0, scale_of(scales, UP), jnp.where(row == 3, scale_of(scales, DOWN), 1.0)
    )
    gate = sigmoid(first_out)
    second_in = (first_out * gate * low).astype(BF)
    slope = gate * (1.0 + first_out * (1.0 - gate)) * (low * row_scale)
    for frame in range(4):
        at = PACK_SECOND + frame * 8
        packet_ref[at] = second_in[frame * 4 + 1]
        packet_ref[at + 1 : at + 7] = second_ref[frame]
        packet_ref[at + 7] = second_in[frame * 4 + 2]

    def put(frame, first_grad):
        blocks_now = first_grad.reshape(4, 16, LAST)
        packet_ref[frame * 10 : frame * 10 + 2] = blocks_now[0:2]
        packet_ref[frame * 10 + 2 : frame * 10 + 8] = first_ref[frame]
        packet_ref[frame * 10 + 8 : frame * 10 + 10] = blocks_now[2:4]

    second_conv_back(cots[...].reshape(128, 1152), w2_ref, slope.reshape(4, 64, LAST), put)


def sibling_kernel(scales, tile_ref, sib_ref, act_ref, sums_ref, token_ref, rows, pair):
    token_ref[...] = scales[...]
    keep = twice(scale_of(scales, SIB_KEEP))
    low = twice(low_mask(scales, SIB_COLS))
    for frame in range(6):
        values = eff_frame(lambda f: tile_rows(sib_ref, f), frame, keep)
        act_ref[frame] = (values * sigmoid(values) * low).astype(BF)
    odd = lax.axis_index("core")
    link = scale_of(scales, SIB_SCALE)
    rows[...] = jnp.zeros((18, 32, LAST), F32)
    for slot, tile, other, which in (
        (0, tile_ref, sib_ref, COLS),
        (1, sib_ref, tile_ref, SIB_COLS),
    ):
        lower = odd if slot == 0 else 1 - odd
        high = high_mask(scales, which)
        for frame in range(2):
            at = TILE_COT + frame * 32
            rows[1:17] = tile[at : at + 32].reshape(16, 32, LAST).astype(F32) * high
            near = other[pl.ds(at + lower * 30, 2)].reshape(1, 32, LAST)
            rows[pl.ds(17 - lower * 17, 1)] = near.astype(F32) * (high * link)

            def put(kw, values):
                for n in range(17):
                    place = n // 2 if n % 2 == 0 else 9 + n // 2
                    sums_ref[kw, slot, frame, place] = values[n]

            pair_sums(rows[...], pair, put)


def input_kernel(scales, in_any, packet_ref, w1_any, grad_ref, in_ref, w1_ref, firsts, sems):
    load_in = pltpu.make_async_copy(in_any, in_ref, sems.at[0])
    load_w1 = pltpu.make_async_copy(w1_any, w1_ref, sems.at[1])
    load_w1.start()
    load_in.start()
    for frame in range(4):
        first_grad = packet_ref[frame * 10 : frame * 10 + 10]
        before, after = column_shifts(first_grad.astype(F32))
        for kw, value in ((0, after.astype(BF)), (1, first_grad), (2, before.astype(BF))):
            for kh in range(3):
                tap = kh * 3 + kw
                firsts[frame, :, :, tap * LAST : (tap + 1) * LAST] = value[2 - kh : 10 - kh]
    load_w1.wait()
    load_in.wait()
    shifted = firsts[...].reshape(512, 1152)
    by_depth = [
        dot(shifted, jnp.concatenate([w1_ref[kt * 9 + tap] for tap in range(9)], 1), NT)
        for kt in range(3)
    ]
    keep = twice(scale_of(scales, KEEP))
    low = twice(low_mask(scales, COLS))
    carried = None
    for frame in range(6):
        total = None
        for kt in range(3):
            if 0 <= frame - kt < 4:
                term = by_depth[kt][(frame - kt) * 128 : (frame - kt + 1) * 128]
                total = term if total is None else total + term
        values = eff_frame(lambda f: in_ref[f].astype(F32), frame, keep)
        gate = sigmoid(values)
        pre = total.reshape(8, 16, 256) * (gate * (1.0 + values * (1.0 - gate)) * low)
        if frame < 4:
            carried = pre if carried is None else carried + pre
            grad_ref[frame] = (pre * keep).astype(BF)
        elif frame == 4:
            grad_ref[frame] = (pre + carried * (1.0 - keep)).astype(BF)
        else:
            grad_ref[frame] = pre.astype(BF)


def weight_kernel(
    packets_ref, scales, tile_ref, sib_ref, act_ref, sib_act_ref, sums_ref,
    part_ref, pair, sums, cols,
):
    odd = lax.axis_index("core")
    packet_ref, sib_packet_ref = packets_ref.at[odd], packets_ref.at[1 - odd]
    reps, quarters, per_quarter, depth = part_ref.shape[:4]
    sums[...] = sums_ref[...]
    for slot, tile, packet, which in (
        (0, tile_ref, packet_ref, COLS),
        (1, sib_ref, sib_packet_ref, SIB_COLS),
    ):
        lower = odd if slot == 0 else 1 - odd
        high = high_mask(scales, which)
        for frame in range(2):
            far = packet[PACK_ROW + frame * 2 : PACK_ROW + frame * 2 + 2].reshape(1, 32, LAST)
            last = tile[pl.ds(TILE_COT + frame * 32 + lower * 30, 2)].reshape(1, 32, LAST)
            rows = jnp.concatenate([far.astype(F32), last.astype(F32) * high], 0)

            def put(kw, values):
                sums[kw, slot, frame, pl.ds(lower * 8, 1)] = values

            pair_sums(rows, pair, put)
        for frame in range(4):
            first_grad = packet[frame * 10 : frame * 10 + 10]
            before, after = column_shifts(first_grad.astype(F32))
            cols[0, slot, frame] = after.astype(BF)
            cols[1, slot, frame] = first_grad
            cols[2, slot, frame] = before.astype(BF)

    def both(refs, kt, frames):
        return jnp.concatenate(
            [ref[kt : kt + frames].reshape(frames * 128, ref.shape[3]) for ref in refs], 0
        )

    act_all = jnp.concatenate([both((act_ref.at[1], sib_act_ref), kt, 4) for kt in range(3)], 1)
    seconds = [
        ref[PACK_SECOND:PACK_ROW].reshape(4, 8, 16, LAST) for ref in (packet_ref, sib_packet_ref)
    ]
    second_all = jnp.concatenate([both(seconds, kt, 2) for kt in range(3)], 1)

    def put_block(block, at):
        halves = block.astype(BF).reshape(reps, 2, depth, LAST)
        for half in range(2):
            quarter, place = divmod(at * 2 + half, per_quarter)
            for rep in range(reps):
                first = rep + (quarter - rep) * odd
                part_ref[first, rep + quarter - first, place] = halves[rep, half]

    def first_taps(step, at):
        tap = 5 * odd + step
        window = cols[tap % 3, :, :, pl.ds(2 - tap // 3, 8)].reshape(1024, LAST)
        block = dot(window, act_all, TN)
        for n in range(6):
            put_block(block[:, n * LAST : (n + 1) * LAST], at + n)

    def second_taps(step, at):
        tap = 4 * odd + step
        kh = tap // 3
        begin = jnp.where(kh == 0, 1, jnp.where(kh == 1, 9, 0))
        window = sums[tap % 3, :, :, pl.ds(begin, 8)].reshape(512, LAST)
        block = dot(window, second_all, TN)
        for n in range(3):
            put_block(block[:, n * LAST : (n + 1) * LAST], at + n)

    for step in range(4):
        first_taps(step, step * 6)
        second_taps(step, SECOND_AT + step * 3)

    @pl.when(odd == 0)
    def _():
        first_taps(4, EXTRA_AT)

    @pl.when(odd == 1)
    def _():
        second_taps(4, EXTRA_AT)
        for at in range(EXTRA_AT + 3, EXTRA_AT + 6):
            put_block(jnp.zeros((LAST, LAST), F32), at)


def near_sum_kernel(parts_ref, sum_ref):
    shares, others, share, _ = sum_ref.shape
    rows = parts_ref.shape[2]
    for other in range(others):
        total = parts_ref[0, other].astype(F32)
        for n in range(1, parts_ref.shape[0]):
            total = total + parts_ref[n, other].astype(F32)
        if shares * share > rows:
            padding = jnp.zeros((shares * share - rows, LAST), F32)
            total = jnp.concatenate([total, padding], 0)
        sum_ref[:, other] = total.reshape(shares, share, LAST).astype(BF)


def far_sum_kernel(parts_ref, scales, copies_ref, token_ref):
    token_ref[...] = scales[...]
    total = parts_ref[0].astype(F32)
    for n in range(1, parts_ref.shape[0]):
        total = total + parts_ref[n].astype(F32)
    copies_ref[...] = jnp.broadcast_to(total.astype(BF)[None], copies_ref.shape)


def sum_groups(sizes):
    numbers = np.arange(math.prod(sizes)).reshape(sizes)
    even, odd = numbers[..., 0, :], numbers[..., 1, :]
    reps, quarters = sizes[5], sizes[1] * sizes[3]
    near = (
        even.reshape(-1, reps),
        odd.transpose(0, 2, 4, 1, 3).reshape(-1, quarters),
    )
    far = (
        even.transpose(4, 2, 0, 1, 3).reshape(reps, -1),
        odd.transpose(1, 3, 2, 0, 4).reshape(quarters, -1),
    )
    return [[row.tolist() for part in parts for row in part] for parts in (near, far)]


def finish_kernel(scale, per_quarter, whole_ref, _, first_ref, second_ref):
    depth = first_ref.shape[1] // 2
    for core in range(2):

        def put(target, tap, columns, at):
            for half in range(2):
                quarter, place = divmod(at * 2 + half, per_quarter)
                rows = whole_ref[core, quarter, place * depth : (place + 1) * depth]
                target[tap, half * depth : (half + 1) * depth, columns] = rows.astype(F32) * scale

        for step in range(5 - core):
            for kt in range(3):
                for half in range(2):
                    at = (step * 6 if step < 4 else EXTRA_AT) + kt * 2 + half
                    columns = slice(half * LAST, (half + 1) * LAST)
                    put(first_ref, kt * 9 + 5 * core + step, columns, at)
        for step in range(4 + core):
            for kt in range(3):
                at = (SECOND_AT + step * 3 if step < 4 else EXTRA_AT) + kt
                put(second_ref, kt * 9 + 4 * core + step, slice(0, LAST), at)


VMEM = pl.BlockSpec(memory_space=pltpu.VMEM)
HBM = pl.BlockSpec(memory_space=pltpu.HBM)
ANY = pl.BlockSpec(memory_space=pl.ANY)


def params(mebibytes):
    return pltpu.CompilerParams(vmem_limit_bytes=mebibytes << 20)


def cost(flops, moved):
    return pl.CostEstimate(flops=flops, bytes_accessed=moved, transcendentals=0)


def wide_sum(parts):
    return jnp.sum(parts.astype(F32), axis=0).astype(BF)


def blocks(count):
    return jax.ShapeDtypeStruct((count, 16, LAST), BF)


def body(inputs, cotangent, first_weight, second_weight, tile_clip, clip_cols, clip_start):
    tiles = lax.axis_size(TILE_AXES)
    reps, near_y, near_z = (lax.axis_size(name) for name in ("x", "yl", "zl"))
    plane = lax.axis_size(PLANE_AXES)
    near_groups, far_groups = sum_groups(tuple(map(lax.axis_size, ALL_AXES)))
    local_in, local_cot, tile_clip, clip_cols, clip_start, w1, w2 = (
        pltpu.with_memory_space_constraint(array, pltpu.HBM)
        for array in (
            inputs[0],
            cotangent[0],
            tile_clip,
            clip_cols,
            clip_start,
            first_weight.reshape(27, 256, LAST),
            second_weight.reshape(27, LAST, LAST),
        )
    )
    swap = [(0, 1), (1, 0)]
    across = [(i, (i + 1) % tiles) for i in range(1, tiles, 2)]
    across += [(b, a) for a, b in across]
    own_rim, tile, scales = pl.pallas_call(
        pack_kernel,
        out_shape=(blocks(RIM_BLOCKS), blocks(TILE_BLOCKS), jax.ShapeDtypeStruct((8, LAST), F32)),
        in_specs=[HBM] * 5,
        out_specs=(VMEM, VMEM, VMEM),
        scratch_shapes=[
            pltpu.SMEM(tile_clip.shape, jnp.int32),
            pltpu.SMEM(clip_cols.shape, jnp.int32),
            pltpu.SMEM(clip_start.shape, jnp.int32),
            pltpu.VMEM(local_in.shape, BF),
            pltpu.VMEM(local_cot.shape, BF),
            pltpu.SemaphoreType.DMA((5,)),
        ],
        compiler_params=params(8),
        cost_estimate=cost(10**6, 2 * 10**6),
    )(tile_clip, clip_cols, clip_start, local_in, local_cot)
    rim = lax.ppermute(own_rim, TILE_AXES, across)
    sibling = lax.ppermute(tile, "core", swap)

    inner_first, inner_second, act, inner_w1, inner_w2 = pl.pallas_call(
        inner_kernel,
        out_shape=(
            jax.ShapeDtypeStruct((4, 6, 16, LAST), BF),
            jax.ShapeDtypeStruct((4, 6, 16, LAST), BF),
            jax.ShapeDtypeStruct((3, 6, 8, 16, 256), BF),
            jax.ShapeDtypeStruct(w1.shape, BF),
            jax.ShapeDtypeStruct(w2.shape, BF),
        ),
        in_specs=[VMEM] * 2 + [HBM] * 2,
        out_specs=(VMEM,) * 5,
        scratch_shapes=[
            pltpu.VMEM((13, 48, LAST), F32),
            pltpu.VMEM((2, 6, 16, 9 * LAST), BF),
            pltpu.SemaphoreType.DMA((2,)),
        ],
        compiler_params=params(24),
        cost_estimate=cost(2 * 10**9, 4 * 10**6),
    )(scales, tile, w1, w2)

    sib_act, sums, scales = pl.pallas_call(
        sibling_kernel,
        out_shape=(
            jax.ShapeDtypeStruct((6, 8, 16, 256), BF),
            jax.ShapeDtypeStruct((3, 2, 2, 17, 16, LAST), BF),
            jax.ShapeDtypeStruct(scales.shape, F32),
        ),
        in_specs=[VMEM] * 3,
        out_specs=(VMEM, VMEM, VMEM),
        scratch_shapes=[
            pltpu.VMEM((18, 32, LAST), F32),
            pltpu.VMEM((17, 48, LAST), F32),
        ],
        compiler_params=params(16),
        cost_estimate=cost(10**9, 2 * 10**6),
    )(scales, tile, sibling)

    packet = pl.pallas_call(
        edge_kernel,
        out_shape=blocks(PACK_BLOCKS),
        in_specs=[VMEM] * 9,
        out_specs=VMEM,
        scratch_shapes=[
            pltpu.VMEM((3, 6, 2, 4, 16, 256), BF),
            pltpu.VMEM((2, 2, 6, 32, LAST), F32),
            pltpu.VMEM((5, 48, LAST), F32),
            pltpu.VMEM((2, 2, 2, 16, 9 * LAST), BF),
        ],
        compiler_params=params(16),
        cost_estimate=cost(10**9, 4 * 10**6),
    )(rim, scales, tile, sibling, inner_first, inner_second, act, inner_w1, inner_w2)
    packets = lax.all_gather(packet, "core", axis=0)

    depth = LAST // reps
    quarters = near_y * near_z
    per_quarter = 2 * GRAD_BLOCKS // quarters
    parts = pl.pallas_call(
        weight_kernel,
        out_shape=jax.ShapeDtypeStruct(
            (reps, quarters, per_quarter, depth // 2, LAST), BF
        ),
        in_specs=[VMEM] * 7,
        out_specs=VMEM,
        scratch_shapes=[
            pltpu.VMEM((1, 48, LAST), F32),
            pltpu.VMEM((3, 2, 2, 17, 16, LAST), BF),
            pltpu.VMEM((3, 2, 4, 10, 16, LAST), BF),
        ],
        compiler_params=params(24),
        cost_estimate=cost(2 * 10**9, 4 * 10**6),
    )(packets, scales, tile, sibling, act, sib_act, sums)

    count = per_quarter * depth // 2
    share = -(-count * quarters // plane // 8) * 8
    parts = parts.reshape(reps, quarters, count, LAST)

    def exchange(values, groups):
        return lax.all_to_all(values, ALL_AXES, 0, 0, axis_index_groups=groups, tiled=True)

    near = pl.pallas_call(
        near_sum_kernel,
        out_shape=jax.ShapeDtypeStruct((plane // quarters, quarters, share, LAST), BF),
        in_specs=[VMEM],
        out_specs=VMEM,
        compiler_params=params(8),
        cost_estimate=cost(10**6, 2 * 10**6),
    )(exchange(parts, near_groups))
    near = near.reshape(plane, share, LAST)
    copies, token = pl.pallas_call(
        far_sum_kernel,
        out_shape=(
            jax.ShapeDtypeStruct((plane, share, LAST), BF),
            jax.ShapeDtypeStruct(scales.shape, F32),
        ),
        in_specs=[VMEM, VMEM],
        out_specs=(VMEM, VMEM),
        compiler_params=params(8),
        cost_estimate=cost(10**5, 5 * 10**5),
    )(exchange(near, far_groups), scales)
    input_grad = pl.pallas_call(
        input_kernel,
        out_shape=jax.ShapeDtypeStruct(local_in.shape, BF),
        in_specs=[VMEM, HBM, VMEM, HBM],
        out_specs=VMEM,
        scratch_shapes=[
            pltpu.VMEM(local_in.shape, BF),
            pltpu.VMEM(w1.shape, BF),
            pltpu.VMEM((4, 8, 16, 9 * LAST), BF),
            pltpu.SemaphoreType.DMA((2,)),
        ],
        compiler_params=params(24),
        cost_estimate=cost(2 * 10**9, 4 * 10**6),
    )(token, local_in, packet, w1)

    half = lax.all_to_all(copies, PLANE_AXES, 0, 0, tiled=True)
    whole = lax.all_gather(half.reshape(quarters, plane // quarters * share, LAST), "core", axis=0)

    cell_total = tiles * reps * cotangent.shape[1] * cotangent.shape[2] * cotangent.shape[3]
    scale = 1.0 / math.sqrt(cell_total)
    first, second = pl.pallas_call(
        lambda *refs: finish_kernel(scale, per_quarter, *refs),
        out_shape=(
            jax.ShapeDtypeStruct((27, depth, 256), F32),
            jax.ShapeDtypeStruct((27, depth, LAST), F32),
        ),
        in_specs=[VMEM, ANY],
        out_specs=(VMEM, VMEM),
        compiler_params=params(16),
    )(whole, pltpu.with_memory_space_constraint(input_grad, pltpu.HBM))
    first = jnp.swapaxes(first, 1, 2).reshape(3, 3, 3, 256, depth)
    second = jnp.swapaxes(second, 1, 2).reshape(3, 3, 3, LAST, depth)
    return input_grad[None], first, second


def solution(mesh):
    devices = mesh.devices
    tiles, reps = devices.shape
    height = math.isqrt(tiles // 2)
    width = tiles // 2 // height
    near_y, near_z = math.gcd(height, 2), math.gcd(width, 2)
    wide_mesh = Mesh(
        devices.reshape(height // near_y, near_y, width // near_z, near_z, 2, reps),
        (*TILE_AXES, "x"),
    )
    in_specs = (
        P("x", None, TILE_AXES, None, None),
        P("x", None, TILE_AXES, None, None),
        P(),
        P(),
        P("x", None),
        P("x", None),
        P("x", None),
    )
    out_specs = (
        P("x", None, TILE_AXES, None, None),
        P(None, None, None, None, "x"),
        P(None, None, None, None, "x"),
    )
    return jax.shard_map(
        body, mesh=wide_mesh, in_specs=in_specs, out_specs=out_specs, check_vma=False
    )
```

```python
import math

import jax
import jax.numpy as jnp
import numpy as np
from jax import lax
from jax.experimental import pallas as pl
from jax.experimental.pallas import tpu as pltpu
from jax.sharding import Mesh
from jax.sharding import PartitionSpec as P

TILE_AXES = ("yh", "yl", "zh", "zl", "core")
ALL_AXES = (*TILE_AXES, "x")
PLANE_AXES = ("yl", "zl", "zh", "yh")
BF = jnp.bfloat16
F32 = jnp.float32
NT = (((1,), (1,)), ((), ()))
TN = (((0,), (0,)), ((), ()))
LAST = 128
TILE_COT = 96
TILE_BLOCKS = 160
RIM_COT = 24
RIM_BLOCKS = 36
PACK_SECOND = 40
PACK_ROW = 72
PACK_BLOCKS = 76
UP, DOWN, COLS, KEEP, SIB_COLS, SIB_KEEP, RIM_SCALE, SIB_SCALE = range(8)
SECOND_AT = 24
EXTRA_AT = 36
GRAD_BLOCKS = 42


def dot(lhs, rhs, dims=(((1,), (0,)), ((), ()))):
    return lax.dot_general(lhs, rhs, dims, preferred_element_type=F32)


def sigmoid(values):
    return 1.0 / (1.0 + jnp.exp(-values))


def column_shifts(values):
    column = lax.broadcasted_iota(jnp.int32, (1, 16, values.shape[2]), 1)
    left = jnp.where(column == 0, 0.0, pltpu.roll(values, 1, 1))
    right = jnp.where(column == 15, 0.0, pltpu.roll(values, 15, 1))
    return left, right


def scale_of(scales, which):
    return scales[which : which + 1].reshape(1, 1, LAST)


def low_mask(scales, which):
    column = lax.broadcasted_iota(jnp.int32, (1, 16, LAST), 1).astype(F32)
    return jnp.where(column < scale_of(scales, which), 1.0, 0.0)


def high_mask(scales, which):
    column = lax.broadcasted_iota(jnp.int32, (1, 32, LAST), 1).astype(F32)
    return jnp.where(column < 2.0 * scale_of(scales, which), 1.0, 0.0)


def twice(values):
    return jnp.concatenate([values, values], 2)


def joined(blocks):
    halves = blocks.reshape(blocks.shape[0] // 2, 2, 16, LAST)
    return jnp.concatenate([halves[:, 0], halves[:, 1]], 2)


def tile_rows(tile_ref, frame):
    return joined(tile_ref[frame * 16 : frame * 16 + 16]).astype(F32)


def eff_frame(read, frame, keep):
    values = read(frame)
    return jnp.where(keep > 0.5, values, read(4)) if frame < 4 else values


def load_scales(clip_ref, cols_ref, start_ref):
    tile = lax.axis_index(TILE_AXES)
    tiles = lax.axis_size(TILE_AXES)
    even = lax.axis_index("core") == 0
    own = clip_ref[0, tile]
    up_same = (tile > 0) & (clip_ref[0, jnp.maximum(tile - 1, 0)] == own)
    down_same = (tile + 1 < tiles) & (clip_ref[0, jnp.minimum(tile + 1, tiles - 1)] == own)
    sibling = clip_ref[0, jnp.where(even, tile + 1, tile - 1)]
    up = jnp.where(up_same, 1.0, 0.0)
    down = jnp.where(down_same, 1.0, 0.0)
    return (
        up,
        down,
        cols_ref[0, own].astype(F32),
        jnp.where(start_ref[0, own] == 0, 0.0, 1.0),
        cols_ref[0, sibling].astype(F32),
        jnp.where(start_ref[0, sibling] == 0, 0.0, 1.0),
        jnp.where(even, up, down),
        jnp.where(even, down, up),
    )


def pack_kernel(
    clip_any, cols_any, start_any, in_any, cot_any, rim_ref, tile_ref, scales_ref,
    clip_ref, cols_ref, start_ref, in_ref, cot_ref, sems,
):
    copies = [
        pltpu.make_async_copy(source, target, sems.at[n])
        for n, (source, target) in enumerate(
            (
                (clip_any, clip_ref),
                (cols_any, cols_ref),
                (start_any, start_ref),
                (in_any, in_ref),
                (cot_any, cot_ref),
            )
        )
    ]
    for copy in copies:
        copy.start()
    copies[3].wait()
    for frame in range(6):
        for row in range(8):
            for half in range(2):
                tile_ref[frame * 16 + row * 2 + half] = in_ref[
                    frame, row, :, half * LAST : (half + 1) * LAST
                ]
    copies[4].wait()
    for frame in range(2):
        for half in range(2):
            for row in range(16):
                tile_ref[TILE_COT + frame * 32 + row * 2 + half] = cot_ref[
                    frame, row, half * 16 : (half + 1) * 16, :
                ]
    odd = lax.axis_index("core")
    for frame in range(6):
        rim_ref[frame * 4 : frame * 4 + 4] = tile_ref[pl.ds(frame * 16 + odd * 12, 4)]
    for frame in range(2):
        at = RIM_COT + frame * 6
        rim_ref[at : at + 6] = tile_ref[pl.ds(TILE_COT + frame * 32 + odd * 26, 6)]
    for copy in copies[:3]:
        copy.wait()
    for row, value in enumerate(load_scales(clip_ref, cols_ref, start_ref)):
        scales_ref[row : row + 1] = jnp.full((1, LAST), value, F32)


def pair_sums(rows, pair, put):
    count = rows.shape[0] - 1
    zeros = jnp.zeros((count, 8, LAST), F32)
    pair[0:count, 0:8] = zeros
    pair[0:count, 40:48] = zeros
    pair[0:count, 8:40] = rows[0:count] + rows[1 : count + 1]
    before, even, odd, after = (pair[0:count, pl.ds(begin, 16, 2), :] for begin in (7, 8, 9, 10))
    for kw, value in ((0, odd + after), (1, even + odd), (2, before + even)):
        put(kw, value.astype(BF))


def tap_sums(rows, first, begin, count, pair, cots):
    def put(kw, sums):
        for n in range(sums.shape[0]):
            row = first + n
            if row % 2 == 0:
                targets = ((1, row // 2),)
            else:
                targets = ((0, (row - 1) // 2), (2, (row + 1) // 2))
            for kh, place in targets:
                if begin <= place < begin + count:
                    tap = kh * 3 + kw
                    cots[place - begin, :, tap * LAST : (tap + 1) * LAST] = sums[n]

    pair_sums(rows, pair, put)


def shifted_act(act, at, values):
    left, right = column_shifts(values)
    for kw, shifted in enumerate((left, values, right)):
        act[(kw, *at)] = shifted.astype(BF)


def first_conv(windows, w1_ref):
    total = None
    for step in range(9):
        window = jnp.concatenate([windows(kw, step // 3, step % 3) for kw in range(3)], 1)
        term = dot(window, w1_ref[step * 3 : step * 3 + 3].reshape(768, LAST))
        total = term if total is None else total + term
    return total


def second_conv_back(cots, w2_ref, slope, put):
    flat = jnp.concatenate(
        [
            jnp.concatenate([w2_ref[kt * 9 + tap] for tap in range(9)], 1)
            for kt in range(3)
        ],
        0,
    )
    spread = dot(cots, flat, NT)
    cells = spread.shape[0] // 2
    for frame in range(4):
        total = None
        for kt in range(3):
            if 0 <= frame - kt < 2:
                term = spread[
                    (frame - kt) * cells : (frame - kt + 1) * cells, kt * LAST : (kt + 1) * LAST
                ]
                total = term if total is None else total + term
        put(frame, (total * slope[frame]).astype(BF))


def inner_kernel(
    scales, tile_ref, w1_any, w2_any, first_ref, second_ref, act, w1_ref, w2_ref,
    pair, cots, sems,
):
    load_w1 = pltpu.make_async_copy(w1_any, w1_ref, sems.at[0])
    load_w2 = pltpu.make_async_copy(w2_any, w2_ref, sems.at[1])
    load_w1.start()
    load_w2.start()
    keep = twice(scale_of(scales, KEEP))
    low = low_mask(scales, COLS)
    for frame in range(6):
        values = eff_frame(lambda f: tile_rows(tile_ref, f), frame, keep)
        values = values * sigmoid(values) * twice(low)
        shifted_act(act, (frame,), values)
    load_w1.wait()
    first_out = first_conv(
        lambda kw, kt, kh: act[kw, kt : kt + 4, kh : kh + 6].reshape(384, 256), w1_ref
    ).reshape(24, 16, LAST)
    gate = sigmoid(first_out)
    second_ref[...] = (first_out * gate * low).astype(BF).reshape(4, 6, 16, LAST)
    slope = gate * (1.0 + first_out * (1.0 - gate)) * low
    high = high_mask(scales, COLS)
    for frame in range(2):
        at = TILE_COT + frame * 32
        rows = tile_ref[at + 2 : at + 30].reshape(14, 32, LAST).astype(F32) * high
        tap_sums(rows, 1, 1, 6, pair, cots.at[frame])
    load_w2.wait()

    def put(frame, first_grad):
        first_ref[frame] = first_grad.reshape(6, 16, LAST)

    second_conv_back(cots[...].reshape(192, 1152), w2_ref, slope.reshape(4, 96, LAST), put)


def edge_kernel(
    rim_ref, scales, tile_ref, sib_ref, first_ref, second_ref, own_act, w1_ref, w2_ref, packet_ref,
    act, rows, pair, cots,
):
    odd = lax.axis_index("core")
    even = 1 - odd
    keep = twice(scale_of(scales, KEEP))
    low = low_mask(scales, COLS)
    wide_low = twice(low)
    rim_scale, sib_scale = scale_of(scales, RIM_SCALE), scale_of(scales, SIB_SCALE)
    for frame in range(6):
        for part, at, read, mask in (
            (odd, odd * 2, lambda f: joined(rim_ref[f * 4 : f * 4 + 4]), wide_low * twice(rim_scale)),
            (even, even * 2, lambda f: joined(sib_ref[pl.ds(f * 16 + odd * 12, 4)]), wide_low * twice(sib_scale)),
        ):
            values = eff_frame(lambda f, read=read: read(f).astype(F32), frame, keep)
            shifted_act(act, (frame, part, pl.ds(at, 2)), values * sigmoid(values) * mask)
    act[:, :, 0, 2:4] = own_act[:, :, 0:2]
    act[:, :, 1, 0:2] = own_act[:, :, 6:8]
    high = high_mask(scales, COLS)
    for frame in range(2):
        at = TILE_COT + frame * 32
        own = tile_ref[at : at + 32].reshape(16, 32, LAST)
        rows[frame, 0, 3:6] = own[0:3].astype(F32) * high
        rows[frame, 1, 0:3] = own[13:16].astype(F32) * high
        raw = rim_ref[RIM_COT + frame * 6 : RIM_COT + frame * 6 + 6].reshape(3, 32, LAST)
        rows[frame, odd, pl.ds(odd * 3, 3)] = raw.astype(F32) * (high * rim_scale)
        raw = sib_ref[pl.ds(at + odd * 26, 6)].reshape(3, 32, LAST)
        rows[frame, even, pl.ds(even * 3, 3)] = raw.astype(F32) * (high * sib_scale)
        far = rows[frame, odd, pl.ds(2 + odd, 1)].reshape(2, 16, LAST)
        packet_ref[PACK_ROW + frame * 2 : PACK_ROW + frame * 2 + 2] = far.astype(BF)
        tap_sums(rows[frame, 0], -3, -1, 2, pair, cots.at[frame, 0])
        tap_sums(rows[frame, 1], 13, 7, 2, pair, cots.at[frame, 1])
    first_out = first_conv(
        lambda kw, kt, kh: act[kw, kt : kt + 4, :, kh : kh + 2].reshape(256, 256), w1_ref
    ).reshape(16, 16, LAST)
    row = lax.broadcasted_iota(jnp.int32, (16, 1, 1), 0) % 4
    row_scale = jnp.where(
        row == 0, scale_of(scales, UP), jnp.where(row == 3, scale_of(scales, DOWN), 1.0)
    )
    gate = sigmoid(first_out)
    second_in = (first_out * gate * low).astype(BF)
    slope = gate * (1.0 + first_out * (1.0 - gate)) * (low * row_scale)
    for frame in range(4):
        at = PACK_SECOND + frame * 8
        packet_ref[at] = second_in[frame * 4 + 1]
        packet_ref[at + 1 : at + 7] = second_ref[frame]
        packet_ref[at + 7] = second_in[frame * 4 + 2]

    def put(frame, first_grad):
        blocks_now = first_grad.reshape(4, 16, LAST)
        packet_ref[frame * 10 : frame * 10 + 2] = blocks_now[0:2]
        packet_ref[frame * 10 + 2 : frame * 10 + 8] = first_ref[frame]
        packet_ref[frame * 10 + 8 : frame * 10 + 10] = blocks_now[2:4]

    second_conv_back(cots[...].reshape(128, 1152), w2_ref, slope.reshape(4, 64, LAST), put)


def sibling_kernel(scales, tile_ref, sib_ref, act_ref, sums_ref, token_ref, rows, pair):
    token_ref[...] = scales[...]
    keep = twice(scale_of(scales, SIB_KEEP))
    low = twice(low_mask(scales, SIB_COLS))
    for frame in range(6):
        values = eff_frame(lambda f: tile_rows(sib_ref, f), frame, keep)
        act_ref[frame] = (values * sigmoid(values) * low).astype(BF)
    odd = lax.axis_index("core")
    link = scale_of(scales, SIB_SCALE)
    rows[...] = jnp.zeros((18, 32, LAST), F32)
    for slot, tile, other, which in (
        (0, tile_ref, sib_ref, COLS),
        (1, sib_ref, tile_ref, SIB_COLS),
    ):
        lower = odd if slot == 0 else 1 - odd
        high = high_mask(scales, which)
        for frame in range(2):
            at = TILE_COT + frame * 32
            rows[1:17] = tile[at : at + 32].reshape(16, 32, LAST).astype(F32) * high
            near = other[pl.ds(at + lower * 30, 2)].reshape(1, 32, LAST)
            rows[pl.ds(17 - lower * 17, 1)] = near.astype(F32) * (high * link)

            def put(kw, values):
                for n in range(17):
                    place = n // 2 if n % 2 == 0 else 9 + n // 2
                    sums_ref[kw, slot, frame, place] = values[n]

            pair_sums(rows[...], pair, put)


def input_kernel(scales, in_any, packet_ref, w1_any, grad_ref, in_ref, w1_ref, firsts, sems):
    load_in = pltpu.make_async_copy(in_any, in_ref, sems.at[0])
    load_w1 = pltpu.make_async_copy(w1_any, w1_ref, sems.at[1])
    load_w1.start()
    load_in.start()
    for frame in range(4):
        first_grad = packet_ref[frame * 10 : frame * 10 + 10]
        before, after = column_shifts(first_grad.astype(F32))
        for kw, value in ((0, after.astype(BF)), (1, first_grad), (2, before.astype(BF))):
            for kh in range(3):
                tap = kh * 3 + kw
                firsts[frame, :, :, tap * LAST : (tap + 1) * LAST] = value[2 - kh : 10 - kh]
    load_w1.wait()
    load_in.wait()
    shifted = firsts[...].reshape(512, 1152)
    by_depth = [
        dot(shifted, jnp.concatenate([w1_ref[kt * 9 + tap] for tap in range(9)], 1), NT)
        for kt in range(3)
    ]
    keep = twice(scale_of(scales, KEEP))
    low = twice(low_mask(scales, COLS))
    carried = None
    for frame in range(6):
        total = None
        for kt in range(3):
            if 0 <= frame - kt < 4:
                term = by_depth[kt][(frame - kt) * 128 : (frame - kt + 1) * 128]
                total = term if total is None else total + term
        values = eff_frame(lambda f: in_ref[f].astype(F32), frame, keep)
        gate = sigmoid(values)
        pre = total.reshape(8, 16, 256) * (gate * (1.0 + values * (1.0 - gate)) * low)
        if frame < 4:
            carried = pre if carried is None else carried + pre
            grad_ref[frame] = (pre * keep).astype(BF)
        elif frame == 4:
            grad_ref[frame] = (pre + carried * (1.0 - keep)).astype(BF)
        else:
            grad_ref[frame] = pre.astype(BF)


def weight_kernel(
    packets_ref, scales, tile_ref, sib_ref, act_ref, sib_act_ref, _,
    part_ref, sums, pair, cols,
):
    odd = lax.axis_index("core")
    packet_ref, sib_packet_ref = packets_ref.at[odd], packets_ref.at[1 - odd]
    reps, quarters, per_quarter, depth = part_ref.shape[:4]
    for slot, tile, packet, which in (
        (0, tile_ref, packet_ref, COLS),
        (1, sib_ref, sib_packet_ref, SIB_COLS),
    ):
        lower = odd if slot == 0 else 1 - odd
        high = high_mask(scales, which)
        for frame in range(2):
            far = packet[PACK_ROW + frame * 2 : PACK_ROW + frame * 2 + 2].reshape(1, 32, LAST)
            last = tile[pl.ds(TILE_COT + frame * 32 + lower * 30, 2)].reshape(1, 32, LAST)
            rows = jnp.concatenate([far.astype(F32), last.astype(F32) * high], 0)

            def put(kw, values):
                sums[kw, slot, frame, pl.ds(lower * 8, 1)] = values

            pair_sums(rows, pair, put)
        for frame in range(4):
            first_grad = packet[frame * 10 : frame * 10 + 10]
            before, after = column_shifts(first_grad.astype(F32))
            cols[0, slot, frame] = after.astype(BF)
            cols[1, slot, frame] = first_grad
            cols[2, slot, frame] = before.astype(BF)

    def both(refs, kt, frames):
        return jnp.concatenate(
            [ref[kt : kt + frames].reshape(frames * 128, ref.shape[3]) for ref in refs], 0
        )

    act_all = jnp.concatenate([both((act_ref.at[1], sib_act_ref), kt, 4) for kt in range(3)], 1)
    seconds = [
        ref[PACK_SECOND:PACK_ROW].reshape(4, 8, 16, LAST) for ref in (packet_ref, sib_packet_ref)
    ]
    second_all = jnp.concatenate([both(seconds, kt, 2) for kt in range(3)], 1)

    def put_block(block, at):
        halves = block.astype(BF).reshape(reps, 2, depth, LAST)
        for half in range(2):
            quarter, place = divmod(at * 2 + half, per_quarter)
            for rep in range(reps):
                first = rep + (quarter - rep) * odd
                part_ref[first, rep + quarter - first, place] = halves[rep, half]

    def first_taps(step, at):
        tap = 5 * odd + step
        window = cols[tap % 3, :, :, pl.ds(2 - tap // 3, 8)].reshape(1024, LAST)
        block = dot(window, act_all, TN)
        for n in range(6):
            put_block(block[:, n * LAST : (n + 1) * LAST], at + n)

    def second_taps(step, at):
        tap = 4 * odd + step
        kh = tap // 3
        begin = jnp.where(kh == 0, 1, jnp.where(kh == 1, 9, 0))
        window = sums[tap % 3, :, :, pl.ds(begin, 8)].reshape(512, LAST)
        block = dot(window, second_all, TN)
        for n in range(3):
            put_block(block[:, n * LAST : (n + 1) * LAST], at + n)

    for step in range(4):
        first_taps(step, step * 6)
        second_taps(step, SECOND_AT + step * 3)

    @pl.when(odd == 0)
    def _():
        first_taps(4, EXTRA_AT)

    @pl.when(odd == 1)
    def _():
        second_taps(4, EXTRA_AT)
        for at in range(EXTRA_AT + 3, EXTRA_AT + 6):
            put_block(jnp.zeros((LAST, LAST), F32), at)


def near_sum_kernel(parts_ref, sum_ref):
    shares, others, share, _ = sum_ref.shape
    rows = parts_ref.shape[2]
    for other in range(others):
        total = parts_ref[0, other].astype(F32)
        for n in range(1, parts_ref.shape[0]):
            total = total + parts_ref[n, other].astype(F32)
        if shares * share > rows:
            padding = jnp.zeros((shares * share - rows, LAST), F32)
            total = jnp.concatenate([total, padding], 0)
        sum_ref[:, other] = total.reshape(shares, share, LAST).astype(BF)


def far_sum_kernel(parts_ref, scales, copies_ref, token_ref):
    token_ref[...] = scales[...]
    total = parts_ref[0].astype(F32)
    for n in range(1, parts_ref.shape[0]):
        total = total + parts_ref[n].astype(F32)
    copies_ref[...] = jnp.broadcast_to(total.astype(BF)[None], copies_ref.shape)


def sum_groups(sizes):
    numbers = np.arange(math.prod(sizes)).reshape(sizes)
    even, odd = numbers[..., 0, :], numbers[..., 1, :]
    reps, quarters = sizes[5], sizes[1] * sizes[3]
    near = (
        even.reshape(-1, reps),
        odd.transpose(0, 2, 4, 1, 3).reshape(-1, quarters),
    )
    far = (
        even.transpose(4, 2, 0, 1, 3).reshape(reps, -1),
        odd.transpose(1, 3, 2, 0, 4).reshape(quarters, -1),
    )
    return [[row.tolist() for part in parts for row in part] for parts in (near, far)]


def finish_kernel(scale, per_quarter, whole_ref, _, first_ref, second_ref):
    depth = first_ref.shape[1] // 2
    for core in range(2):

        def put(target, tap, columns, at):
            for half in range(2):
                quarter, place = divmod(at * 2 + half, per_quarter)
                rows = whole_ref[core, quarter, place * depth : (place + 1) * depth]
                target[tap, half * depth : (half + 1) * depth, columns] = rows.astype(F32) * scale

        for step in range(5 - core):
            for kt in range(3):
                for half in range(2):
                    at = (step * 6 if step < 4 else EXTRA_AT) + kt * 2 + half
                    columns = slice(half * LAST, (half + 1) * LAST)
                    put(first_ref, kt * 9 + 5 * core + step, columns, at)
        for step in range(4 + core):
            for kt in range(3):
                at = (SECOND_AT + step * 3 if step < 4 else EXTRA_AT) + kt
                put(second_ref, kt * 9 + 4 * core + step, slice(0, LAST), at)


VMEM = pl.BlockSpec(memory_space=pltpu.VMEM)
HBM = pl.BlockSpec(memory_space=pltpu.HBM)
ANY = pl.BlockSpec(memory_space=pl.ANY)


def params(mebibytes):
    return pltpu.CompilerParams(vmem_limit_bytes=mebibytes << 20)


def cost(flops, moved):
    return pl.CostEstimate(flops=flops, bytes_accessed=moved, transcendentals=0)


def wide_sum(parts):
    return jnp.sum(parts.astype(F32), axis=0).astype(BF)


def blocks(count):
    return jax.ShapeDtypeStruct((count, 16, LAST), BF)


def body(inputs, cotangent, first_weight, second_weight, tile_clip, clip_cols, clip_start):
    tiles = lax.axis_size(TILE_AXES)
    reps, near_y, near_z = (lax.axis_size(name) for name in ("x", "yl", "zl"))
    plane = lax.axis_size(PLANE_AXES)
    near_groups, far_groups = sum_groups(tuple(map(lax.axis_size, ALL_AXES)))
    local_in, local_cot, tile_clip, clip_cols, clip_start, w1, w2 = (
        pltpu.with_memory_space_constraint(array, pltpu.HBM)
        for array in (
            inputs[0],
            cotangent[0],
            tile_clip,
            clip_cols,
            clip_start,
            first_weight.reshape(27, 256, LAST),
            second_weight.reshape(27, LAST, LAST),
        )
    )
    swap = [(0, 1), (1, 0)]
    across = [(i, (i + 1) % tiles) for i in range(1, tiles, 2)]
    across += [(b, a) for a, b in across]
    own_rim, tile, scales = pl.pallas_call(
        pack_kernel,
        out_shape=(blocks(RIM_BLOCKS), blocks(TILE_BLOCKS), jax.ShapeDtypeStruct((8, LAST), F32)),
        in_specs=[HBM] * 5,
        out_specs=(VMEM, VMEM, VMEM),
        scratch_shapes=[
            pltpu.SMEM(tile_clip.shape, jnp.int32),
            pltpu.SMEM(clip_cols.shape, jnp.int32),
            pltpu.SMEM(clip_start.shape, jnp.int32),
            pltpu.VMEM(local_in.shape, BF),
            pltpu.VMEM(local_cot.shape, BF),
            pltpu.SemaphoreType.DMA((5,)),
        ],
        compiler_params=params(8),
        cost_estimate=cost(10**6, 2 * 10**6),
    )(tile_clip, clip_cols, clip_start, local_in, local_cot)
    rim = lax.ppermute(own_rim, TILE_AXES, across)
    sibling = lax.ppermute(tile, "core", swap)

    inner_first, inner_second, act, inner_w1, inner_w2 = pl.pallas_call(
        inner_kernel,
        out_shape=(
            jax.ShapeDtypeStruct((4, 6, 16, LAST), BF),
            jax.ShapeDtypeStruct((4, 6, 16, LAST), BF),
            jax.ShapeDtypeStruct((3, 6, 8, 16, 256), BF),
            jax.ShapeDtypeStruct(w1.shape, BF),
            jax.ShapeDtypeStruct(w2.shape, BF),
        ),
        in_specs=[VMEM] * 2 + [HBM] * 2,
        out_specs=(VMEM,) * 5,
        scratch_shapes=[
            pltpu.VMEM((13, 48, LAST), F32),
            pltpu.VMEM((2, 6, 16, 9 * LAST), BF),
            pltpu.SemaphoreType.DMA((2,)),
        ],
        compiler_params=params(24),
        cost_estimate=cost(2 * 10**9, 4 * 10**6),
    )(scales, tile, w1, w2)

    sib_act, sums, scales = pl.pallas_call(
        sibling_kernel,
        out_shape=(
            jax.ShapeDtypeStruct((6, 8, 16, 256), BF),
            jax.ShapeDtypeStruct((3, 2, 2, 17, 16, LAST), BF),
            jax.ShapeDtypeStruct(scales.shape, F32),
        ),
        in_specs=[VMEM] * 3,
        out_specs=(VMEM, VMEM, VMEM),
        scratch_shapes=[
            pltpu.VMEM((18, 32, LAST), F32),
            pltpu.VMEM((17, 48, LAST), F32),
        ],
        compiler_params=params(16),
        cost_estimate=cost(10**9, 2 * 10**6),
    )(scales, tile, sibling)

    packet = pl.pallas_call(
        edge_kernel,
        out_shape=blocks(PACK_BLOCKS),
        in_specs=[VMEM] * 9,
        out_specs=VMEM,
        scratch_shapes=[
            pltpu.VMEM((3, 6, 2, 4, 16, 256), BF),
            pltpu.VMEM((2, 2, 6, 32, LAST), F32),
            pltpu.VMEM((5, 48, LAST), F32),
            pltpu.VMEM((2, 2, 2, 16, 9 * LAST), BF),
        ],
        compiler_params=params(16),
        cost_estimate=cost(10**9, 4 * 10**6),
    )(rim, scales, tile, sibling, inner_first, inner_second, act, inner_w1, inner_w2)
    packets = lax.all_gather(packet, "core", axis=0)

    depth = LAST // reps
    quarters = near_y * near_z
    per_quarter = 2 * GRAD_BLOCKS // quarters
    parts, _ = pl.pallas_call(
        weight_kernel,
        out_shape=(
            jax.ShapeDtypeStruct((reps, quarters, per_quarter, depth // 2, LAST), BF),
            jax.ShapeDtypeStruct(sums.shape, BF),
        ),
        in_specs=[VMEM] * 7,
        out_specs=(VMEM, VMEM),
        input_output_aliases={6: 1},
        scratch_shapes=[
            pltpu.VMEM((1, 48, LAST), F32),
            pltpu.VMEM((3, 2, 4, 10, 16, LAST), BF),
        ],
        compiler_params=params(24),
        cost_estimate=cost(2 * 10**9, 4 * 10**6),
    )(packets, scales, tile, sibling, act, sib_act, sums)

    count = per_quarter * depth // 2
    share = -(-count * quarters // plane // 8) * 8
    parts = parts.reshape(reps, quarters, count, LAST)

    def exchange(values, groups):
        return lax.all_to_all(values, ALL_AXES, 0, 0, axis_index_groups=groups, tiled=True)

    near = pl.pallas_call(
        near_sum_kernel,
        out_shape=jax.ShapeDtypeStruct((plane // quarters, quarters, share, LAST), BF),
        in_specs=[VMEM],
        out_specs=VMEM,
        compiler_params=params(8),
        cost_estimate=cost(10**6, 2 * 10**6),
    )(exchange(parts, near_groups))
    near = near.reshape(plane, share, LAST)
    copies, token = pl.pallas_call(
        far_sum_kernel,
        out_shape=(
            jax.ShapeDtypeStruct((plane, share, LAST), BF),
            jax.ShapeDtypeStruct(scales.shape, F32),
        ),
        in_specs=[VMEM, VMEM],
        out_specs=(VMEM, VMEM),
        compiler_params=params(8),
        cost_estimate=cost(10**5, 5 * 10**5),
    )(exchange(near, far_groups), scales)
    input_grad = pl.pallas_call(
        input_kernel,
        out_shape=jax.ShapeDtypeStruct(local_in.shape, BF),
        in_specs=[VMEM, HBM, VMEM, HBM],
        out_specs=VMEM,
        scratch_shapes=[
            pltpu.VMEM(local_in.shape, BF),
            pltpu.VMEM(w1.shape, BF),
            pltpu.VMEM((4, 8, 16, 9 * LAST), BF),
            pltpu.SemaphoreType.DMA((2,)),
        ],
        compiler_params=params(24),
        cost_estimate=cost(2 * 10**9, 4 * 10**6),
    )(token, local_in, packet, w1)

    half = lax.all_to_all(copies, PLANE_AXES, 0, 0, tiled=True)
    whole = lax.all_gather(half.reshape(quarters, plane // quarters * share, LAST), "core", axis=0)

    cell_total = tiles * reps * cotangent.shape[1] * cotangent.shape[2] * cotangent.shape[3]
    scale = 1.0 / math.sqrt(cell_total)
    first, second = pl.pallas_call(
        lambda *refs: finish_kernel(scale, per_quarter, *refs),
        out_shape=(
            jax.ShapeDtypeStruct((27, depth, 256), F32),
            jax.ShapeDtypeStruct((27, depth, LAST), F32),
        ),
        in_specs=[VMEM, ANY],
        out_specs=(VMEM, VMEM),
        compiler_params=params(16),
    )(whole, pltpu.with_memory_space_constraint(input_grad, pltpu.HBM))
    first = jnp.swapaxes(first, 1, 2).reshape(3, 3, 3, 256, depth)
    second = jnp.swapaxes(second, 1, 2).reshape(3, 3, 3, LAST, depth)
    return input_grad[None], first, second


def solution(mesh):
    devices = mesh.devices
    tiles, reps = devices.shape
    height = math.isqrt(tiles // 2)
    width = tiles // 2 // height
    near_y, near_z = math.gcd(height, 2), math.gcd(width, 2)
    wide_mesh = Mesh(
        devices.reshape(height // near_y, near_y, width // near_z, near_z, 2, reps),
        (*TILE_AXES, "x"),
    )
    in_specs = (
        P("x", None, TILE_AXES, None, None),
        P("x", None, TILE_AXES, None, None),
        P(),
        P(),
        P("x", None),
        P("x", None),
        P("x", None),
    )
    out_specs = (
        P("x", None, TILE_AXES, None, None),
        P(None, None, None, None, "x"),
        P(None, None, None, None, "x"),
    )
    return jax.shard_map(
        body, mesh=wide_mesh, in_specs=in_specs, out_specs=out_specs, check_vma=False
    )
```

```python
import math

import jax
import jax.numpy as jnp
import numpy as np
from jax import lax
from jax.experimental import pallas as pl
from jax.experimental.pallas import tpu as pltpu
from jax.sharding import Mesh
from jax.sharding import PartitionSpec as P

TILE_AXES = ("yh", "yl", "zh", "zl", "core")
ALL_AXES = (*TILE_AXES, "x")
PLANE_AXES = ("yl", "zl", "zh", "yh")
BF = jnp.bfloat16
F32 = jnp.float32
NT = (((1,), (1,)), ((), ()))
TN = (((0,), (0,)), ((), ()))
LAST = 128
TILE_COT = 96
TILE_BLOCKS = 160
RIM_COT = 24
RIM_BLOCKS = 36
PACK_SECOND = 40
PACK_ROW = 72
PACK_BLOCKS = 76
UP, DOWN, COLS, KEEP, SIB_COLS, SIB_KEEP, RIM_SCALE, SIB_SCALE = range(8)
SECOND_AT = 24
EXTRA_AT = 36
GRAD_BLOCKS = 42


def dot(lhs, rhs, dims=(((1,), (0,)), ((), ()))):
    return lax.dot_general(lhs, rhs, dims, preferred_element_type=F32)


def sigmoid(values):
    return 1.0 / (1.0 + jnp.exp(-values))


def column_shifts(values):
    column = lax.broadcasted_iota(jnp.int32, (1, 16, values.shape[2]), 1)
    left = jnp.where(column == 0, 0.0, pltpu.roll(values, 1, 1))
    right = jnp.where(column == 15, 0.0, pltpu.roll(values, 15, 1))
    return left, right


def scale_of(scales, which):
    return scales[which : which + 1].reshape(1, 1, LAST)


def low_mask(scales, which):
    column = lax.broadcasted_iota(jnp.int32, (1, 16, LAST), 1).astype(F32)
    return jnp.where(column < scale_of(scales, which), 1.0, 0.0)


def high_mask(scales, which):
    column = lax.broadcasted_iota(jnp.int32, (1, 32, LAST), 1).astype(F32)
    return jnp.where(column < 2.0 * scale_of(scales, which), 1.0, 0.0)


def twice(values):
    return jnp.concatenate([values, values], 2)


def joined(blocks):
    halves = blocks.reshape(blocks.shape[0] // 2, 2, 16, LAST)
    return jnp.concatenate([halves[:, 0], halves[:, 1]], 2)


def tile_rows(tile_ref, frame):
    return joined(tile_ref[frame * 16 : frame * 16 + 16]).astype(F32)


def eff_frame(read, frame, keep):
    values = read(frame)
    return jnp.where(keep > 0.5, values, read(4)) if frame < 4 else values


def load_scales(clip_ref, cols_ref, start_ref):
    tile = lax.axis_index(TILE_AXES)
    tiles = lax.axis_size(TILE_AXES)
    even = lax.axis_index("core") == 0
    own = clip_ref[0, tile]
    up_same = (tile > 0) & (clip_ref[0, jnp.maximum(tile - 1, 0)] == own)
    down_same = (tile + 1 < tiles) & (clip_ref[0, jnp.minimum(tile + 1, tiles - 1)] == own)
    sibling = clip_ref[0, jnp.where(even, tile + 1, tile - 1)]
    up = jnp.where(up_same, 1.0, 0.0)
    down = jnp.where(down_same, 1.0, 0.0)
    return (
        up,
        down,
        cols_ref[0, own].astype(F32),
        jnp.where(start_ref[0, own] == 0, 0.0, 1.0),
        cols_ref[0, sibling].astype(F32),
        jnp.where(start_ref[0, sibling] == 0, 0.0, 1.0),
        jnp.where(even, up, down),
        jnp.where(even, down, up),
    )


def pack_kernel(
    clip_any, cols_any, start_any, in_any, cot_any, rim_ref, tile_ref, scales_ref,
    clip_ref, cols_ref, start_ref, in_ref, cot_ref, sems,
):
    copies = [
        pltpu.make_async_copy(source, target, sems.at[n])
        for n, (source, target) in enumerate(
            (
                (clip_any, clip_ref),
                (cols_any, cols_ref),
                (start_any, start_ref),
                (in_any, in_ref),
                (cot_any, cot_ref),
            )
        )
    ]
    for copy in copies[3:] + copies[:3]:
        copy.start()
    copies[3].wait()
    for frame in range(6):
        for row in range(8):
            for half in range(2):
                tile_ref[frame * 16 + row * 2 + half] = in_ref[
                    frame, row, :, half * LAST : (half + 1) * LAST
                ]
    copies[4].wait()
    for frame in range(2):
        for half in range(2):
            for row in range(16):
                tile_ref[TILE_COT + frame * 32 + row * 2 + half] = cot_ref[
                    frame, row, half * 16 : (half + 1) * 16, :
                ]
    odd = lax.axis_index("core")
    for frame in range(6):
        rim_ref[frame * 4 : frame * 4 + 4] = tile_ref[pl.ds(frame * 16 + odd * 12, 4)]
    for frame in range(2):
        at = RIM_COT + frame * 6
        rim_ref[at : at + 6] = tile_ref[pl.ds(TILE_COT + frame * 32 + odd * 26, 6)]
    for copy in copies[:3]:
        copy.wait()
    for row, value in enumerate(load_scales(clip_ref, cols_ref, start_ref)):
        scales_ref[row : row + 1] = jnp.full((1, LAST), value, F32)


def pair_sums(rows, pair, put):
    count = rows.shape[0] - 1
    zeros = jnp.zeros((count, 8, LAST), F32)
    pair[0:count, 0:8] = zeros
    pair[0:count, 40:48] = zeros
    pair[0:count, 8:40] = rows[0:count] + rows[1 : count + 1]
    before, even, odd, after = (pair[0:count, pl.ds(begin, 16, 2), :] for begin in (7, 8, 9, 10))
    for kw, value in ((0, odd + after), (1, even + odd), (2, before + even)):
        put(kw, value.astype(BF))


def tap_sums(rows, first, begin, count, pair, cots):
    def put(kw, sums):
        for n in range(sums.shape[0]):
            row = first + n
            if row % 2 == 0:
                targets = ((1, row // 2),)
            else:
                targets = ((0, (row - 1) // 2), (2, (row + 1) // 2))
            for kh, place in targets:
                if begin <= place < begin + count:
                    tap = kh * 3 + kw
                    cots[place - begin, :, tap * LAST : (tap + 1) * LAST] = sums[n]

    pair_sums(rows, pair, put)


def shifted_act(act, at, values):
    left, right = column_shifts(values)
    for kw, shifted in enumerate((left, values, right)):
        act[(kw, *at)] = shifted.astype(BF)


def first_conv(windows, w1_ref):
    total = None
    for step in range(9):
        window = jnp.concatenate([windows(kw, step // 3, step % 3) for kw in range(3)], 1)
        term = dot(window, w1_ref[step * 3 : step * 3 + 3].reshape(768, LAST))
        total = term if total is None else total + term
    return total


def second_conv_back(cots, w2_ref, slope, put):
    flat = jnp.concatenate(
        [
            jnp.concatenate([w2_ref[kt * 9 + tap] for tap in range(9)], 1)
            for kt in range(3)
        ],
        0,
    )
    spread = dot(cots, flat, NT)
    cells = spread.shape[0] // 2
    for frame in range(4):
        total = None
        for kt in range(3):
            if 0 <= frame - kt < 2:
                term = spread[
                    (frame - kt) * cells : (frame - kt + 1) * cells, kt * LAST : (kt + 1) * LAST
                ]
                total = term if total is None else total + term
        put(frame, (total * slope[frame]).astype(BF))


def inner_kernel(
    scales, tile_ref, w1_any, w2_any, first_ref, second_ref, act, w1_ref, w2_ref,
    pair, cots, sems,
):
    load_w1 = pltpu.make_async_copy(w1_any, w1_ref, sems.at[0])
    load_w2 = pltpu.make_async_copy(w2_any, w2_ref, sems.at[1])
    load_w1.start()
    load_w2.start()
    keep = twice(scale_of(scales, KEEP))
    low = low_mask(scales, COLS)
    for frame in range(6):
        values = eff_frame(lambda f: tile_rows(tile_ref, f), frame, keep)
        values = values * sigmoid(values) * twice(low)
        shifted_act(act, (frame,), values)
    load_w1.wait()
    first_out = first_conv(
        lambda kw, kt, kh: act[kw, kt : kt + 4, kh : kh + 6].reshape(384, 256), w1_ref
    ).reshape(24, 16, LAST)
    gate = sigmoid(first_out)
    second_ref[...] = (first_out * gate * low).astype(BF).reshape(4, 6, 16, LAST)
    slope = gate * (1.0 + first_out * (1.0 - gate)) * low
    high = high_mask(scales, COLS)
    for frame in range(2):
        at = TILE_COT + frame * 32
        rows = tile_ref[at + 2 : at + 30].reshape(14, 32, LAST).astype(F32) * high
        tap_sums(rows, 1, 1, 6, pair, cots.at[frame])
    load_w2.wait()

    def put(frame, first_grad):
        first_ref[frame] = first_grad.reshape(6, 16, LAST)

    second_conv_back(cots[...].reshape(192, 1152), w2_ref, slope.reshape(4, 96, LAST), put)


def edge_kernel(
    rim_ref, scales, tile_ref, sib_ref, first_ref, second_ref, own_act, w1_ref, w2_ref, packet_ref,
    act, rows, pair, cots,
):
    odd = lax.axis_index("core")
    even = 1 - odd
    keep = twice(scale_of(scales, KEEP))
    low = low_mask(scales, COLS)
    wide_low = twice(low)
    rim_scale, sib_scale = scale_of(scales, RIM_SCALE), scale_of(scales, SIB_SCALE)
    for frame in range(6):
        for part, at, read, mask in (
            (odd, odd * 2, lambda f: joined(rim_ref[f * 4 : f * 4 + 4]), wide_low * twice(rim_scale)),
            (even, even * 2, lambda f: joined(sib_ref[pl.ds(f * 16 + odd * 12, 4)]), wide_low * twice(sib_scale)),
        ):
            values = eff_frame(lambda f, read=read: read(f).astype(F32), frame, keep)
            shifted_act(act, (frame, part, pl.ds(at, 2)), values * sigmoid(values) * mask)
    act[:, :, 0, 2:4] = own_act[:, :, 0:2]
    act[:, :, 1, 0:2] = own_act[:, :, 6:8]
    high = high_mask(scales, COLS)
    for frame in range(2):
        at = TILE_COT + frame * 32
        own = tile_ref[at : at + 32].reshape(16, 32, LAST)
        rows[frame, 0, 3:6] = own[0:3].astype(F32) * high
        rows[frame, 1, 0:3] = own[13:16].astype(F32) * high
        raw = rim_ref[RIM_COT + frame * 6 : RIM_COT + frame * 6 + 6].reshape(3, 32, LAST)
        rows[frame, odd, pl.ds(odd * 3, 3)] = raw.astype(F32) * (high * rim_scale)
        raw = sib_ref[pl.ds(at + odd * 26, 6)].reshape(3, 32, LAST)
        rows[frame, even, pl.ds(even * 3, 3)] = raw.astype(F32) * (high * sib_scale)
        far = rows[frame, odd, pl.ds(2 + odd, 1)].reshape(2, 16, LAST)
        packet_ref[PACK_ROW + frame * 2 : PACK_ROW + frame * 2 + 2] = far.astype(BF)
        tap_sums(rows[frame, 0], -3, -1, 2, pair, cots.at[frame, 0])
        tap_sums(rows[frame, 1], 13, 7, 2, pair, cots.at[frame, 1])
    first_out = first_conv(
        lambda kw, kt, kh: act[kw, kt : kt + 4, :, kh : kh + 2].reshape(256, 256), w1_ref
    ).reshape(16, 16, LAST)
    row = lax.broadcasted_iota(jnp.int32, (16, 1, 1), 0) % 4
    row_scale = jnp.where(
        row == 0, scale_of(scales, UP), jnp.where(row == 3, scale_of(scales, DOWN), 1.0)
    )
    gate = sigmoid(first_out)
    second_in = (first_out * gate * low).astype(BF)
    slope = gate * (1.0 + first_out * (1.0 - gate)) * (low * row_scale)
    for frame in range(4):
        at = PACK_SECOND + frame * 8
        packet_ref[at] = second_in[frame * 4 + 1]
        packet_ref[at + 1 : at + 7] = second_ref[frame]
        packet_ref[at + 7] = second_in[frame * 4 + 2]

    def put(frame, first_grad):
        blocks_now = first_grad.reshape(4, 16, LAST)
        packet_ref[frame * 10 : frame * 10 + 2] = blocks_now[0:2]
        packet_ref[frame * 10 + 2 : frame * 10 + 8] = first_ref[frame]
        packet_ref[frame * 10 + 8 : frame * 10 + 10] = blocks_now[2:4]

    second_conv_back(cots[...].reshape(128, 1152), w2_ref, slope.reshape(4, 64, LAST), put)


def sibling_kernel(scales, tile_ref, sib_ref, act_ref, sums_ref, token_ref, rows, pair):
    token_ref[...] = scales[...]
    keep = twice(scale_of(scales, SIB_KEEP))
    low = twice(low_mask(scales, SIB_COLS))
    for frame in range(6):
        values = eff_frame(lambda f: tile_rows(sib_ref, f), frame, keep)
        act_ref[frame] = (values * sigmoid(values) * low).astype(BF)
    odd = lax.axis_index("core")
    link = scale_of(scales, SIB_SCALE)
    rows[...] = jnp.zeros((18, 32, LAST), F32)
    for slot, tile, other, which in (
        (0, tile_ref, sib_ref, COLS),
        (1, sib_ref, tile_ref, SIB_COLS),
    ):
        lower = odd if slot == 0 else 1 - odd
        high = high_mask(scales, which)
        for frame in range(2):
            at = TILE_COT + frame * 32
            rows[1:17] = tile[at : at + 32].reshape(16, 32, LAST).astype(F32) * high
            near = other[pl.ds(at + lower * 30, 2)].reshape(1, 32, LAST)
            rows[pl.ds(17 - lower * 17, 1)] = near.astype(F32) * (high * link)

            def put(kw, values):
                for n in range(17):
                    place = n // 2 if n % 2 == 0 else 9 + n // 2
                    sums_ref[kw, slot, frame, place] = values[n]

            pair_sums(rows[...], pair, put)


def input_kernel(scales, in_any, packet_ref, w1_any, grad_ref, in_ref, w1_ref, firsts, sems):
    load_in = pltpu.make_async_copy(in_any, in_ref, sems.at[0])
    load_w1 = pltpu.make_async_copy(w1_any, w1_ref, sems.at[1])
    load_w1.start()
    load_in.start()
    for frame in range(4):
        first_grad = packet_ref[frame * 10 : frame * 10 + 10]
        before, after = column_shifts(first_grad.astype(F32))
        for kw, value in ((0, after.astype(BF)), (1, first_grad), (2, before.astype(BF))):
            for kh in range(3):
                tap = kh * 3 + kw
                firsts[frame, :, :, tap * LAST : (tap + 1) * LAST] = value[2 - kh : 10 - kh]
    load_w1.wait()
    load_in.wait()
    shifted = firsts[...].reshape(512, 1152)
    by_depth = [
        dot(shifted, jnp.concatenate([w1_ref[kt * 9 + tap] for tap in range(9)], 1), NT)
        for kt in range(3)
    ]
    keep = twice(scale_of(scales, KEEP))
    low = twice(low_mask(scales, COLS))
    carried = None
    for frame in range(6):
        total = None
        for kt in range(3):
            if 0 <= frame - kt < 4:
                term = by_depth[kt][(frame - kt) * 128 : (frame - kt + 1) * 128]
                total = term if total is None else total + term
        values = eff_frame(lambda f: in_ref[f].astype(F32), frame, keep)
        gate = sigmoid(values)
        pre = total.reshape(8, 16, 256) * (gate * (1.0 + values * (1.0 - gate)) * low)
        if frame < 4:
            carried = pre if carried is None else carried + pre
            grad_ref[frame] = (pre * keep).astype(BF)
        elif frame == 4:
            grad_ref[frame] = (pre + carried * (1.0 - keep)).astype(BF)
        else:
            grad_ref[frame] = pre.astype(BF)


def weight_kernel(
    packets_ref, scales, tile_ref, sib_ref, act_ref, sib_act_ref, _,
    part_ref, sums, pair, cols,
):
    odd = lax.axis_index("core")
    packet_ref, sib_packet_ref = packets_ref.at[odd], packets_ref.at[1 - odd]
    reps, quarters, per_quarter, depth = part_ref.shape[:4]
    for slot, tile, packet, which in (
        (0, tile_ref, packet_ref, COLS),
        (1, sib_ref, sib_packet_ref, SIB_COLS),
    ):
        lower = odd if slot == 0 else 1 - odd
        high = high_mask(scales, which)
        for frame in range(2):
            far = packet[PACK_ROW + frame * 2 : PACK_ROW + frame * 2 + 2].reshape(1, 32, LAST)
            last = tile[pl.ds(TILE_COT + frame * 32 + lower * 30, 2)].reshape(1, 32, LAST)
            rows = jnp.concatenate([far.astype(F32), last.astype(F32) * high], 0)

            def put(kw, values):
                sums[kw, slot, frame, pl.ds(lower * 8, 1)] = values

            pair_sums(rows, pair, put)
        for frame in range(4):
            first_grad = packet[frame * 10 : frame * 10 + 10]
            before, after = column_shifts(first_grad.astype(F32))
            cols[0, slot, frame] = after.astype(BF)
            cols[1, slot, frame] = first_grad
            cols[2, slot, frame] = before.astype(BF)

    def both(refs, kt, frames):
        return jnp.concatenate(
            [ref[kt : kt + frames].reshape(frames * 128, ref.shape[3]) for ref in refs], 0
        )

    act_all = jnp.concatenate([both((act_ref.at[1], sib_act_ref), kt, 4) for kt in range(3)], 1)
    seconds = [
        ref[PACK_SECOND:PACK_ROW].reshape(4, 8, 16, LAST) for ref in (packet_ref, sib_packet_ref)
    ]
    second_all = jnp.concatenate([both(seconds, kt, 2) for kt in range(3)], 1)

    def put_block(block, at):
        halves = block.astype(BF).reshape(reps, 2, depth, LAST)
        for half in range(2):
            quarter, place = divmod(at * 2 + half, per_quarter)
            for rep in range(reps):
                first = rep + (quarter - rep) * odd
                part_ref[first, rep + quarter - first, place] = halves[rep, half]

    def first_taps(step, at):
        tap = 5 * odd + step
        window = cols[tap % 3, :, :, pl.ds(2 - tap // 3, 8)].reshape(1024, LAST)
        block = dot(window, act_all, TN)
        for n in range(6):
            put_block(block[:, n * LAST : (n + 1) * LAST], at + n)

    def second_taps(step, at):
        tap = 4 * odd + step
        kh = tap // 3
        begin = jnp.where(kh == 0, 1, jnp.where(kh == 1, 9, 0))
        window = sums[tap % 3, :, :, pl.ds(begin, 8)].reshape(512, LAST)
        block = dot(window, second_all, TN)
        for n in range(3):
            put_block(block[:, n * LAST : (n + 1) * LAST], at + n)

    for step in range(4):
        first_taps(step, step * 6)
        second_taps(step, SECOND_AT + step * 3)

    @pl.when(odd == 0)
    def _():
        first_taps(4, EXTRA_AT)

    @pl.when(odd == 1)
    def _():
        second_taps(4, EXTRA_AT)
        for at in range(EXTRA_AT + 3, EXTRA_AT + 6):
            put_block(jnp.zeros((LAST, LAST), F32), at)


def near_sum_kernel(parts_ref, sum_ref):
    shares, others, share, _ = sum_ref.shape
    rows = parts_ref.shape[2]
    for other in range(others):
        total = parts_ref[0, other].astype(F32)
        for n in range(1, parts_ref.shape[0]):
            total = total + parts_ref[n, other].astype(F32)
        if shares * share > rows:
            padding = jnp.zeros((shares * share - rows, LAST), F32)
            total = jnp.concatenate([total, padding], 0)
        sum_ref[:, other] = total.reshape(shares, share, LAST).astype(BF)


def far_sum_kernel(parts_ref, scales, copies_ref, token_ref):
    token_ref[...] = scales[...]
    total = parts_ref[0].astype(F32)
    for n in range(1, parts_ref.shape[0]):
        total = total + parts_ref[n].astype(F32)
    copies_ref[...] = jnp.broadcast_to(total.astype(BF)[None], copies_ref.shape)


def sum_groups(sizes):
    numbers = np.arange(math.prod(sizes)).reshape(sizes)
    even, odd = numbers[..., 0, :], numbers[..., 1, :]
    reps, quarters = sizes[5], sizes[1] * sizes[3]
    near = (
        even.reshape(-1, reps),
        odd.transpose(0, 2, 4, 1, 3).reshape(-1, quarters),
    )
    far = (
        even.transpose(4, 2, 0, 1, 3).reshape(reps, -1),
        odd.transpose(1, 3, 2, 0, 4).reshape(quarters, -1),
    )
    return [[row.tolist() for part in parts for row in part] for parts in (near, far)]


def finish_kernel(scale, per_quarter, whole_ref, _, first_ref, second_ref):
    depth = first_ref.shape[1] // 2
    for core in range(2):

        def put(target, tap, columns, at):
            for half in range(2):
                quarter, place = divmod(at * 2 + half, per_quarter)
                rows = whole_ref[core, quarter, place * depth : (place + 1) * depth]
                target[tap, half * depth : (half + 1) * depth, columns] = rows.astype(F32) * scale

        for step in range(5 - core):
            for kt in range(3):
                for half in range(2):
                    at = (step * 6 if step < 4 else EXTRA_AT) + kt * 2 + half
                    columns = slice(half * LAST, (half + 1) * LAST)
                    put(first_ref, kt * 9 + 5 * core + step, columns, at)
        for step in range(4 + core):
            for kt in range(3):
                at = (SECOND_AT + step * 3 if step < 4 else EXTRA_AT) + kt
                put(second_ref, kt * 9 + 4 * core + step, slice(0, LAST), at)


VMEM = pl.BlockSpec(memory_space=pltpu.VMEM)
HBM = pl.BlockSpec(memory_space=pltpu.HBM)
ANY = pl.BlockSpec(memory_space=pl.ANY)


def params(mebibytes):
    return pltpu.CompilerParams(vmem_limit_bytes=mebibytes << 20)


def cost(flops, moved):
    return pl.CostEstimate(flops=flops, bytes_accessed=moved, transcendentals=0)


def wide_sum(parts):
    return jnp.sum(parts.astype(F32), axis=0).astype(BF)


def blocks(count):
    return jax.ShapeDtypeStruct((count, 16, LAST), BF)


def body(inputs, cotangent, first_weight, second_weight, tile_clip, clip_cols, clip_start):
    tiles = lax.axis_size(TILE_AXES)
    reps, near_y, near_z = (lax.axis_size(name) for name in ("x", "yl", "zl"))
    plane = lax.axis_size(PLANE_AXES)
    near_groups, far_groups = sum_groups(tuple(map(lax.axis_size, ALL_AXES)))
    local_in, local_cot, tile_clip, clip_cols, clip_start, w1, w2 = (
        pltpu.with_memory_space_constraint(array, pltpu.HBM)
        for array in (
            inputs[0],
            cotangent[0],
            tile_clip,
            clip_cols,
            clip_start,
            first_weight.reshape(27, 256, LAST),
            second_weight.reshape(27, LAST, LAST),
        )
    )
    swap = [(0, 1), (1, 0)]
    across = [(i, (i + 1) % tiles) for i in range(1, tiles, 2)]
    across += [(b, a) for a, b in across]
    own_rim, tile, scales = pl.pallas_call(
        pack_kernel,
        out_shape=(blocks(RIM_BLOCKS), blocks(TILE_BLOCKS), jax.ShapeDtypeStruct((8, LAST), F32)),
        in_specs=[HBM] * 5,
        out_specs=(VMEM, VMEM, VMEM),
        scratch_shapes=[
            pltpu.SMEM(tile_clip.shape, jnp.int32),
            pltpu.SMEM(clip_cols.shape, jnp.int32),
            pltpu.SMEM(clip_start.shape, jnp.int32),
            pltpu.VMEM(local_in.shape, BF),
            pltpu.VMEM(local_cot.shape, BF),
            pltpu.SemaphoreType.DMA((5,)),
        ],
        compiler_params=params(8),
        cost_estimate=cost(10**6, 2 * 10**6),
    )(tile_clip, clip_cols, clip_start, local_in, local_cot)
    rim = lax.ppermute(own_rim, TILE_AXES, across)
    sibling = lax.ppermute(tile, "core", swap)

    inner_first, inner_second, act, inner_w1, inner_w2 = pl.pallas_call(
        inner_kernel,
        out_shape=(
            jax.ShapeDtypeStruct((4, 6, 16, LAST), BF),
            jax.ShapeDtypeStruct((4, 6, 16, LAST), BF),
            jax.ShapeDtypeStruct((3, 6, 8, 16, 256), BF),
            jax.ShapeDtypeStruct(w1.shape, BF),
            jax.ShapeDtypeStruct(w2.shape, BF),
        ),
        in_specs=[VMEM] * 2 + [HBM] * 2,
        out_specs=(VMEM,) * 5,
        scratch_shapes=[
            pltpu.VMEM((13, 48, LAST), F32),
            pltpu.VMEM((2, 6, 16, 9 * LAST), BF),
            pltpu.SemaphoreType.DMA((2,)),
        ],
        compiler_params=params(24),
        cost_estimate=cost(2 * 10**9, 4 * 10**6),
    )(scales, tile, w1, w2)

    sib_act, sums, scales = pl.pallas_call(
        sibling_kernel,
        out_shape=(
            jax.ShapeDtypeStruct((6, 8, 16, 256), BF),
            jax.ShapeDtypeStruct((3, 2, 2, 17, 16, LAST), BF),
            jax.ShapeDtypeStruct(scales.shape, F32),
        ),
        in_specs=[VMEM] * 3,
        out_specs=(VMEM, VMEM, VMEM),
        scratch_shapes=[
            pltpu.VMEM((18, 32, LAST), F32),
            pltpu.VMEM((17, 48, LAST), F32),
        ],
        compiler_params=params(16),
        cost_estimate=cost(10**9, 2 * 10**6),
    )(scales, tile, sibling)

    packet = pl.pallas_call(
        edge_kernel,
        out_shape=blocks(PACK_BLOCKS),
        in_specs=[VMEM] * 9,
        out_specs=VMEM,
        scratch_shapes=[
            pltpu.VMEM((3, 6, 2, 4, 16, 256), BF),
            pltpu.VMEM((2, 2, 6, 32, LAST), F32),
            pltpu.VMEM((5, 48, LAST), F32),
            pltpu.VMEM((2, 2, 2, 16, 9 * LAST), BF),
        ],
        compiler_params=params(16),
        cost_estimate=cost(10**9, 4 * 10**6),
    )(rim, scales, tile, sibling, inner_first, inner_second, act, inner_w1, inner_w2)
    packets = lax.all_gather(packet, "core", axis=0)

    depth = LAST // reps
    quarters = near_y * near_z
    per_quarter = 2 * GRAD_BLOCKS // quarters
    parts, _ = pl.pallas_call(
        weight_kernel,
        out_shape=(
            jax.ShapeDtypeStruct((reps, quarters, per_quarter, depth // 2, LAST), BF),
            jax.ShapeDtypeStruct(sums.shape, BF),
        ),
        in_specs=[VMEM] * 7,
        out_specs=(VMEM, VMEM),
        input_output_aliases={6: 1},
        scratch_shapes=[
            pltpu.VMEM((1, 48, LAST), F32),
            pltpu.VMEM((3, 2, 4, 10, 16, LAST), BF),
        ],
        compiler_params=params(24),
        cost_estimate=cost(2 * 10**9, 4 * 10**6),
    )(packets, scales, tile, sibling, act, sib_act, sums)

    count = per_quarter * depth // 2
    share = -(-count * quarters // plane // 8) * 8
    parts = parts.reshape(reps, quarters, count, LAST)

    def exchange(values, groups):
        return lax.all_to_all(values, ALL_AXES, 0, 0, axis_index_groups=groups, tiled=True)

    near = pl.pallas_call(
        near_sum_kernel,
        out_shape=jax.ShapeDtypeStruct((plane // quarters, quarters, share, LAST), BF),
        in_specs=[VMEM],
        out_specs=VMEM,
        compiler_params=params(8),
        cost_estimate=cost(10**6, 2 * 10**6),
    )(exchange(parts, near_groups))
    near = near.reshape(plane, share, LAST)
    copies, token = pl.pallas_call(
        far_sum_kernel,
        out_shape=(
            jax.ShapeDtypeStruct((plane, share, LAST), BF),
            jax.ShapeDtypeStruct(scales.shape, F32),
        ),
        in_specs=[VMEM, VMEM],
        out_specs=(VMEM, VMEM),
        compiler_params=params(8),
        cost_estimate=cost(10**5, 5 * 10**5),
    )(exchange(near, far_groups), scales)
    input_grad = pl.pallas_call(
        input_kernel,
        out_shape=jax.ShapeDtypeStruct(local_in.shape, BF),
        in_specs=[VMEM, HBM, VMEM, HBM],
        out_specs=VMEM,
        scratch_shapes=[
            pltpu.VMEM(local_in.shape, BF),
            pltpu.VMEM(w1.shape, BF),
            pltpu.VMEM((4, 8, 16, 9 * LAST), BF),
            pltpu.SemaphoreType.DMA((2,)),
        ],
        compiler_params=params(24),
        cost_estimate=cost(2 * 10**9, 4 * 10**6),
    )(token, local_in, packet, w1)

    half = lax.all_to_all(copies, PLANE_AXES, 0, 0, tiled=True)
    whole = lax.all_gather(half.reshape(quarters, plane // quarters * share, LAST), "core", axis=0)

    cell_total = tiles * reps * cotangent.shape[1] * cotangent.shape[2] * cotangent.shape[3]
    scale = 1.0 / math.sqrt(cell_total)
    first, second = pl.pallas_call(
        lambda *refs: finish_kernel(scale, per_quarter, *refs),
        out_shape=(
            jax.ShapeDtypeStruct((27, depth, 256), F32),
            jax.ShapeDtypeStruct((27, depth, LAST), F32),
        ),
        in_specs=[VMEM, ANY],
        out_specs=(VMEM, VMEM),
        compiler_params=params(16),
    )(whole, pltpu.with_memory_space_constraint(input_grad, pltpu.HBM))
    first = jnp.swapaxes(first, 1, 2).reshape(3, 3, 3, 256, depth)
    second = jnp.swapaxes(second, 1, 2).reshape(3, 3, 3, LAST, depth)
    return input_grad[None], first, second


def solution(mesh):
    devices = mesh.devices
    tiles, reps = devices.shape
    height = math.isqrt(tiles // 2)
    width = tiles // 2 // height
    near_y, near_z = math.gcd(height, 2), math.gcd(width, 2)
    wide_mesh = Mesh(
        devices.reshape(height // near_y, near_y, width // near_z, near_z, 2, reps),
        (*TILE_AXES, "x"),
    )
    in_specs = (
        P("x", None, TILE_AXES, None, None),
        P("x", None, TILE_AXES, None, None),
        P(),
        P(),
        P("x", None),
        P("x", None),
        P("x", None),
    )
    out_specs = (
        P("x", None, TILE_AXES, None, None),
        P(None, None, None, None, "x"),
        P(None, None, None, None, "x"),
    )
    return jax.shard_map(
        body, mesh=wide_mesh, in_specs=in_specs, out_specs=out_specs, check_vma=False
    )
```
